512 devices in a mesh: ctx: 16 (over y, core), tp: 32 (over z, x).
Axes of the slice: x: 4, y: 8, z: 8, core: 2. Of those that a mesh axis runs over, the one named last changes fastest.
Arguments:
- queries: bfloat16 [4096, 8192], P('ctx', 'tp'), may hold values from -6 to 6
- keys: bfloat16 [4096, 8192], P('ctx', 'tp'), may hold values from -0.5 to 0.5
- values: bfloat16 [4096, 8192], P('ctx', 'tp'), may hold values from -64 to 64
- log_decay: float32 [4096, 64], P('ctx', 'tp'), may hold values from -0.8 to 0
- gate: bfloat16 [4096, 8192], P('ctx', 'tp'), may hold values from -6 to 6
- norm_gain: float32 [8192], P('tp'), may hold values from 0.1 to 1.9
- out_weight: bfloat16 [6144, 8192], P('tp'), may hold values from -0.125 to 0.125
- target: bfloat16 [4096, 6144], P('ctx', 'tp'), may hold values from -3 to 3
Outputs:
- output: bfloat16 [4096, 6144], P('ctx', 'tp')
- query_grad: bfloat16 [4096, 8192], P('ctx', 'tp')
- key_grad: bfloat16 [4096, 8192], P('ctx', 'tp')
- value_grad: bfloat16 [4096, 8192], P('ctx', 'tp')
- gate_grad: bfloat16 [4096, 8192], P('ctx', 'tp')
The draws below stay inside these ranges and needn't reach their ends.
All inputs are finite; a program needn't handle non-finite values.
Results may differ from the reference program's by a relative error of at most 0.03.
Values may be sent and summed in bfloat16 or wider, within the bound.
A program may use at most 64 MiB of HBM per device.

```python
import jax
import jax.numpy as jnp
from jax import lax

D = 6144
HEAD_TOTAL = 64
DH = 128
TOK_DEV = 256
SEQUENCE_TOKENS = 4096
N_TP = 32


def draw_values(key, part):
    key = jax.random.fold_in(key, 5)
    first_key = jax.random.fold_in(key, 0)
    column_head = jnp.arange(HEAD_TOTAL * DH) // DH
    head_scale = 10.0 ** (column_head.astype(jnp.float32) / max(HEAD_TOTAL - 1, 1))
    base = jax.random.normal(first_key, (SEQUENCE_TOKENS, HEAD_TOTAL * DH), jnp.float32)
    return (base * head_scale[None]).astype(jnp.bfloat16)


def draw_log_decay(key, part):
    key = jax.random.fold_in(key, 9)
    key_sequence = jax.random.split(key, 7)
    fast_share = 0.5
    fast_heads = jax.random.uniform(key_sequence[0], (HEAD_TOTAL,), jnp.float32) < fast_share
    fast_rate = jax.random.uniform(key_sequence[1], (HEAD_TOTAL,), jnp.float32, 1.0 / 50.0, 1.0 / 30.0)
    slow_rate = jax.random.uniform(key_sequence[2], (HEAD_TOTAL,), jnp.float32, 0.02, 0.1) / SEQUENCE_TOKENS
    head_rate = jnp.where(fast_heads, fast_rate, slow_rate)
    roughness = jax.random.uniform(key_sequence[3], (SEQUENCE_TOKENS, HEAD_TOTAL), jnp.float32, 0.5, 1.5)
    block_count = SEQUENCE_TOKENS // TOK_DEV
    block_factor = jnp.exp(jax.random.uniform(key_sequence[4], (block_count, HEAD_TOTAL), jnp.float32, -0.6931, 0.6931))
    block_factor = jnp.repeat(block_factor, TOK_DEV, axis=0)
    spike_locations = jax.random.randint(key_sequence[5], (2,), 0, SEQUENCE_TOKENS)
    spike_match = jnp.any(jnp.arange(SEQUENCE_TOKENS)[:, None] == spike_locations[None, :], axis=1)
    spike_penalty = jnp.log(jax.random.uniform(key_sequence[6], (SEQUENCE_TOKENS, HEAD_TOTAL), jnp.float32, 0.5, 0.8))
    stable_value = -(head_rate[None] * roughness * block_factor)
    return stable_value + jnp.where(spike_match[:, None], spike_penalty, 0.0)


def raised(drawn, rng, source, target, parts, factor):
    owner, partner = [(jnp.arange(drawn.shape[axis_at]) // (drawn.shape[axis_at] // parts)).reshape([-1 if axis == axis_at else 1 for axis in range(drawn.ndim)]) for axis_at in (source, target)]
    chosen = jax.random.permutation(rng, parts)[partner]
    strong = (owner == chosen) | (owner == (partner + parts // 2) % parts)
    return jnp.where(strong, factor * drawn, drawn)


def levels(rng, extent, cuts, low, high):
    def one(position, parts):
        draws = jax.random.uniform(jax.random.fold_in(jax.random.fold_in(rng, 6), position), (parts,), jnp.float32, low / len(cuts), high / len(cuts))
        return jnp.repeat(jnp.exp(draws), extent[position] // parts).reshape((-1,) + (1,) * (len(extent) - position - 1))

    factor_of = one(*cuts[0])
    for cut in cuts[1:]:
        factor_of = factor_of * one(*cut)
    return factor_of


def normal_values(stream_key, extent, deviation, limit, shards=(), held_as=jnp.bfloat16):
    drawn = jax.random.normal(stream_key, extent, jnp.float32) * deviation
    if len(shards) > 0:
        drawn = levels(stream_key, extent, shards, -0.22, 0.18) * drawn
    return jnp.clip(drawn, min=-limit, max=limit).astype(held_as)


def noise_with(own_key, extent, deviation, most, shards, heavy, kind=jnp.bfloat16):
    drawn = deviation * jax.random.normal(own_key, extent, jnp.float32)
    if shards:
        drawn = drawn * levels(own_key, extent, shards, -0.22, 0.18)
    return jnp.clip(raised(drawn, jax.random.fold_in(own_key, 3), *heavy), -most, most).astype(kind)


def setup_inputs(seed: int = 0) -> dict:
    arg_keys = jax.random.split(jax.random.key(seed), 9)
    return {
        "queries": normal_values(arg_keys[0], (SEQUENCE_TOKENS, HEAD_TOTAL * DH), 1.0, 6.0, ((0, 16), (1, 32))),
        "keys": normal_values(arg_keys[1], (SEQUENCE_TOKENS, HEAD_TOTAL * DH), DH ** -0.5, 0.5, ((0, 16), (1, 32))),
        "values": draw_values(jax.random.fold_in(arg_keys[8], 71), 0),
        "log_decay": draw_log_decay(jax.random.fold_in(arg_keys[8], 71), 0),
        "gate": normal_values(arg_keys[4], (SEQUENCE_TOKENS, HEAD_TOTAL * DH), 1.0, 6.0, ((0, 16), (1, 32))),
        "norm_gain": jnp.clip(1.0 + 0.18 * jax.random.normal(arg_keys[5], (HEAD_TOTAL * DH,), jnp.float32), 0.1, 1.9),
        "out_weight": noise_with(arg_keys[6], (D, HEAD_TOTAL * DH), (HEAD_TOTAL * DH) ** -0.5, 0.125, ((0, 32),), (0, 1, 32, 2.75)),
        "target": normal_values(arg_keys[7], (SEQUENCE_TOKENS, D), 0.5, 3.0, ((0, 16), (1, 32))),
    }


EPS = 1e-06

def to_float(array):
    return array.astype(jnp.float32)

def decay_tables(log_block):
    cum_decay = jnp.cumsum(log_block, axis=0)
    block_total = cum_decay[-1]
    by_head = cum_decay.T
    gaps = by_head[:, :, None] - by_head[:, None, :]
    length = log_block.shape[0]
    causal = jnp.arange(length)[:, None] >= jnp.arange(length)[None, :]
    weight = jnp.where(causal[None], jnp.exp(jnp.minimum(gaps, 0.0)), 0.0)
    return (cum_decay, block_total, weight)

def block_common(query_heads, key_heads, log_block):
    cum_decay, block_total, weight = decay_tables(log_block)
    scores = jnp.einsum('thd,shd->hts', to_float(query_heads), to_float(key_heads))
    probs = (scores * weight).astype(jnp.bfloat16)
    decayed_keys = (to_float(key_heads) * jnp.exp(block_total[None] - cum_decay)[:, :, None]).astype(jnp.bfloat16)
    return (cum_decay, block_total, weight, probs, decayed_keys)

def forward_block(carried, block_items):
    query_heads, key_heads, value_heads, log_block = block_items
    cum_decay, block_total, weight, probs, decayed_keys = block_common(query_heads, key_heads, log_block)
    within_block = jnp.einsum('hts,she->the', to_float(probs), to_float(value_heads))
    state_half = carried.astype(jnp.bfloat16)
    from_state = jnp.einsum('thd,hde->the', to_float(query_heads), to_float(state_half)) * jnp.exp(cum_decay)[:, :, None]
    own_state = jnp.einsum('thd,the->hde', to_float(decayed_keys), to_float(value_heads))
    next_state = jnp.exp(block_total)[:, None, None] * carried + own_state
    return (next_state, (within_block + from_state, carried))

def backward_block(grad_carried, block_items):
    query_heads, key_heads, value_heads, log_block, attn_grad, carried = block_items
    cum_decay, block_total, weight, probs, decayed_keys = block_common(query_heads, key_heads, log_block)
    state_half = carried.astype(jnp.bfloat16)
    grad_half = grad_carried.astype(jnp.bfloat16)
    value_scores = jnp.einsum('the,she->hts', to_float(attn_grad), to_float(value_heads))
    score_grad = (value_scores * weight).astype(jnp.bfloat16)
    query_grad = jnp.einsum('hts,shd->thd', to_float(score_grad), to_float(key_heads))
    query_grad = query_grad + jnp.exp(cum_decay)[:, :, None] * jnp.einsum('the,hde->thd', to_float(attn_grad), to_float(state_half))
    key_grad = jnp.einsum('hts,thd->shd', to_float(score_grad), to_float(query_heads))
    key_grad = key_grad + jnp.exp(block_total[None] - cum_decay)[:, :, None] * jnp.einsum('she,hde->shd', to_float(value_heads), to_float(grad_half))
    value_grad = jnp.einsum('hts,the->she', to_float(probs), to_float(attn_grad))
    value_grad = value_grad + jnp.einsum('shd,hde->she', to_float(decayed_keys), to_float(grad_half))
    decayed_queries = (to_float(query_heads) * jnp.exp(cum_decay)[:, :, None]).astype(jnp.bfloat16)
    own_grad = jnp.einsum('thd,the->hde', to_float(decayed_queries), to_float(attn_grad))
    next_grad = own_grad + jnp.exp(block_total)[:, None, None] * grad_carried
    outs = (query_grad.astype(jnp.bfloat16), key_grad.astype(jnp.bfloat16), value_grad.astype(jnp.bfloat16))
    return (next_grad, outs)

def reference(queries, keys, values, log_decay, gate, norm_gain, out_weight, target):
    block_count = SEQUENCE_TOKENS // TOK_DEV
    head_shape = (block_count, TOK_DEV, HEAD_TOTAL, DH)
    query_blocks = queries.reshape(head_shape)
    key_blocks = keys.reshape(head_shape)
    value_blocks = values.reshape(head_shape)
    decay_blocks = log_decay.reshape(block_count, TOK_DEV, HEAD_TOTAL)
    start_state = jnp.zeros((HEAD_TOTAL, DH, DH), jnp.float32)
    _, (attended, carried_all) = lax.scan(forward_block, start_state, (query_blocks, key_blocks, value_blocks, decay_blocks))
    attended = attended.reshape(SEQUENCE_TOKENS, HEAD_TOTAL * DH)
    inv_rms = lax.rsqrt(lax.optimization_barrier(jnp.mean(attended * attended, axis=1, keepdims=True)) + EPS)
    gate_open = jax.nn.sigmoid(gate.astype(jnp.float32))
    normed = (attended * inv_rms * norm_gain * gate_open).astype(jnp.bfloat16)
    output = lax.dot_general(normed, out_weight, (((1,), (1,)), ((), ())), preferred_element_type=jnp.float32).astype(jnp.bfloat16)
    output_grad = (output.astype(jnp.float32) - target.astype(jnp.float32)).astype(jnp.bfloat16)
    column_width = D // N_TP

    def add_columns(running, column_index):
        grad_part = lax.dynamic_slice_in_dim(output_grad, column_index * column_width, column_width, 1)
        weight_part = lax.dynamic_slice_in_dim(out_weight, column_index * column_width, column_width, 0)
        partial_sum = jnp.dot(grad_part, weight_part, preferred_element_type=jnp.float32)
        partial_sum = lax.optimization_barrier(partial_sum.astype(jnp.bfloat16))
        return (running + partial_sum.astype(jnp.float32), None)
    feature_grad, _ = lax.scan(add_columns, jnp.zeros((SEQUENCE_TOKENS, HEAD_TOTAL * DH), jnp.float32), jnp.arange(N_TP, dtype=jnp.int32))
    gate_grad = (feature_grad * attended * inv_rms * norm_gain * gate_open * (1.0 - gate_open)).astype(jnp.bfloat16)
    normed_grad = feature_grad * norm_gain * gate_open
    mean_product = lax.optimization_barrier(jnp.mean(normed_grad * attended, axis=1, keepdims=True))
    attn_grad = (inv_rms * normed_grad - inv_rms ** 3 * attended * mean_product).astype(jnp.bfloat16)
    grad_blocks = attn_grad.reshape(head_shape)
    _, (query_grad, key_grad, value_grad) = lax.scan(backward_block, start_state, (query_blocks, key_blocks, value_blocks, decay_blocks, grad_blocks, carried_all), reverse=True)
    return (output, query_grad.reshape(SEQUENCE_TOKENS, HEAD_TOTAL * DH), key_grad.reshape(SEQUENCE_TOKENS, HEAD_TOTAL * DH), value_grad.reshape(SEQUENCE_TOKENS, HEAD_TOTAL * DH), gate_grad)
```

```python
import functools

import jax
import jax.numpy as jnp
from jax import lax
from jax.experimental import pallas as pl
from jax.experimental.pallas import tpu as pltpu
from jax.sharding import PartitionSpec as P

DH = 128
EPS = 1e-06
MESH = pl.DeviceIdType.MESH
F32 = jnp.float32
BF16 = jnp.bfloat16
X = 4


def nn(a, b):
    return lax.dot_general(a, b, (((1,), (0,)), ((), ())), preferred_element_type=F32)


def nt(a, b):
    return lax.dot_general(a, b, (((1,), (1,)), ((), ())), preferred_element_type=F32)


def tn(a, b):
    return lax.dot_general(a, b, (((0,), (0,)), ((), ())), preferred_element_type=F32)


def identity(size):
    row = lax.broadcasted_iota(jnp.int32, (size, size), 0)
    column = lax.broadcasted_iota(jnp.int32, (size, size), 1)
    return jnp.where(row == column, 1.0, 0.0).astype(BF16)


def as_row(column):
    return jnp.broadcast_to(column, (column.shape[0], 128)).T[0:1, :]


def as_columns(row):
    return jnp.broadcast_to(row, (128, row.shape[1])).T


def kernel(
    sizes,
    q_ref,
    k_ref,
    v_ref,
    ld_ref,
    gate_ref,
    gain_ref,
    w_ref,
    target_ref,
    out_ref,
    qg_ref,
    kg_ref,
    vg_ref,
    gg_ref,
    wb,
    wrelay,
    uall,
    yacc,
    ystage,
    yrecv,
    gx,
    gall,
    fstage,
    frecv,
    weight,
    probs,
    kdec,
    att,
    klocal,
    vlocal,
    targett,
    agrad,
    bown,
    bsib,
    bchip,
    s_out,
    s_in,
    s_keep,
    t_out,
    t_in,
    c_acc,
    d_acc,
    c_out,
    state,
    small_z,
    small_x,
    w_send,
    w_recv,
    w_own,
    ws_send,
    ws_recv,
    u_send,
    u_recv,
    y_send,
    y_recv,
    g_send,
    g_recv,
    f_send,
    f_recv,
    b_send,
    b_recv,
    bc_send,
    bc_recv,
    s_send,
    s_recv,
    t_send,
    t_recv,
    c_send,
    c_recv,
    sz_send,
    sz_recv,
    sx_send,
    sx_recv,
):
    Y, Z = sizes
    tokens = q_ref.shape[0]
    half_tokens = tokens // 2
    rows = w_ref.shape[0]
    half = rows // 2
    width = q_ref.shape[1]
    total_features = w_ref.shape[1]
    heads = width // DH

    ctx = lax.axis_index("ctx")
    tp = lax.axis_index("tp")
    core = lax.rem(ctx, 2)
    y = lax.div(ctx, 2)
    x = lax.rem(tp, X)
    z = lax.div(tp, X)
    sibling = (y * 2 + 1 - core, tp)
    is_zero = core == 0

    def xs(step):
        return lax.rem(x + step + X, X)

    def zs(step):
        return lax.rem(z + step + 2 * Z, Z)

    def at_x(step):
        return (ctx, z * X + xs(step))

    def at_z(step):
        return (ctx, zs(step) * X + x)

    def at_y(place):
        return (place * 2 + core, tp)

    sign = 1 - 2 * core
    left, right, opp = xs(-1), xs(1), xs(2)

    def send(src, dst, send_sem, recv_sem, device):
        copy = pltpu.make_async_remote_copy(
            src_ref=src,
            dst_ref=dst,
            send_sem=send_sem,
            recv_sem=recv_sem,
            device_id=device,
            device_id_type=MESH,
        )
        copy.start()

    def arrived(ref, sem):
        pltpu.make_async_copy(ref, ref, sem).wait()

    barrier = pltpu.get_barrier_semaphore()
    partners = [sibling] + [at_x(step) for step in range(1, X)]
    partners += [at_z(step) for step in range(1, Z)]
    partners += [at_y(lax.rem(y + step, Y)) for step in range(1, Y)]
    for partner in partners:
        pl.semaphore_signal(barrier, inc=1, device_id=partner, device_id_type=MESH)
    pl.semaphore_wait(barrier, len(partners))

    def w_columns(block, x_to):
        start = pl.multiple_of((block * X + x_to) * width, width)
        return pl.ds(start, width)

    my_rows = pl.ds(pl.multiple_of(core * half, half), half)
    x_far = xs(sign)

    def w_far(block, carry):
        send(w_ref.at[my_rows, w_columns(block, opp)], wrelay.at[block], w_send.at[0], w_recv.at[0], (ctx, z * X + x_far))
        return carry

    def w_near(block, carry):
        send(w_ref.at[my_rows, w_columns(block, right)], wb.at[block, x, core], w_send.at[1], w_recv.at[1], at_x(1))
        send(w_ref.at[my_rows, w_columns(block, left)], wb.at[block, x, core], w_send.at[2], w_recv.at[2], at_x(-1))
        return carry

    def w_mine(block, carry):
        for part in range(2):
            pltpu.make_async_copy(
                w_ref.at[pl.ds(part * half, half), w_columns(block, x)], wb.at[block, x, part], w_own
            ).start()
        return carry

    lax.fori_loop(0, Z, w_far, 0)
    lax.fori_loop(0, Z, w_near, 0)
    lax.fori_loop(0, Z, w_mine, 0)

    row = lax.broadcasted_iota(jnp.int32, (tokens, tokens), 0)
    column = lax.broadcasted_iota(jnp.int32, (tokens, tokens), 1)
    causal = row >= column
    cum = lax.dot_general(
        jnp.where(causal, 1.0, 0.0).astype(F32),
        ld_ref[...],
        (((1,), (0,)), ((), ())),
        precision=lax.Precision.HIGHEST,
        preferred_element_type=F32,
    )
    cums = [cum[:, h : h + 1] for h in range(heads)]
    totals = [c[tokens - 1 : tokens, :] for c in cums]
    bown[...] = jnp.zeros_like(bown)
    for h in range(heads):
        bown[h : h + 1, :] = jnp.broadcast_to(totals[h], (1, 128))
    send(bown, bsib, b_send, b_recv, sibling)

    def lanes(h):
        return slice(h * DH, (h + 1) * DH)

    own = []
    for h in range(heads):
        decayed = (k_ref[:, lanes(h)].astype(F32) * jnp.exp(totals[h] - cums[h])).astype(BF16)
        kdec[:, lanes(h)] = decayed
        own.append(tn(decayed, v_ref[:, lanes(h)]))

    def of_core(pair):
        return jnp.where(is_zero, pair[0], pair[1])

    def scan_share(turn, states):
        s_out[turn] = of_core((states[1], states[0])).astype(BF16)
        s_keep[turn] = of_core((states[0], states[1]))
        send(s_out.at[turn], s_in.at[turn], s_send.at[turn], s_recv.at[turn], sibling)

    def scan_way(turn):
        step = 1 if turn == 0 else -1
        first_here = is_zero if turn == 0 else jnp.logical_not(is_zero)
        return step, first_here

    def decays(ref):
        return of_core((ref[0:1, :], ref[1:2, :]))

    def reaches(place):
        return jnp.logical_and(place >= 0, place < Y)

    def scan_send(turn):
        step, first_here = scan_way(turn)
        arrived(s_in.at[turn], s_recv.at[turn])
        mine = s_keep[turn]
        theirs = s_in[turn].astype(F32)
        first = jnp.where(first_here, mine, theirs)
        second = jnp.where(first_here, theirs, mine)
        s_keep[turn] = first
        b_second = jnp.where(first_here, decays(bsib), decays(bown))
        t_out[turn] = (jnp.exp(b_second) * first + second).astype(BF16)
        for distance in range(1, Y):
            place = y + step * distance

            @pl.when(reaches(place))
            def _():
                send(
                    t_out.at[turn],
                    t_in.at[turn, distance - 1],
                    t_send.at[turn, distance - 1],
                    t_recv.at[turn, distance - 1],
                    at_y(place),
                )

    def scan_end(turn):
        step, first_here = scan_way(turn)
        c_acc[...] = jnp.zeros_like(c_acc)
        d_acc[...] = jnp.zeros_like(d_acc)
        for distance in range(1, Y):
            place = y - step * distance

            @pl.when(reaches(place))
            def _():
                slot = t_in.at[turn, distance - 1]
                arrived(slot, t_recv.at[turn, distance - 1])
                between = d_acc[0:1, :]
                c_acc[...] += jnp.exp(between) * slot[...].astype(F32)
                d_acc[0:1, :] = between + decays(bchip.at[place])

        b_first = jnp.where(first_here, decays(bown), decays(bsib))
        carried = c_acc[...]
        after = jnp.exp(b_first) * carried + s_keep[turn]
        state[turn, core] = jnp.where(first_here, carried, after).astype(BF16)
        c_out[turn] = jnp.where(first_here, after, carried).astype(BF16)
        send(c_out.at[turn], state.at[turn, core], c_send.at[turn], c_recv.at[turn], sibling)
        arrived(c_out.at[turn], c_recv.at[turn])

    scan_share(0, own)

    arrived(bsib, b_recv)
    bchip[y] = bown[...] + bsib[...]
    for distance in range(1, Y):
        place = lax.rem(y + distance, Y)
        send(bchip.at[y], bchip.at[y], bc_send.at[distance - 1], bc_recv.at[distance - 1], at_y(place))
    scan_send(0)

    for h in range(heads):
        gaps = cums[h] - as_row(cums[h])
        decay = jnp.where(causal, jnp.exp(jnp.minimum(gaps, 0.0)), 0.0)
        weight[h] = decay
        probs[h] = (nt(q_ref[:, lanes(h)], k_ref[:, lanes(h)]) * decay).astype(BF16)
        att[:, lanes(h)] = nn(probs[h], v_ref[:, lanes(h)])
    targett[...] = nt(identity(rows), target_ref[...])

    for distance in range(1, Y):
        arrived(bchip.at[lax.rem(y - distance + Y, Y)], bc_recv.at[distance - 1])

    arrived(wrelay, w_recv.at[0])
    send(wrelay, wb.at[:, xs(-sign), core], w_send.at[3], w_recv.at[3], (ctx, z * X + x_far))

    scan_end(0)

    gain = gain_ref[...]
    squares = jnp.zeros((tokens, 1), F32)
    for h in range(heads):
        from_state = nn(q_ref[:, lanes(h)], state[0, h]) * jnp.exp(cums[h])
        attended = att[:, lanes(h)] + from_state
        att[:, lanes(h)] = attended
        squares = squares + jnp.sum(attended * attended, axis=1, keepdims=True)
        gate_open = jax.nn.sigmoid(gate_ref[:, lanes(h)].astype(F32))
        uall[z, :, lanes(h)] = (attended * gain[:, lanes(h)] * gate_open).astype(BF16)

    far, near = Z // 2, Z - 1 - Z // 2
    hops = (far, near)
    ways = (sign, -sign)

    def u_part(way, step, part):
        return uall.at[zs(-ways[way] * step), pl.ds(part * half_tokens, half_tokens)]

    def u_start(way, step, part):
        ref = u_part(way, step, part)
        send(ref, ref, u_send.at[way, step, part], u_recv.at[way, step, part], at_z(ways[way]))

    for part in range(2):
        for way in range(2):
            if hops[way] > 0:
                u_start(way, 0, part)

    def small_share(turn, value):
        small_z[turn, 0] = value
        for step in range(1, Z):
            send(small_z.at[turn, 0], small_z.at[turn, step], sz_send.at[turn, step - 1], sz_recv.at[turn, step - 1], at_z(step))

    def small_cross(turn):
        for step in range(1, Z):
            arrived(small_z.at[turn, step], sz_recv.at[turn, step - 1])
        sum_z = small_z[turn, 0]
        for step in range(1, Z):
            sum_z = sum_z + small_z[turn, step]
        small_x[turn, 0] = sum_z
        for step in range(1, X):
            send(small_x.at[turn, 0], small_x.at[turn, step], sx_send.at[turn, step - 1], sx_recv.at[turn, step - 1], at_x(step))

    def small_sum(turn):
        for step in range(1, X):
            arrived(small_x.at[turn, step], sx_recv.at[turn, step - 1])
        sum_x = small_x[turn, 0]
        for step in range(1, X):
            sum_x = sum_x + small_x[turn, step]
        return sum_x

    small_share(0, as_row(squares))

    def w_pair(source, sem, slot):
        ref = wb.at[:, source, core]
        arrived(ref, sem)
        send(ref, ref, ws_send.at[slot], ws_recv.at[slot], sibling)

    w_pair(left, w_recv.at[1], 0)
    w_pair(right, w_recv.at[2], 1)
    w_pair(opp, w_recv.at[3], 2)
    for part in range(2):
        arrived(wb.at[:, x, part], w_own)
    for slot, source in enumerate((left, right, opp)):
        arrived(wb.at[:, source, 1 - core], ws_recv.at[slot])

    def w_block(block):
        return wb[block].reshape(X * rows, width)

    yacc[...] = nt(w_block(z), uall[z]).reshape(yacc.shape)

    def accumulate(block):
        yacc[...] += nt(w_block(block), uall[block]).reshape(yacc.shape)

    for step in range(far):
        for part in range(2):
            for way in range(2):
                if step < hops[way]:
                    arrived(u_part(way, step + 1, part), u_recv.at[way, step, part])
                    if step + 1 < hops[way]:
                        u_start(way, step + 1, part)
        for way in range(2):
            if step < hops[way]:
                accumulate(zs(-ways[way] * (step + 1)))

    small_cross(0)

    def y_start(kind, part, value, device):
        ystage[kind, part] = value.astype(BF16)
        send(ystage.at[kind, part], yrecv.at[kind, part], y_send.at[kind, part], y_recv.at[kind, part], device)

    y_start(0, 0, yacc[opp, 0], at_x(1))
    y_start(0, 1, yacc[opp, 1], at_x(-1))
    y_start(1, 1, yacc[right, 1], at_x(1))
    y_start(1, 0, yacc[left, 0], at_x(-1))
    arrived(yrecv.at[0, 0], y_recv.at[0, 0])
    y_start(2, 0, yacc[right, 0] + yrecv[0, 0].astype(F32), at_x(1))
    arrived(yrecv.at[0, 1], y_recv.at[0, 1])
    y_start(2, 1, yacc[left, 1] + yrecv[0, 1].astype(F32), at_x(-1))

    mean_square = small_sum(0) / total_features
    inv_rms = lax.rsqrt(mean_square + EPS)

    product = jnp.zeros((1, tokens), F32)
    outs = []
    for part in range(2):
        for kind in (1, 2):
            arrived(yrecv.at[kind, part], y_recv.at[kind, part])
        total = yacc[x, part] + yrecv[1, part].astype(F32) + yrecv[2, part].astype(F32)
        out_half = (total * inv_rms).astype(BF16)
        grad = (out_half.astype(F32) - targett[part * half : (part + 1) * half, :]).astype(BF16)
        gx[x, part] = grad
        outs.append(out_half)
        product = product + jnp.sum(grad.astype(F32) * total, axis=0, keepdims=True)

    def g_start(source, part, kind, device):
        ref = gx.at[source, part]
        send(ref, ref, g_send.at[kind, part], g_recv.at[kind, part], device)

    g_start(x, 0, 0, at_x(1))
    g_start(x, 1, 1, at_x(-1))
    g_start(x, 1, 0, at_x(1))
    g_start(x, 0, 1, at_x(-1))
    small_share(1, product)
    eye = identity(tokens)
    out_ref[...] = nt(eye, jnp.concatenate(outs, axis=0)).astype(BF16)
    arrived(gx.at[left, 0], g_recv.at[0, 0])
    g_start(left, 0, 2, at_x(1))
    arrived(gx.at[right, 1], g_recv.at[1, 1])
    g_start(right, 1, 2, at_x(-1))
    arrived(gx.at[left, 1], g_recv.at[0, 1])
    arrived(gx.at[right, 0], g_recv.at[1, 0])
    small_cross(1)
    for part in range(2):
        arrived(gx.at[opp, part], g_recv.at[2, part])
    gall[...] = nt(eye, gx[...].reshape(X * rows, tokens)).astype(BF16)

    def feature_part(block):
        return nn(gall[...], w_block(block))

    def f_slot(way, step):
        return way * far + step

    def f_start(way, step, part, value):
        piece = pl.ds(part * half_tokens, half_tokens)
        slot = f_slot(way, step)
        fstage[slot, piece] = value.astype(BF16)
        send(fstage.at[slot, piece], frecv.at[slot, piece], f_send.at[slot, part], f_recv.at[slot, part], at_z(ways[way]))

    def f_arrived(way, step, part):
        piece = pl.ds(part * half_tokens, half_tokens)
        slot = f_slot(way, step)
        arrived(frecv.at[slot, piece], f_recv.at[slot, part])
        return frecv[slot, piece].astype(F32)

    for step in range(far):
        sums = [feature_part(zs(ways[way] * (hops[way] - step))) if step < hops[way] else None for way in range(2)]
        for part in range(2):
            for way in range(2):
                if step < hops[way]:
                    value = sums[way][part * half_tokens : (part + 1) * half_tokens, :]
                    if step > 0:
                        value = value + f_arrived(way, step - 1, part)
                    f_start(way, step, part, value)

    own_feature = feature_part(z)
    mean_product = small_sum(1) / total_features
    inv = as_columns(inv_rms)
    mean_product = as_columns(mean_product)
    feature = []
    for part in range(2):
        value = own_feature[part * half_tokens : (part + 1) * half_tokens, :]
        for way in range(2):
            if hops[way] > 0:
                value = value + f_arrived(way, hops[way] - 1, part)
        feature.append(value)
    feature_grad = jnp.concatenate(feature, axis=0)

    own = []
    for h in range(heads):
        attended = att[:, lanes(h)]
        gate_open = jax.nn.sigmoid(gate_ref[:, lanes(h)].astype(F32))
        normed_grad = feature_grad[:, lanes(h)] * gain[:, lanes(h)] * gate_open
        gg_ref[:, lanes(h)] = (normed_grad * attended * inv * (1.0 - gate_open)).astype(BF16)
        grad = (inv * normed_grad - inv * inv * inv * attended * mean_product).astype(BF16)
        agrad[:, lanes(h)] = grad
        decayed = (q_ref[:, lanes(h)].astype(F32) * jnp.exp(cums[h])).astype(BF16)
        own.append(tn(decayed, grad))

    scan_share(1, own)
    for h in range(heads):
        grad = agrad[:, lanes(h)]
        score_grad = (nt(grad, v_ref[:, lanes(h)]) * weight[h]).astype(BF16)
        if h == 0:
            scan_send(1)
        qg_ref[:, lanes(h)] = (
            nn(score_grad, k_ref[:, lanes(h)]) + jnp.exp(cums[h]) * nt(grad, state[0, h])
        ).astype(BF16)
        klocal[:, lanes(h)] = tn(score_grad, q_ref[:, lanes(h)])
        vlocal[:, lanes(h)] = tn(probs[h], grad)
    scan_end(1)
    for h in range(heads):
        later = state[1, h]
        kg_ref[:, lanes(h)] = (
            klocal[:, lanes(h)] + jnp.exp(totals[h] - cums[h]) * nt(v_ref[:, lanes(h)], later)
        ).astype(BF16)
        vg_ref[:, lanes(h)] = (vlocal[:, lanes(h)] + nn(kdec[:, lanes(h)], later)).astype(BF16)

    for index in range(4):
        arrived(wrelay, w_send.at[index])
    for index in range(3):
        arrived(wrelay, ws_send.at[index])
    for way in range(2):
        for step in range(hops[way]):
            for part in range(2):
                arrived(u_part(way, step, part), u_send.at[way, step, part])
                arrived(u_part(way, step, part), f_send.at[f_slot(way, step), part])
    for kind in range(3):
        for part in range(2):
            arrived(ystage.at[kind, part], y_send.at[kind, part])
            arrived(ystage.at[kind, part], g_send.at[kind, part])
    arrived(bown, b_send)
    for distance in range(1, Y):
        arrived(bown, bc_send.at[distance - 1])
    for turn in range(2):
        arrived(s_out.at[turn], s_send.at[turn])
        arrived(c_out.at[turn], c_send.at[turn])
        step, _ = scan_way(turn)
        for distance in range(1, Y):

            @pl.when(reaches(y + step * distance))
            def _():
                arrived(t_out.at[turn], t_send.at[turn, distance - 1])

        for distance in range(1, Z):
            arrived(small_z.at[turn, 0], sz_send.at[turn, distance - 1])
        for distance in range(1, X):
            arrived(small_x.at[turn, 0], sx_send.at[turn, distance - 1])


def on_device(chips, queries, keys, values, log_decay, gate, norm_gain, out_weight, target):
    Y, Z = chips
    tokens, width = queries.shape
    rows, features = out_weight.shape
    half = rows // 2
    far = Z // 2
    vmem = pltpu.VMEM
    dma = pltpu.SemaphoreType.DMA
    scratch = [
        vmem((Z, X, 2, half, width), BF16),
        vmem((Z, half, width), BF16),
        vmem((Z, tokens, width), BF16),
        vmem((X, 2, half, tokens), F32),
        vmem((3, 2, half, tokens), BF16),
        vmem((3, 2, half, tokens), BF16),
        vmem((X, 2, half, tokens), BF16),
        vmem((tokens, X * rows), BF16),
        vmem((Z - 1, tokens, width), BF16),
        vmem((Z - 1, tokens, width), BF16),
        vmem((width // DH, tokens, tokens), F32),
        vmem((width // DH, tokens, tokens), BF16),
        vmem((tokens, width), BF16),
        vmem((tokens, width), F32),
        vmem((tokens, width), F32),
        vmem((tokens, width), F32),
        vmem((rows, tokens), F32),
        vmem((tokens, width), BF16),
        vmem((8, 128), F32),
        vmem((8, 128), F32),
        vmem((Y, 8, 128), F32),
        vmem((2, DH, DH), BF16),
        vmem((2, DH, DH), BF16),
        vmem((2, DH, DH), F32),
        vmem((2, DH, DH), BF16),
        vmem((2, max(Y - 1, 1), DH, DH), BF16),
        vmem((DH, DH), F32),
        vmem((8, 128), F32),
        vmem((2, DH, DH), BF16),
        vmem((2, 2, DH, DH), BF16),
        vmem((2, Z, 1, tokens), F32),
        vmem((2, X, 1, tokens), F32),
        dma((4,)),
        dma((4,)),
        dma,
        dma((3,)),
        dma((3,)),
        dma((2, far, 2)),
        dma((2, far, 2)),
        dma((3, 2)),
        dma((3, 2)),
        dma((3, 2)),
        dma((3, 2)),
        dma((Z - 1, 2)),
        dma((Z - 1, 2)),
        dma,
        dma,
        dma((max(Y - 1, 1),)),
        dma((max(Y - 1, 1),)),
        dma((2,)),
        dma((2,)),
        dma((2, max(Y - 1, 1))),
        dma((2, max(Y - 1, 1))),
        dma((2,)),
        dma((2,)),
        dma((2, Z - 1)),
        dma((2, Z - 1)),
        dma((2, X - 1)),
        dma((2, X - 1)),
    ]
    in_vmem = pl.BlockSpec(memory_space=pltpu.VMEM)
    wide = jax.ShapeDtypeStruct((tokens, width), BF16)
    return pl.pallas_call(
        functools.partial(kernel, chips),
        out_shape=(jax.ShapeDtypeStruct((tokens, rows), BF16), wide, wide, wide, wide),
        in_specs=[in_vmem] * 6 + [pl.BlockSpec(memory_space=pl.ANY), in_vmem],
        out_specs=(in_vmem,) * 5,
        scratch_shapes=scratch,
        compiler_params=pltpu.CompilerParams(
            collective_id=0, has_side_effects=True, vmem_limit_bytes=48 * 1024 * 1024
        ),
        cost_estimate=pl.CostEstimate(flops=2 * 10**9, bytes_accessed=8 * 10**6, transcendentals=10**6),
        name="attention_layer",
    )(queries, keys, values, log_decay, gate, norm_gain.reshape(1, width), out_weight, target)


def solution(mesh):
    chips = (mesh.shape["ctx"] // 2, mesh.shape["tp"] // X)
    return jax.shard_map(
        functools.partial(on_device, chips),
        mesh=mesh,
        in_specs=(
            P("ctx", "tp"),
            P("ctx", "tp"),
            P("ctx", "tp"),
            P("ctx", "tp"),
            P("ctx", "tp"),
            P("tp"),
            P("tp", None),
            P("ctx", "tp"),
        ),
        out_specs=(P("ctx", "tp"),) * 5,
        check_vma=False,
    )
```

```python
import functools

import jax
import jax.numpy as jnp
from jax import lax
from jax.experimental import pallas as pl
from jax.experimental.pallas import tpu as pltpu
from jax.sharding import PartitionSpec as P

DH = 128
EPS = 1e-06
MESH = pl.DeviceIdType.MESH
F32 = jnp.float32
BF16 = jnp.bfloat16
X = 4


def nn(a, b):
    return lax.dot_general(a, b, (((1,), (0,)), ((), ())), preferred_element_type=F32)


def nt(a, b):
    return lax.dot_general(a, b, (((1,), (1,)), ((), ())), preferred_element_type=F32)


def tn(a, b):
    return lax.dot_general(a, b, (((0,), (0,)), ((), ())), preferred_element_type=F32)


def identity(size):
    row = lax.broadcasted_iota(jnp.int32, (size, size), 0)
    column = lax.broadcasted_iota(jnp.int32, (size, size), 1)
    return jnp.where(row == column, 1.0, 0.0).astype(BF16)


def as_row(column):
    return jnp.broadcast_to(column, (column.shape[0], 128)).T[0:1, :]


def as_columns(row):
    return jnp.broadcast_to(row, (128, row.shape[1])).T


def kernel(
    sizes,
    q_in,
    k_in,
    v_in,
    ld_in,
    gate_in,
    gain_in,
    w_ref,
    target_in,
    out_ref,
    qg_ref,
    kg_ref,
    vg_ref,
    gg_ref,
    q_ref,
    k_ref,
    v_ref,
    ld_ref,
    gate_ref,
    gain_ref,
    target_ref,
    in_sems,
    wb,
    wrelay,
    uall,
    yacc,
    ystage,
    yrecv,
    gx,
    gall,
    fstage,
    frecv,
    weight,
    probs,
    kdec,
    att,
    klocal,
    vlocal,
    agrad,
    bown,
    bsib,
    bchip,
    s_out,
    s_in,
    s_keep,
    t_out,
    t_in,
    c_acc,
    d_acc,
    c_out,
    state,
    small_z,
    small_x,
    w_send,
    w_recv,
    w_own,
    ws_send,
    ws_recv,
    u_send,
    u_recv,
    y_send,
    y_recv,
    g_send,
    g_recv,
    f_send,
    f_recv,
    b_send,
    b_recv,
    bc_send,
    bc_recv,
    s_send,
    s_recv,
    t_send,
    t_recv,
    c_send,
    c_recv,
    sz_send,
    sz_recv,
    sx_send,
    sx_recv,
):
    Y, Z = sizes
    tokens = q_ref.shape[0]
    half_tokens = tokens // 2
    rows = w_ref.shape[0]
    half = rows // 2
    width = q_ref.shape[1]
    total_features = w_ref.shape[1]
    heads = width // DH

    ctx = lax.axis_index("ctx")
    tp = lax.axis_index("tp")
    core = lax.rem(ctx, 2)
    y = lax.div(ctx, 2)
    x = lax.rem(tp, X)
    z = lax.div(tp, X)
    sibling = (y * 2 + 1 - core, tp)
    is_zero = core == 0

    def xs(step):
        return lax.rem(x + step + X, X)

    def zs(step):
        return lax.rem(z + step + 2 * Z, Z)

    def at_x(step):
        return (ctx, z * X + xs(step))

    def at_z(step):
        return (ctx, zs(step) * X + x)

    def at_y(place):
        return (place * 2 + core, tp)

    sign = 1 - 2 * core
    left, right, opp = xs(-1), xs(1), xs(2)

    def send(src, dst, send_sem, recv_sem, device):
        copy = pltpu.make_async_remote_copy(
            src_ref=src,
            dst_ref=dst,
            send_sem=send_sem,
            recv_sem=recv_sem,
            device_id=device,
            device_id_type=MESH,
        )
        copy.start()

    def arrived(ref, sem):
        pltpu.make_async_copy(ref, ref, sem).wait()

    loads = [
        pltpu.make_async_copy(src, dst, in_sems.at[index])
        for index, (src, dst) in enumerate(
            (
                (ld_in, ld_ref),
                (k_in, k_ref),
                (v_in, v_ref),
                (q_in, q_ref),
                (gate_in, gate_ref),
                (gain_in, gain_ref),
                (target_in, target_ref),
            )
        )
    ]
    for load in loads:
        load.start()
    barrier = pltpu.get_barrier_semaphore()
    partners = [sibling] + [at_x(step) for step in range(1, X)]
    partners += [at_z(step) for step in range(1, Z)]
    partners += [at_y(lax.rem(y + step, Y)) for step in range(1, Y)]
    for partner in partners:
        pl.semaphore_signal(barrier, inc=1, device_id=partner, device_id_type=MESH)

    def w_columns(block, x_to):
        start = pl.multiple_of((block * X + x_to) * width, width)
        return pl.ds(start, width)

    my_rows = pl.ds(pl.multiple_of(core * half, half), half)
    x_far = xs(sign)

    def w_far(block, carry):
        send(w_ref.at[my_rows, w_columns(block, opp)], wrelay.at[block], w_send.at[0], w_recv.at[0], (ctx, z * X + x_far))
        return carry

    def w_near(block, carry):
        send(w_ref.at[my_rows, w_columns(block, right)], wb.at[block, x, core], w_send.at[1], w_recv.at[1], at_x(1))
        send(w_ref.at[my_rows, w_columns(block, left)], wb.at[block, x, core], w_send.at[2], w_recv.at[2], at_x(-1))
        return carry

    def w_mine(block, carry):
        for part in range(2):
            pltpu.make_async_copy(
                w_ref.at[pl.ds(part * half, half), w_columns(block, x)], wb.at[block, x, part], w_own
            ).start()
        return carry

    row = lax.broadcasted_iota(jnp.int32, (tokens, tokens), 0)
    column = lax.broadcasted_iota(jnp.int32, (tokens, tokens), 1)
    causal = row >= column
    loads[0].wait()
    cum = lax.dot_general(
        ld_ref[...],
        jnp.where(row <= column, 1.0, 0.0).astype(F32),
        (((1,), (0,)), ((), ())),
        precision=lax.Precision.HIGHEST,
        preferred_element_type=F32,
    )
    cum_rows = [cum[h : h + 1, :] for h in range(heads)]
    cums = [as_columns(c) for c in cum_rows]
    totals = [c[tokens - 1 : tokens, :] for c in cums]
    bown[...] = jnp.zeros_like(bown)
    for h in range(heads):
        bown[h : h + 1, :] = totals[h]
    loads[1].wait()
    loads[2].wait()

    def lanes(h):
        return slice(h * DH, (h + 1) * DH)

    own = []
    for h in range(heads):
        decayed = (k_ref[:, lanes(h)].astype(F32) * jnp.exp(totals[h] - cums[h])).astype(BF16)
        kdec[:, lanes(h)] = decayed
        own.append(tn(decayed, v_ref[:, lanes(h)]))

    def of_core(pair):
        return jnp.where(is_zero, pair[0], pair[1])

    def scan_share(turn, states):
        s_out[turn] = of_core((states[1], states[0])).astype(BF16)
        s_keep[turn] = of_core((states[0], states[1]))
        send(s_out.at[turn], s_in.at[turn], s_send.at[turn], s_recv.at[turn], sibling)

    def scan_way(turn):
        step = 1 if turn == 0 else -1
        first_here = is_zero if turn == 0 else jnp.logical_not(is_zero)
        return step, first_here

    def decays(ref):
        return of_core((ref[0:1, :], ref[1:2, :]))

    def reaches(place):
        return jnp.logical_and(place >= 0, place < Y)

    def scan_send(turn):
        step, first_here = scan_way(turn)
        arrived(s_in.at[turn], s_recv.at[turn])
        mine = s_keep[turn]
        theirs = s_in[turn].astype(F32)
        first = jnp.where(first_here, mine, theirs)
        second = jnp.where(first_here, theirs, mine)
        s_keep[turn] = first
        b_second = jnp.where(first_here, decays(bsib), decays(bown))
        t_out[turn] = (jnp.exp(b_second) * first + second).astype(BF16)
        for distance in range(1, Y):
            place = y + step * distance

            @pl.when(reaches(place))
            def _():
                send(
                    t_out.at[turn],
                    t_in.at[turn, distance - 1],
                    t_send.at[turn, distance - 1],
                    t_recv.at[turn, distance - 1],
                    at_y(place),
                )

    def scan_end(turn):
        step, first_here = scan_way(turn)
        c_acc[...] = jnp.zeros_like(c_acc)
        d_acc[...] = jnp.zeros_like(d_acc)
        for distance in range(1, Y):
            place = y - step * distance

            @pl.when(reaches(place))
            def _():
                slot = t_in.at[turn, distance - 1]
                arrived(slot, t_recv.at[turn, distance - 1])
                between = d_acc[0:1, :]
                c_acc[...] += jnp.exp(between) * slot[...].astype(F32)
                d_acc[0:1, :] = between + decays(bchip.at[place])

        b_first = jnp.where(first_here, decays(bown), decays(bsib))
        carried = c_acc[...]
        after = jnp.exp(b_first) * carried + s_keep[turn]
        state[turn, core] = jnp.where(first_here, carried, after).astype(BF16)
        c_out[turn] = jnp.where(first_here, after, carried).astype(BF16)
        send(c_out.at[turn], state.at[turn, core], c_send.at[turn], c_recv.at[turn], sibling)
        arrived(c_out.at[turn], c_recv.at[turn])

    pl.semaphore_wait(barrier, len(partners))
    scan_share(0, own)
    send(bown, bsib, b_send, b_recv, sibling)
    lax.fori_loop(0, Z, w_far, 0)
    lax.fori_loop(0, Z, w_near, 0)
    lax.fori_loop(0, Z, w_mine, 0)

    arrived(bsib, b_recv)
    bchip[y] = bown[...] + bsib[...]
    for distance in range(1, Y):
        place = lax.rem(y + distance, Y)
        send(bchip.at[y], bchip.at[y], bc_send.at[distance - 1], bc_recv.at[distance - 1], at_y(place))
    scan_send(0)

    for load in loads[3:]:
        load.wait()
    for h in range(heads):
        gaps = cums[h][:, 0:1] - cum_rows[h]
        decay = jnp.where(causal, jnp.exp(jnp.minimum(gaps, 0.0)), 0.0)
        weight[h] = decay
        probs[h] = (nt(q_ref[:, lanes(h)], k_ref[:, lanes(h)]) * decay).astype(BF16)
        att[:, lanes(h)] = nn(probs[h], v_ref[:, lanes(h)])

    for distance in range(1, Y):
        arrived(bchip.at[lax.rem(y - distance + Y, Y)], bc_recv.at[distance - 1])

    arrived(wrelay, w_recv.at[0])
    send(wrelay, wb.at[:, xs(-sign), core], w_send.at[3], w_recv.at[3], (ctx, z * X + x_far))

    scan_end(0)

    gain = gain_ref[...]
    squares = jnp.zeros((tokens, 1), F32)
    for h in range(heads):
        from_state = nn(q_ref[:, lanes(h)], state[0, h]) * jnp.exp(cums[h])
        attended = att[:, lanes(h)] + from_state
        att[:, lanes(h)] = attended
        squares = squares + jnp.sum(attended * attended, axis=1, keepdims=True)
        gate_open = jax.nn.sigmoid(gate_ref[:, lanes(h)].astype(F32))
        uall[z, :, lanes(h)] = (attended * gain[:, lanes(h)] * gate_open).astype(BF16)

    far, near = Z // 2, Z - 1 - Z // 2
    hops = (far, near)
    ways = (sign, -sign)

    def u_part(way, step, part):
        return uall.at[zs(-ways[way] * step), pl.ds(part * half_tokens, half_tokens)]

    def u_start(way, step, part):
        ref = u_part(way, step, part)
        send(ref, ref, u_send.at[way, step, part], u_recv.at[way, step, part], at_z(ways[way]))

    for part in range(2):
        for way in range(2):
            if hops[way] > 0:
                u_start(way, 0, part)

    def small_share(turn, value):
        small_z[turn, 0] = value
        for step in range(1, Z):
            send(small_z.at[turn, 0], small_z.at[turn, step], sz_send.at[turn, step - 1], sz_recv.at[turn, step - 1], at_z(step))

    def small_cross(turn):
        for step in range(1, Z):
            arrived(small_z.at[turn, step], sz_recv.at[turn, step - 1])
        sum_z = small_z[turn, 0]
        for step in range(1, Z):
            sum_z = sum_z + small_z[turn, step]
        small_x[turn, 0] = sum_z
        for step in range(1, X):
            send(small_x.at[turn, 0], small_x.at[turn, step], sx_send.at[turn, step - 1], sx_recv.at[turn, step - 1], at_x(step))

    def small_sum(turn):
        for step in range(1, X):
            arrived(small_x.at[turn, step], sx_recv.at[turn, step - 1])
        sum_x = small_x[turn, 0]
        for step in range(1, X):
            sum_x = sum_x + small_x[turn, step]
        return sum_x

    small_share(0, as_row(squares))

    def w_pair(source, sem, slot):
        ref = wb.at[:, source, core]
        arrived(ref, sem)
        send(ref, ref, ws_send.at[slot], ws_recv.at[slot], sibling)

    w_pair(left, w_recv.at[1], 0)
    w_pair(right, w_recv.at[2], 1)
    w_pair(opp, w_recv.at[3], 2)
    for part in range(2):
        arrived(wb.at[:, x, part], w_own)
    for slot, source in enumerate((left, right, opp)):
        arrived(wb.at[:, source, 1 - core], ws_recv.at[slot])

    def w_block(block):
        return wb[block].reshape(X * rows, width)

    yacc[...] = nt(w_block(z), uall[z]).reshape(yacc.shape)

    def accumulate(block):
        yacc[...] += nt(w_block(block), uall[block]).reshape(yacc.shape)

    for step in range(far):
        for part in range(2):
            for way in range(2):
                if step < hops[way]:
                    arrived(u_part(way, step + 1, part), u_recv.at[way, step, part])
                    if step + 1 < hops[way]:
                        u_start(way, step + 1, part)
        for way in range(2):
            if step < hops[way]:
                accumulate(zs(-ways[way] * (step + 1)))

    small_cross(0)

    def y_start(kind, part, value, device):
        ystage[kind, part] = value.astype(BF16)
        send(ystage.at[kind, part], yrecv.at[kind, part], y_send.at[kind, part], y_recv.at[kind, part], device)

    y_start(0, 0, yacc[opp, 0], at_x(1))
    y_start(0, 1, yacc[opp, 1], at_x(-1))
    y_start(1, 1, yacc[right, 1], at_x(1))
    y_start(1, 0, yacc[left, 0], at_x(-1))
    arrived(yrecv.at[0, 0], y_recv.at[0, 0])
    y_start(2, 0, yacc[right, 0] + yrecv[0, 0].astype(F32), at_x(1))
    arrived(yrecv.at[0, 1], y_recv.at[0, 1])
    y_start(2, 1, yacc[left, 1] + yrecv[0, 1].astype(F32), at_x(-1))

    mean_square = small_sum(0) / total_features
    inv_rms = lax.rsqrt(mean_square + EPS)

    product = jnp.zeros((1, tokens), F32)
    for part in range(2):
        for kind in (1, 2):
            arrived(yrecv.at[kind, part], y_recv.at[kind, part])
        total = yacc[x, part] + yrecv[1, part].astype(F32) + yrecv[2, part].astype(F32)
        out_half = (total * inv_rms).astype(BF16)
        grad = (out_half.astype(F32) - target_ref[part * half : (part + 1) * half, :].astype(F32)).astype(BF16)
        gx[x, part] = grad
        out_ref[part * half : (part + 1) * half, :] = out_half
        product = product + jnp.sum(grad.astype(F32) * total, axis=0, keepdims=True)

    def g_start(source, part, kind, device):
        ref = gx.at[source, part]
        send(ref, ref, g_send.at[kind, part], g_recv.at[kind, part], device)

    g_start(x, 0, 0, at_x(1))
    g_start(x, 1, 1, at_x(-1))
    g_start(x, 1, 0, at_x(1))
    g_start(x, 0, 1, at_x(-1))
    small_share(1, product)
    eye = identity(tokens)
    arrived(gx.at[left, 0], g_recv.at[0, 0])
    g_start(left, 0, 2, at_x(1))
    arrived(gx.at[right, 1], g_recv.at[1, 1])
    g_start(right, 1, 2, at_x(-1))
    arrived(gx.at[left, 1], g_recv.at[0, 1])
    arrived(gx.at[right, 0], g_recv.at[1, 0])
    small_cross(1)
    for part in range(2):
        arrived(gx.at[opp, part], g_recv.at[2, part])
    gall[...] = nt(eye, gx[...].reshape(X * rows, tokens)).astype(BF16)

    def feature_part(block):
        return nn(gall[...], w_block(block))

    def f_slot(way, step):
        return way * far + step

    def f_start(way, step, part, value):
        piece = pl.ds(part * half_tokens, half_tokens)
        slot = f_slot(way, step)
        fstage[slot, piece] = value.astype(BF16)
        send(fstage.at[slot, piece], frecv.at[slot, piece], f_send.at[slot, part], f_recv.at[slot, part], at_z(ways[way]))

    def f_arrived(way, step, part):
        piece = pl.ds(part * half_tokens, half_tokens)
        slot = f_slot(way, step)
        arrived(frecv.at[slot, piece], f_recv.at[slot, part])
        return frecv[slot, piece].astype(F32)

    for step in range(far):
        sums = [feature_part(zs(ways[way] * (hops[way] - step))) if step < hops[way] else None for way in range(2)]
        for part in range(2):
            for way in range(2):
                if step < hops[way]:
                    value = sums[way][part * half_tokens : (part + 1) * half_tokens, :]
                    if step > 0:
                        value = value + f_arrived(way, step - 1, part)
                    f_start(way, step, part, value)

    own_feature = feature_part(z)
    mean_product = small_sum(1) / total_features
    inv = as_columns(inv_rms)
    mean_product = as_columns(mean_product)
    feature = []
    for part in range(2):
        value = own_feature[part * half_tokens : (part + 1) * half_tokens, :]
        for way in range(2):
            if hops[way] > 0:
                value = value + f_arrived(way, hops[way] - 1, part)
        feature.append(value)
    feature_grad = jnp.concatenate(feature, axis=0)

    own = []
    for h in range(heads):
        attended = att[:, lanes(h)]
        gate_open = jax.nn.sigmoid(gate_ref[:, lanes(h)].astype(F32))
        normed_grad = feature_grad[:, lanes(h)] * gain[:, lanes(h)] * gate_open
        gg_ref[:, lanes(h)] = (normed_grad * attended * inv * (1.0 - gate_open)).astype(BF16)
        grad = (inv * normed_grad - inv * inv * inv * attended * mean_product).astype(BF16)
        agrad[:, lanes(h)] = grad
        decayed = (q_ref[:, lanes(h)].astype(F32) * jnp.exp(cums[h])).astype(BF16)
        own.append(tn(decayed, grad))

    scan_share(1, own)
    for h in range(heads):
        grad = agrad[:, lanes(h)]
        score_grad = (nt(grad, v_ref[:, lanes(h)]) * weight[h]).astype(BF16)
        if h == 0:
            scan_send(1)
        qg_ref[:, lanes(h)] = (
            nn(score_grad, k_ref[:, lanes(h)]) + jnp.exp(cums[h]) * nt(grad, state[0, h])
        ).astype(BF16)
        klocal[:, lanes(h)] = tn(score_grad, q_ref[:, lanes(h)])
        vlocal[:, lanes(h)] = tn(probs[h], grad)
    scan_end(1)
    for h in range(heads):
        later = state[1, h]
        kg_ref[:, lanes(h)] = (
            klocal[:, lanes(h)] + jnp.exp(totals[h] - cums[h]) * nt(v_ref[:, lanes(h)], later)
        ).astype(BF16)
        vg_ref[:, lanes(h)] = (vlocal[:, lanes(h)] + nn(kdec[:, lanes(h)], later)).astype(BF16)

    for index in range(4):
        arrived(wrelay, w_send.at[index])
    for index in range(3):
        arrived(wrelay, ws_send.at[index])
    for way in range(2):
        for step in range(hops[way]):
            for part in range(2):
                arrived(u_part(way, step, part), u_send.at[way, step, part])
                arrived(u_part(way, step, part), f_send.at[f_slot(way, step), part])
    for kind in range(3):
        for part in range(2):
            arrived(ystage.at[kind, part], y_send.at[kind, part])
            arrived(ystage.at[kind, part], g_send.at[kind, part])
    arrived(bown, b_send)
    for distance in range(1, Y):
        arrived(bown, bc_send.at[distance - 1])
    for turn in range(2):
        arrived(s_out.at[turn], s_send.at[turn])
        arrived(c_out.at[turn], c_send.at[turn])
        step, _ = scan_way(turn)
        for distance in range(1, Y):

            @pl.when(reaches(y + step * distance))
            def _():
                arrived(t_out.at[turn], t_send.at[turn, distance - 1])

        for distance in range(1, Z):
            arrived(small_z.at[turn, 0], sz_send.at[turn, distance - 1])
        for distance in range(1, X):
            arrived(small_x.at[turn, 0], sx_send.at[turn, distance - 1])


def store(*refs):
    count = len(refs) // 2
    sems = refs[-1]
    copies = [pltpu.make_async_copy(refs[i], refs[count + i], sems.at[i]) for i in range(count)]
    for copy in copies:
        copy.start()
    for copy in copies:
        copy.wait()


def on_device(chips, queries, keys, values, log_decay, gate, norm_gain, out_weight, target):
    Y, Z = chips
    tokens, width = queries.shape
    rows, features = out_weight.shape
    half = rows // 2
    far = Z // 2
    vmem = pltpu.VMEM
    dma = pltpu.SemaphoreType.DMA
    scratch = [
        vmem((tokens, width), BF16),
        vmem((tokens, width), BF16),
        vmem((tokens, width), BF16),
        vmem((width // DH, tokens), F32),
        vmem((tokens, width), BF16),
        vmem((1, width), F32),
        vmem((rows, tokens), BF16),
        dma((7,)),
        vmem((Z, X, 2, half, width), BF16),
        vmem((Z, half, width), BF16),
        vmem((Z, tokens, width), BF16),
        vmem((X, 2, half, tokens), F32),
        vmem((3, 2, half, tokens), BF16),
        vmem((3, 2, half, tokens), BF16),
        vmem((X, 2, half, tokens), BF16),
        vmem((tokens, X * rows), BF16),
        vmem((Z - 1, tokens, width), BF16),
        vmem((Z - 1, tokens, width), BF16),
        vmem((width // DH, tokens, tokens), F32),
        vmem((width // DH, tokens, tokens), BF16),
        vmem((tokens, width), BF16),
        vmem((tokens, width), F32),
        vmem((tokens, width), F32),
        vmem((tokens, width), F32),
        vmem((tokens, width), BF16),
        vmem((8, 128), F32),
        vmem((8, 128), F32),
        vmem((Y, 8, 128), F32),
        vmem((2, DH, DH), BF16),
        vmem((2, DH, DH), BF16),
        vmem((2, DH, DH), F32),
        vmem((2, DH, DH), BF16),
        vmem((2, max(Y - 1, 1), DH, DH), BF16),
        vmem((DH, DH), F32),
        vmem((8, 128), F32),
        vmem((2, DH, DH), BF16),
        vmem((2, 2, DH, DH), BF16),
        vmem((2, Z, 1, tokens), F32),
        vmem((2, X, 1, tokens), F32),
        dma((4,)),
        dma((4,)),
        dma,
        dma((3,)),
        dma((3,)),
        dma((2, far, 2)),
        dma((2, far, 2)),
        dma((3, 2)),
        dma((3, 2)),
        dma((3, 2)),
        dma((3, 2)),
        dma((Z - 1, 2)),
        dma((Z - 1, 2)),
        dma,
        dma,
        dma((max(Y - 1, 1),)),
        dma((max(Y - 1, 1),)),
        dma((2,)),
        dma((2,)),
        dma((2, max(Y - 1, 1))),
        dma((2, max(Y - 1, 1))),
        dma((2,)),
        dma((2,)),
        dma((2, Z - 1)),
        dma((2, Z - 1)),
        dma((2, X - 1)),
        dma((2, X - 1)),
    ]
    in_vmem = pl.BlockSpec(memory_space=pltpu.VMEM)
    in_hbm = pl.BlockSpec(memory_space=pltpu.HBM)
    wide = jax.ShapeDtypeStruct((tokens, width), BF16)
    out_shape = (jax.ShapeDtypeStruct((rows, tokens), BF16), wide, wide, wide, wide)
    results = pl.pallas_call(
        functools.partial(kernel, chips),
        out_shape=out_shape,
        in_specs=[in_hbm] * 8,
        out_specs=(in_vmem,) * 5,
        scratch_shapes=scratch,
        compiler_params=pltpu.CompilerParams(
            collective_id=0, has_side_effects=True, vmem_limit_bytes=63 * 1024 * 1024
        ),
        cost_estimate=pl.CostEstimate(flops=2 * 10**9, bytes_accessed=8 * 10**6, transcendentals=10**6),
        name="attention_layer",
    )(queries, keys, values, log_decay.T, gate, norm_gain.reshape(1, width), out_weight, target.T)
    output, *grads = pl.pallas_call(
        store,
        out_shape=out_shape,
        in_specs=[pl.BlockSpec(memory_space=pl.ANY)] * 5,
        out_specs=(in_hbm,) * 5,
        scratch_shapes=[dma((5,))],
        compiler_params=pltpu.CompilerParams(vmem_limit_bytes=63 * 1024 * 1024),
        name="store",
    )(*results)
    return (output.T, *grads)


def solution(mesh):
    chips = (mesh.shape["ctx"] // 2, mesh.shape["tp"] // X)
    return jax.shard_map(
        functools.partial(on_device, chips),
        mesh=mesh,
        in_specs=(
            P("ctx", "tp"),
            P("ctx", "tp"),
            P("ctx", "tp"),
            P("ctx", "tp"),
            P("ctx", "tp"),
            P("tp"),
            P("tp", None),
            P("ctx", "tp"),
        ),
        out_specs=(P("ctx", "tp"),) * 5,
        check_vma=False,
    )
```

```python
import functools

import jax
import jax.numpy as jnp
from jax import lax
from jax.experimental import pallas as pl
from jax.experimental.pallas import tpu as pltpu
from jax.sharding import PartitionSpec as P

DH = 128
EPS = 1e-06
MESH = pl.DeviceIdType.MESH
F32 = jnp.float32
BF16 = jnp.bfloat16
X = 4


def nn(a, b):
    return lax.dot_general(a, b, (((1,), (0,)), ((), ())), preferred_element_type=F32)


def nt(a, b):
    return lax.dot_general(a, b, (((1,), (1,)), ((), ())), preferred_element_type=F32)


def tn(a, b):
    return lax.dot_general(a, b, (((0,), (0,)), ((), ())), preferred_element_type=F32)


def identity(size):
    row = lax.broadcasted_iota(jnp.int32, (size, size), 0)
    column = lax.broadcasted_iota(jnp.int32, (size, size), 1)
    return jnp.where(row == column, 1.0, 0.0).astype(BF16)


def as_row(column):
    return jnp.broadcast_to(column, (column.shape[0], 128)).T[0:1, :]


def as_columns(row):
    return jnp.broadcast_to(row, (128, row.shape[1])).T


def kernel(
    sizes,
    q_in,
    k_in,
    v_in,
    ld_in,
    gate_in,
    gain_in,
    w_ref,
    target_in,
    out_to,
    qg_to,
    kg_to,
    vg_to,
    gg_to,
    out_ref,
    qg_ref,
    kg_ref,
    vg_ref,
    gg_ref,
    out_sems,
    q_ref,
    k_ref,
    v_ref,
    ld_ref,
    gate_ref,
    gain_ref,
    target_ref,
    in_sems,
    wb,
    wrelay,
    uall,
    yacc,
    ystage,
    yrecv,
    gx,
    gall,
    fstage,
    frecv,
    weight,
    probs,
    kdec,
    att,
    klocal,
    vlocal,
    agrad,
    bown,
    bsib,
    bchip,
    s_out,
    s_in,
    s_keep,
    t_out,
    t_in,
    c_acc,
    d_acc,
    c_out,
    state,
    small_z,
    small_x,
    w_send,
    w_recv,
    w_own,
    ws_send,
    ws_recv,
    u_send,
    u_recv,
    y_send,
    y_recv,
    g_send,
    g_recv,
    f_send,
    f_recv,
    b_send,
    b_recv,
    bc_send,
    bc_recv,
    s_send,
    s_recv,
    t_send,
    t_recv,
    c_send,
    c_recv,
    sz_send,
    sz_recv,
    sx_send,
    sx_recv,
):
    Y, Z = sizes
    tokens = q_ref.shape[0]
    half_tokens = tokens // 2
    rows = w_ref.shape[0]
    half = rows // 2
    width = q_ref.shape[1]
    total_features = w_ref.shape[1]
    heads = width // DH

    ctx = lax.axis_index("ctx")
    tp = lax.axis_index("tp")
    core = lax.rem(ctx, 2)
    y = lax.div(ctx, 2)
    x = lax.rem(tp, X)
    z = lax.div(tp, X)
    sibling = (y * 2 + 1 - core, tp)
    is_zero = core == 0

    def xs(step):
        return lax.rem(x + step + X, X)

    def zs(step):
        return lax.rem(z + step + 2 * Z, Z)

    def at_x(step):
        return (ctx, z * X + xs(step))

    def at_z(step):
        return (ctx, zs(step) * X + x)

    def at_y(place):
        return (place * 2 + core, tp)

    sign = 1 - 2 * core
    left, right, opp = xs(-1), xs(1), xs(2)

    def send(src, dst, send_sem, recv_sem, device):
        copy = pltpu.make_async_remote_copy(
            src_ref=src,
            dst_ref=dst,
            send_sem=send_sem,
            recv_sem=recv_sem,
            device_id=device,
            device_id_type=MESH,
        )
        copy.start()

    def arrived(ref, sem):
        pltpu.make_async_copy(ref, ref, sem).wait()

    loads = [
        pltpu.make_async_copy(src, dst, in_sems.at[index])
        for index, (src, dst) in enumerate(
            (
                (ld_in, ld_ref),
                (k_in, k_ref),
                (v_in, v_ref),
                (q_in, q_ref),
                (gate_in, gate_ref),
                (gain_in, gain_ref),
                (target_in, target_ref),
            )
        )
    ]
    for load in loads:
        load.start()
    barrier = pltpu.get_barrier_semaphore()
    partners = [sibling] + [at_x(step) for step in range(1, X)]
    partners += [at_z(step) for step in range(1, Z)]
    partners += [at_y(lax.rem(y + step, Y)) for step in range(1, Y)]
    for partner in partners:
        pl.semaphore_signal(barrier, inc=1, device_id=partner, device_id_type=MESH)

    def w_columns(block, x_to):
        start = pl.multiple_of((block * X + x_to) * width, width)
        return pl.ds(start, width)

    my_rows = pl.ds(pl.multiple_of(core * half, half), half)
    x_far = xs(sign)

    def w_far(block, carry):
        send(w_ref.at[my_rows, w_columns(block, opp)], wrelay.at[block], w_send.at[0], w_recv.at[0], (ctx, z * X + x_far))
        return carry

    def w_near(block, carry):
        send(w_ref.at[my_rows, w_columns(block, right)], wb.at[block, x, core], w_send.at[1], w_recv.at[1], at_x(1))
        send(w_ref.at[my_rows, w_columns(block, left)], wb.at[block, x, core], w_send.at[2], w_recv.at[2], at_x(-1))
        return carry

    def w_mine(block, carry):
        for part in range(2):
            pltpu.make_async_copy(
                w_ref.at[pl.ds(part * half, half), w_columns(block, x)], wb.at[block, x, part], w_own
            ).start()
        return carry

    pl.semaphore_wait(barrier, len(partners))
    lax.fori_loop(0, Z, w_far, 0)
    lax.fori_loop(0, Z, w_near, 0)

    row = lax.broadcasted_iota(jnp.int32, (tokens, tokens), 0)
    column = lax.broadcasted_iota(jnp.int32, (tokens, tokens), 1)
    causal = row >= column
    loads[0].wait()
    cum = lax.dot_general(
        ld_ref[...],
        jnp.where(row <= column, 1.0, 0.0).astype(F32),
        (((1,), (0,)), ((), ())),
        precision=lax.Precision.HIGHEST,
        preferred_element_type=F32,
    )
    cum_rows = [cum[h : h + 1, :] for h in range(heads)]
    cums = [as_columns(c) for c in cum_rows]
    totals = [c[tokens - 1 : tokens, :] for c in cums]
    bown[...] = jnp.zeros_like(bown)
    for h in range(heads):
        bown[h : h + 1, :] = totals[h]
    send(bown, bsib, b_send, b_recv, sibling)
    loads[1].wait()
    loads[2].wait()

    def lanes(h):
        return slice(h * DH, (h + 1) * DH)

    own = []
    for h in range(heads):
        decayed = (k_ref[:, lanes(h)].astype(F32) * jnp.exp(totals[h] - cums[h])).astype(BF16)
        kdec[:, lanes(h)] = decayed
        own.append(tn(decayed, v_ref[:, lanes(h)]))

    def of_core(pair):
        return jnp.where(is_zero, pair[0], pair[1])

    def scan_give(turn, h, value):
        @pl.when(core == h)
        def _():
            s_keep[turn] = value

        @pl.when(core != h)
        def _():
            s_out[turn] = value.astype(BF16)
            send(s_out.at[turn], s_in.at[turn], s_send.at[turn], s_recv.at[turn], sibling)

    def scan_way(turn):
        step = 1 if turn == 0 else -1
        first_here = is_zero if turn == 0 else jnp.logical_not(is_zero)
        return step, first_here

    def decays(ref):
        return of_core((ref[0:1, :], ref[1:2, :]))

    def reaches(place):
        return jnp.logical_and(place >= 0, place < Y)

    def scan_send(turn):
        step, first_here = scan_way(turn)
        arrived(s_in.at[turn], s_recv.at[turn])
        mine = s_keep[turn]
        theirs = s_in[turn].astype(F32)
        first = jnp.where(first_here, mine, theirs)
        second = jnp.where(first_here, theirs, mine)
        s_keep[turn] = first
        b_second = jnp.where(first_here, decays(bsib), decays(bown))
        t_out[turn] = (jnp.exp(b_second) * first + second).astype(BF16)
        for distance in range(1, Y):
            place = y + step * distance

            @pl.when(reaches(place))
            def _():
                send(
                    t_out.at[turn],
                    t_in.at[turn, distance - 1],
                    t_send.at[turn, distance - 1],
                    t_recv.at[turn, distance - 1],
                    at_y(place),
                )

    def scan_end(turn):
        step, first_here = scan_way(turn)
        c_acc[...] = jnp.zeros_like(c_acc)
        d_acc[...] = jnp.zeros_like(d_acc)
        for distance in range(1, Y):
            place = y - step * distance

            @pl.when(reaches(place))
            def _():
                slot = t_in.at[turn, distance - 1]
                arrived(slot, t_recv.at[turn, distance - 1])
                between = d_acc[0:1, :]
                c_acc[...] += jnp.exp(between) * slot[...].astype(F32)
                d_acc[0:1, :] = between + decays(bchip.at[place])

        b_first = jnp.where(first_here, decays(bown), decays(bsib))
        carried = c_acc[...]
        after = jnp.exp(b_first) * carried + s_keep[turn]
        state[turn, core] = jnp.where(first_here, carried, after).astype(BF16)
        c_out[turn] = jnp.where(first_here, after, carried).astype(BF16)
        send(c_out.at[turn], state.at[turn, core], c_send.at[turn], c_recv.at[turn], sibling)
        arrived(c_out.at[turn], c_recv.at[turn])

    for h in range(heads):
        scan_give(0, h, own[h])
    lax.fori_loop(0, Z, w_mine, 0)

    arrived(bsib, b_recv)
    bchip[y] = bown[...] + bsib[...]
    for distance in range(1, Y):
        place = lax.rem(y + distance, Y)
        send(bchip.at[y], bchip.at[y], bc_send.at[distance - 1], bc_recv.at[distance - 1], at_y(place))
    scan_send(0)

    for load in loads[3:]:
        load.wait()
    for h in range(heads):
        gaps = cums[h][:, 0:1] - cum_rows[h]
        decay = jnp.where(causal, jnp.exp(jnp.minimum(gaps, 0.0)), 0.0)
        weight[h] = decay
        probs[h] = (nt(q_ref[:, lanes(h)], k_ref[:, lanes(h)]) * decay).astype(BF16)
        att[:, lanes(h)] = nn(probs[h], v_ref[:, lanes(h)])

    for distance in range(1, Y):
        arrived(bchip.at[lax.rem(y - distance + Y, Y)], bc_recv.at[distance - 1])

    arrived(wrelay, w_recv.at[0])
    send(wrelay, wb.at[:, xs(-sign), core], w_send.at[3], w_recv.at[3], (ctx, z * X + x_far))

    scan_end(0)

    gain = gain_ref[...]
    squares = jnp.zeros((tokens, 1), F32)
    for h in range(heads):
        from_state = nn(q_ref[:, lanes(h)], state[0, h]) * jnp.exp(cums[h])
        attended = att[:, lanes(h)] + from_state
        att[:, lanes(h)] = attended
        squares = squares + jnp.sum(attended * attended, axis=1, keepdims=True)
        gate_open = jax.nn.sigmoid(gate_ref[:, lanes(h)].astype(F32))
        gated = (attended * gain[:, lanes(h)] * gate_open).astype(BF16)
        for part in range(2):
            uall[z, part, :, lanes(h)] = gated[part * half_tokens : (part + 1) * half_tokens, :]

    far, near = Z // 2, Z - 1 - Z // 2
    hops = (far, near)
    ways = (sign, -sign)

    def u_part(way, step, part):
        return uall.at[zs(-ways[way] * step), part]

    def u_start(way, step, part):
        ref = u_part(way, step, part)
        send(ref, ref, u_send.at[way, step, part], u_recv.at[way, step, part], at_z(ways[way]))

    for part in range(2):
        for way in range(2):
            if hops[way] > 0:
                u_start(way, 0, part)

    def small_share(turn, value):
        small_z[turn, 0] = value
        for step in range(1, Z):
            send(small_z.at[turn, 0], small_z.at[turn, step], sz_send.at[turn, step - 1], sz_recv.at[turn, step - 1], at_z(step))

    def small_cross(turn):
        for step in range(1, Z):
            arrived(small_z.at[turn, step], sz_recv.at[turn, step - 1])
        sum_z = small_z[turn, 0]
        for step in range(1, Z):
            sum_z = sum_z + small_z[turn, step]
        small_x[turn, 0] = sum_z
        for step in range(1, X):
            send(small_x.at[turn, 0], small_x.at[turn, step], sx_send.at[turn, step - 1], sx_recv.at[turn, step - 1], at_x(step))

    def small_sum(turn):
        for step in range(1, X):
            arrived(small_x.at[turn, step], sx_recv.at[turn, step - 1])
        sum_x = small_x[turn, 0]
        for step in range(1, X):
            sum_x = sum_x + small_x[turn, step]
        return sum_x

    small_share(0, as_row(squares))

    def w_pair(source, sem, slot):
        ref = wb.at[:, source, core]
        arrived(ref, sem)
        send(ref, ref, ws_send.at[slot], ws_recv.at[slot], sibling)

    w_pair(left, w_recv.at[1], 0)
    w_pair(right, w_recv.at[2], 1)

    def w_block(block):
        return wb[block].reshape(X * rows, width)

    def accumulate(block, part):
        yacc[part] += nt(w_block(block), uall[block, part]).reshape(yacc.shape[1:])

    def u_pass(step, part):
        for way in range(2):
            if step < hops[way]:
                arrived(u_part(way, step + 1, part), u_recv.at[way, step, part])
                if step + 1 < hops[way]:
                    u_start(way, step + 1, part)

    for step in range(far - 1):
        for part in range(2):
            u_pass(step, part)
    small_cross(0)
    w_pair(opp, w_recv.at[3], 2)
    for part in range(2):
        arrived(wb.at[:, x, part], w_own)
    for slot, source in enumerate((left, right, opp)):
        arrived(wb.at[:, source, 1 - core], ws_recv.at[slot])
    for part in range(2):
        yacc[part] = nt(w_block(z), uall[z, part]).reshape(yacc.shape[1:])
        for step in range(far - 1):
            for way in range(2):
                if step < hops[way]:
                    accumulate(zs(-ways[way] * (step + 1)), part)

    def y_start(part, kind, piece, value, device):
        ystage[part, kind, piece] = value.astype(BF16)
        send(
            ystage.at[part, kind, piece],
            yrecv.at[part, kind, piece],
            y_send.at[part, kind, piece],
            y_recv.at[part, kind, piece],
            device,
        )

    def y_arrived(part, kind, piece):
        arrived(yrecv.at[part, kind, piece], y_recv.at[part, kind, piece])
        return yrecv[part, kind, piece].astype(F32)

    for part in range(2):
        u_pass(far - 1, part)
        for way in range(2):
            if far == hops[way]:
                accumulate(zs(-ways[way] * far), part)
        y_start(part, 0, 0, yacc[part, opp, 0], at_x(1))
        y_start(part, 0, 1, yacc[part, opp, 1], at_x(-1))
        y_start(part, 1, 1, yacc[part, right, 1], at_x(1))
        y_start(part, 1, 0, yacc[part, left, 0], at_x(-1))
    for part in range(2):
        y_start(part, 2, 0, yacc[part, right, 0] + y_arrived(part, 0, 0), at_x(1))
        y_start(part, 2, 1, yacc[part, left, 1] + y_arrived(part, 0, 1), at_x(-1))

    inv_rms = lax.rsqrt(small_sum(0) / total_features + EPS)

    def g_start(part, source, piece, kind, device):
        ref = gx.at[part, source, piece]
        send(ref, ref, g_send.at[part, kind, piece], g_recv.at[part, kind, piece], device)

    def g_arrived(part, source, piece, kind):
        arrived(gx.at[part, source, piece], g_recv.at[part, kind, piece])

    products = []
    for part in range(2):
        span = slice(part * half_tokens, (part + 1) * half_tokens)
        product = jnp.zeros((1, half_tokens), F32)
        for piece in range(2):
            total = yacc[part, x, piece] + y_arrived(part, 1, piece) + y_arrived(part, 2, piece)
            rounded = (total * inv_rms[:, span]).astype(BF16)
            out_ref[piece * half : (piece + 1) * half, span] = rounded
            wanted = target_ref[piece * half : (piece + 1) * half, span].astype(F32)
            grad = (rounded.astype(F32) - wanted).astype(BF16)
            gx[part, x, piece] = grad
            g_start(part, x, piece, piece, at_x(1 - 2 * piece))
            product = product + jnp.sum(grad.astype(F32) * total, axis=0, keepdims=True)
        g_start(part, x, 1, 0, at_x(1))
        g_start(part, x, 0, 1, at_x(-1))
        products.append(product)
    small_share(1, jnp.concatenate(products, axis=1))
    stores = [
        pltpu.make_async_copy(src, dst, out_sems.at[index])
        for index, (src, dst) in enumerate(
            ((out_ref, out_to), (qg_ref, qg_to), (kg_ref, kg_to), (vg_ref, vg_to), (gg_ref, gg_to))
        )
    ]
    stores[0].start()
    for part in range(2):
        g_arrived(part, left, 0, 0)
        g_start(part, left, 0, 2, at_x(1))
        g_arrived(part, right, 1, 1)
        g_start(part, right, 1, 2, at_x(-1))

    eye = identity(half_tokens)

    def feature_part(block, part):
        return nn(gall[part], w_block(block))

    def f_slot(way, step):
        return way * far + step

    def f_start(way, step, part, h, value):
        slot = f_slot(way, step)
        fstage[slot, part, h] = value.astype(BF16)
        send(
            fstage.at[slot, part, h],
            frecv.at[slot, part, h],
            f_send.at[slot, part, h],
            f_recv.at[slot, part, h],
            at_z(ways[way]),
        )

    def f_arrived(way, step, part, h):
        slot = f_slot(way, step)
        arrived(frecv.at[slot, part, h], f_recv.at[slot, part, h])
        return frecv[slot, part, h].astype(F32)

    for step in range(far):
        for part in range(2):
            if step == 0:
                g_arrived(part, left, 1, 0)
                g_arrived(part, right, 0, 1)
                for piece in range(2):
                    g_arrived(part, opp, piece, 2)
                gall[part] = nt(eye, gx[part].reshape(X * rows, half_tokens)).astype(BF16)
            sums = [
                feature_part(zs(ways[way] * (hops[way] - step)), part) if step < hops[way] else None
                for way in range(2)
            ]
            for h in range(heads):
                for way in range(2):
                    if step < hops[way]:
                        value = sums[way][:, lanes(h)]
                        if step > 0:
                            value = value + f_arrived(way, step - 1, part, h)
                        f_start(way, step, part, h, value)
        if step == 0:
            small_cross(1)

    own_feature = [feature_part(z, part) for part in range(2)]
    mean_product = as_columns(small_sum(1) / total_features)
    inv = as_columns(inv_rms)

    for h in range(heads):
        pieces = []
        for part in range(2):
            value = own_feature[part][:, lanes(h)]
            for way in range(2):
                if hops[way] > 0:
                    value = value + f_arrived(way, hops[way] - 1, part, h)
            pieces.append(value)
        attended = att[:, lanes(h)]
        gate_open = jax.nn.sigmoid(gate_ref[:, lanes(h)].astype(F32))
        normed_grad = jnp.concatenate(pieces, axis=0) * gain[:, lanes(h)] * gate_open
        grad = (inv * normed_grad - inv * inv * inv * attended * mean_product).astype(BF16)
        agrad[:, lanes(h)] = grad
        decayed = (q_ref[:, lanes(h)].astype(F32) * jnp.exp(cums[h])).astype(BF16)
        scan_give(1, h, tn(decayed, grad))
        gg_ref[:, lanes(h)] = (normed_grad * attended * inv * (1.0 - gate_open)).astype(BF16)
    stores[4].start()

    for h in range(heads):
        grad = agrad[:, lanes(h)]
        score_grad = (nt(grad, v_ref[:, lanes(h)]) * weight[h]).astype(BF16)
        if h == 0:
            scan_send(1)
        qg_ref[:, lanes(h)] = (
            nn(score_grad, k_ref[:, lanes(h)]) + jnp.exp(cums[h]) * nt(grad, state[0, h])
        ).astype(BF16)
        klocal[:, lanes(h)] = tn(score_grad, q_ref[:, lanes(h)])
        vlocal[:, lanes(h)] = tn(probs[h], grad)
    stores[1].start()
    scan_end(1)
    for h in range(heads):
        later = state[1, h]
        kg_ref[:, lanes(h)] = (
            klocal[:, lanes(h)] + jnp.exp(totals[h] - cums[h]) * nt(v_ref[:, lanes(h)], later)
        ).astype(BF16)
        vg_ref[:, lanes(h)] = (vlocal[:, lanes(h)] + nn(kdec[:, lanes(h)], later)).astype(BF16)

    stores[2].start()
    stores[3].start()

    for index in range(4):
        arrived(wrelay, w_send.at[index])
    for index in range(3):
        arrived(wrelay, ws_send.at[index])
    for way in range(2):
        for step in range(hops[way]):
            for part in range(2):
                arrived(u_part(way, step, part), u_send.at[way, step, part])
                slot = f_slot(way, step)
                for h in range(heads):
                    arrived(fstage.at[slot, part, h], f_send.at[slot, part, h])
    for part in range(2):
        for kind in range(3):
            for piece in range(2):
                arrived(ystage.at[part, kind, piece], y_send.at[part, kind, piece])
                arrived(ystage.at[part, kind, piece], g_send.at[part, kind, piece])
    arrived(bown, b_send)
    for distance in range(1, Y):
        arrived(bown, bc_send.at[distance - 1])
    for turn in range(2):
        arrived(s_out.at[turn], s_send.at[turn])
        arrived(c_out.at[turn], c_send.at[turn])
        step, _ = scan_way(turn)
        for distance in range(1, Y):

            @pl.when(reaches(y + step * distance))
            def _():
                arrived(t_out.at[turn], t_send.at[turn, distance - 1])

        for distance in range(1, Z):
            arrived(small_z.at[turn, 0], sz_send.at[turn, distance - 1])
        for distance in range(1, X):
            arrived(small_x.at[turn, 0], sx_send.at[turn, distance - 1])
    for copy in stores:
        copy.wait()


def store(*refs):
    count = len(refs) // 2
    for src, dst in zip(refs[:count], refs[count:]):
        dst[...] = src[...]


def on_device(chips, queries, keys, values, log_decay, gate, norm_gain, out_weight, target):
    Y, Z = chips
    tokens, width = queries.shape
    rows, features = out_weight.shape
    half = rows // 2
    far = Z // 2
    vmem = pltpu.VMEM
    dma = pltpu.SemaphoreType.DMA
    scratch = [
        vmem((rows, tokens), BF16),
        vmem((tokens, width), BF16),
        vmem((tokens, width), BF16),
        vmem((tokens, width), BF16),
        vmem((tokens, width), BF16),
        dma((5,)),
        vmem((tokens, width), BF16),
        vmem((tokens, width), BF16),
        vmem((tokens, width), BF16),
        vmem((width // DH, tokens), F32),
        vmem((tokens, width), BF16),
        vmem((1, width), F32),
        vmem((rows, tokens), BF16),
        dma((7,)),
        vmem((Z, X, 2, half, width), BF16),
        vmem((Z, half, width), BF16),
        vmem((Z, 2, tokens // 2, width), BF16),
        vmem((2, X, 2, half, tokens // 2), F32),
        vmem((2, 3, 2, half, tokens // 2), BF16),
        vmem((2, 3, 2, half, tokens // 2), BF16),
        vmem((2, X, 2, half, tokens // 2), BF16),
        vmem((2, tokens // 2, X * rows), BF16),
        vmem((Z - 1, 2, 2, tokens // 2, DH), BF16),
        vmem((Z - 1, 2, 2, tokens // 2, DH), BF16),
        vmem((width // DH, tokens, tokens), F32),
        vmem((width // DH, tokens, tokens), BF16),
        vmem((tokens, width), BF16),
        vmem((tokens, width), F32),
        vmem((tokens, width), F32),
        vmem((tokens, width), F32),
        vmem((tokens, width), BF16),
        vmem((8, 128), F32),
        vmem((8, 128), F32),
        vmem((Y, 8, 128), F32),
        vmem((2, DH, DH), BF16),
        vmem((2, DH, DH), BF16),
        vmem((2, DH, DH), F32),
        vmem((2, DH, DH), BF16),
        vmem((2, max(Y - 1, 1), DH, DH), BF16),
        vmem((DH, DH), F32),
        vmem((8, 128), F32),
        vmem((2, DH, DH), BF16),
        vmem((2, 2, DH, DH), BF16),
        vmem((2, Z, 1, tokens), F32),
        vmem((2, X, 1, tokens), F32),
        dma((4,)),
        dma((4,)),
        dma,
        dma((3,)),
        dma((3,)),
        dma((2, far, 2)),
        dma((2, far, 2)),
        dma((2, 3, 2)),
        dma((2, 3, 2)),
        dma((2, 3, 2)),
        dma((2, 3, 2)),
        dma((Z - 1, 2, 2)),
        dma((Z - 1, 2, 2)),
        dma,
        dma,
        dma((max(Y - 1, 1),)),
        dma((max(Y - 1, 1),)),
        dma((2,)),
        dma((2,)),
        dma((2, max(Y - 1, 1))),
        dma((2, max(Y - 1, 1))),
        dma((2,)),
        dma((2,)),
        dma((2, Z - 1)),
        dma((2, Z - 1)),
        dma((2, X - 1)),
        dma((2, X - 1)),
    ]
    in_vmem = pl.BlockSpec(memory_space=pltpu.VMEM)
    in_hbm = pl.BlockSpec(memory_space=pltpu.HBM)
    wide = jax.ShapeDtypeStruct((tokens, width), BF16)
    out_shape = (jax.ShapeDtypeStruct((rows, tokens), BF16), wide, wide, wide, wide)
    results = pl.pallas_call(
        functools.partial(kernel, chips),
        out_shape=out_shape,
        in_specs=[in_hbm] * 8,
        out_specs=(in_hbm,) * 5,
        scratch_shapes=scratch,
        compiler_params=pltpu.CompilerParams(
            collective_id=0, has_side_effects=True, vmem_limit_bytes=63 * 1024 * 1024
        ),
        cost_estimate=pl.CostEstimate(flops=2 * 10**9, bytes_accessed=8 * 10**6, transcendentals=10**6),
        name="attention_layer",
    )(queries, keys, values, log_decay.T, gate, norm_gain.reshape(1, width), out_weight, target.T)
    output, *grads = pl.pallas_call(
        store,
        out_shape=out_shape,
        in_specs=[in_vmem] * 5,
        out_specs=(in_vmem,) * 5,
        compiler_params=pltpu.CompilerParams(vmem_limit_bytes=63 * 1024 * 1024),
        name="store",
    )(*results)
    return (output.T, *grads)


def solution(mesh):
    chips = (mesh.shape["ctx"] // 2, mesh.shape["tp"] // X)
    return jax.shard_map(
        functools.partial(on_device, chips),
        mesh=mesh,
        in_specs=(
            P("ctx", "tp"),
            P("ctx", "tp"),
            P("ctx", "tp"),
            P("ctx", "tp"),
            P("ctx", "tp"),
            P("tp"),
            P("tp", None),
            P("ctx", "tp"),
        ),
        out_specs=(P("ctx", "tp"),) * 5,
        check_vma=False,
    )
```

```python
import functools

import jax
import jax.numpy as jnp
from jax import lax
from jax.experimental import pallas as pl
from jax.experimental.pallas import tpu as pltpu
from jax.sharding import PartitionSpec as P

DH = 128
EPS = 1e-06
MESH = pl.DeviceIdType.MESH
F32 = jnp.float32
BF16 = jnp.bfloat16
X = 4


def nn(a, b):
    return lax.dot_general(a, b, (((1,), (0,)), ((), ())), preferred_element_type=F32)


def nt(a, b):
    return lax.dot_general(a, b, (((1,), (1,)), ((), ())), preferred_element_type=F32)


def tn(a, b):
    return lax.dot_general(a, b, (((0,), (0,)), ((), ())), preferred_element_type=F32)


def identity(size):
    row = lax.broadcasted_iota(jnp.int32, (size, size), 0)
    column = lax.broadcasted_iota(jnp.int32, (size, size), 1)
    return jnp.where(row == column, 1.0, 0.0).astype(BF16)


def as_row(column):
    return jnp.broadcast_to(column, (column.shape[0], 128)).T[0:1, :]


def as_columns(row):
    return jnp.broadcast_to(row, (128, row.shape[1])).T


def kernel(
    sizes,
    q_in,
    k_in,
    v_in,
    ld_in,
    gate_in,
    gain_in,
    w_ref,
    target_in,
    out_to,
    qg_to,
    kg_to,
    vg_to,
    gg_to,
    out_ref,
    qg_ref,
    kg_ref,
    vg_ref,
    gg_ref,
    out_sems,
    q_ref,
    k_ref,
    v_ref,
    ld_ref,
    gate_ref,
    gain_ref,
    target_ref,
    in_sems,
    wb,
    wrelay,
    uall,
    yacc,
    ystage,
    yrecv,
    gx,
    gall,
    fstage,
    frecv,
    weight,
    probs,
    kdec,
    att,
    klocal,
    vlocal,
    agrad,
    bown,
    bsib,
    bchip,
    s_out,
    s_in,
    s_keep,
    t_out,
    t_in,
    c_acc,
    d_acc,
    c_out,
    state,
    small_z,
    small_x,
    w_send,
    w_recv,
    w_own,
    ws_send,
    ws_recv,
    wy_send,
    wy_recv,
    u_send,
    u_recv,
    y_send,
    y_recv,
    g_send,
    g_recv,
    f_send,
    f_recv,
    b_send,
    b_recv,
    bc_send,
    bc_recv,
    s_send,
    s_recv,
    t_send,
    t_recv,
    c_send,
    c_recv,
    sz_send,
    sz_recv,
    sx_send,
    sx_recv,
):
    Y, Z = sizes
    tokens = q_ref.shape[0]
    half_tokens = tokens // 2
    rows = w_ref.shape[0]
    half = rows // 2
    width = q_ref.shape[1]
    total_features = w_ref.shape[1]
    heads = width // DH

    ctx = lax.axis_index("ctx")
    tp = lax.axis_index("tp")
    core = lax.rem(ctx, 2)
    y = lax.div(ctx, 2)
    x = lax.rem(tp, X)
    z = lax.div(tp, X)
    sibling = (y * 2 + 1 - core, tp)
    is_zero = core == 0

    def xs(step):
        return lax.rem(x + step + X, X)

    def zs(step):
        return lax.rem(z + step + 2 * Z, Z)

    def at_x(step):
        return (ctx, z * X + xs(step))

    def at_z(step):
        return (ctx, zs(step) * X + x)

    def at_y(place):
        return (place * 2 + core, tp)

    sign = 1 - 2 * core
    left, right, opp = xs(-1), xs(1), xs(2)

    def send(src, dst, send_sem, recv_sem, device):
        copy = pltpu.make_async_remote_copy(
            src_ref=src,
            dst_ref=dst,
            send_sem=send_sem,
            recv_sem=recv_sem,
            device_id=device,
            device_id_type=MESH,
        )
        copy.start()

    def arrived(ref, sem):
        pltpu.make_async_copy(ref, ref, sem).wait()

    loads = [
        pltpu.make_async_copy(src, dst, in_sems.at[index])
        for index, (src, dst) in enumerate(
            (
                (ld_in, ld_ref),
                (k_in, k_ref),
                (v_in, v_ref),
                (q_in, q_ref),
                (gate_in, gate_ref),
                (gain_in, gain_ref),
                (target_in, target_ref),
            )
        )
    ]
    for load in loads:
        load.start()
    barrier = pltpu.get_barrier_semaphore()
    partners = [sibling] + [at_x(step) for step in range(1, X)]
    partners += [at_z(step) for step in range(1, Z)]
    partners += [at_y(lax.rem(y + step, Y)) for step in range(1, Y)]
    for partner in partners:
        pl.semaphore_signal(barrier, inc=1, device_id=partner, device_id_type=MESH)

    def w_columns(block, x_to):
        start = pl.multiple_of((block * X + x_to) * width, width)
        return pl.ds(start, width)

    my_rows = pl.ds(pl.multiple_of(core * half, half), half)
    x_far = xs(sign)

    odd = lax.rem(y, 2)

    def w_far(place, carry):
        columns = w_columns(2 * place + odd, opp)
        send(w_ref.at[my_rows, columns], wrelay.at[place], w_send.at[0], w_recv.at[0], (ctx, z * X + x_far))
        return carry

    def w_near(place, carry):
        block = 2 * place + odd
        slot = wb.at[odd, place, x, core]
        send(w_ref.at[my_rows, w_columns(block, right)], slot, w_send.at[1], w_recv.at[1], at_x(1))
        send(w_ref.at[my_rows, w_columns(block, left)], slot, w_send.at[2], w_recv.at[2], at_x(-1))
        return carry

    def w_mine(place, carry):
        for other in range(2):
            for part in range(2):
                pltpu.make_async_copy(
                    w_ref.at[pl.ds(part * half, half), w_columns(2 * place + other, x)],
                    wb.at[other, place, x, part],
                    w_own,
                ).start()
        return carry

    pl.semaphore_wait(barrier, len(partners))
    lax.fori_loop(0, Z // 2, w_far, 0)
    lax.fori_loop(0, Z // 2, w_near, 0)

    row = lax.broadcasted_iota(jnp.int32, (tokens, tokens), 0)
    column = lax.broadcasted_iota(jnp.int32, (tokens, tokens), 1)
    causal = row >= column
    loads[0].wait()
    cum = lax.dot_general(
        ld_ref[...],
        jnp.where(row <= column, 1.0, 0.0).astype(F32),
        (((1,), (0,)), ((), ())),
        precision=lax.Precision.HIGHEST,
        preferred_element_type=F32,
    )
    cum_rows = [cum[h : h + 1, :] for h in range(heads)]
    cums = [as_columns(c) for c in cum_rows]
    totals = [c[tokens - 1 : tokens, :] for c in cums]
    bown[...] = jnp.zeros_like(bown)
    for h in range(heads):
        bown[h : h + 1, :] = totals[h]
    send(bown, bsib, b_send, b_recv, sibling)
    loads[1].wait()
    loads[2].wait()

    def lanes(h):
        return slice(h * DH, (h + 1) * DH)

    own = []
    for h in range(heads):
        decayed = (k_ref[:, lanes(h)].astype(F32) * jnp.exp(totals[h] - cums[h])).astype(BF16)
        kdec[:, lanes(h)] = decayed
        own.append(tn(decayed, v_ref[:, lanes(h)]))

    def of_core(pair):
        return jnp.where(is_zero, pair[0], pair[1])

    def scan_give(turn, h, value):
        @pl.when(core == h)
        def _():
            s_keep[turn] = value

        @pl.when(core != h)
        def _():
            s_out[turn] = value.astype(BF16)
            send(s_out.at[turn], s_in.at[turn], s_send.at[turn], s_recv.at[turn], sibling)

    def scan_way(turn):
        step = 1 if turn == 0 else -1
        first_here = is_zero if turn == 0 else jnp.logical_not(is_zero)
        return step, first_here

    def decays(ref):
        return of_core((ref[0:1, :], ref[1:2, :]))

    def reaches(place):
        return jnp.logical_and(place >= 0, place < Y)

    def scan_send(turn):
        step, first_here = scan_way(turn)
        arrived(s_in.at[turn], s_recv.at[turn])
        mine = s_keep[turn]
        theirs = s_in[turn].astype(F32)
        first = jnp.where(first_here, mine, theirs)
        second = jnp.where(first_here, theirs, mine)
        s_keep[turn] = first
        b_second = jnp.where(first_here, decays(bsib), decays(bown))
        t_out[turn] = (jnp.exp(b_second) * first + second).astype(BF16)
        for distance in range(1, Y):
            place = y + step * distance

            @pl.when(reaches(place))
            def _():
                send(
                    t_out.at[turn],
                    t_in.at[turn, distance - 1],
                    t_send.at[turn, distance - 1],
                    t_recv.at[turn, distance - 1],
                    at_y(place),
                )

    def scan_end(turn):
        step, first_here = scan_way(turn)
        c_acc[...] = jnp.zeros_like(c_acc)
        d_acc[...] = jnp.zeros_like(d_acc)
        for distance in range(1, Y):
            place = y - step * distance

            @pl.when(reaches(place))
            def _():
                slot = t_in.at[turn, distance - 1]
                arrived(slot, t_recv.at[turn, distance - 1])
                between = d_acc[0:1, :]
                c_acc[...] += jnp.exp(between) * slot[...].astype(F32)
                d_acc[0:1, :] = between + decays(bchip.at[place])

        b_first = jnp.where(first_here, decays(bown), decays(bsib))
        carried = c_acc[...]
        after = jnp.exp(b_first) * carried + s_keep[turn]
        state[turn, core] = jnp.where(first_here, carried, after).astype(BF16)
        c_out[turn] = jnp.where(first_here, after, carried).astype(BF16)
        send(c_out.at[turn], state.at[turn, core], c_send.at[turn], c_recv.at[turn], sibling)
        arrived(c_out.at[turn], c_recv.at[turn])

    for h in range(heads):
        scan_give(0, h, own[h])
    lax.fori_loop(0, Z // 2, w_mine, 0)

    arrived(bsib, b_recv)
    bchip[y] = bown[...] + bsib[...]
    for distance in range(1, Y):
        place = lax.rem(y + distance, Y)
        send(bchip.at[y], bchip.at[y], bc_send.at[distance - 1], bc_recv.at[distance - 1], at_y(place))
    scan_send(0)

    for load in loads[3:]:
        load.wait()
    for h in range(heads):
        gaps = cums[h][:, 0:1] - cum_rows[h]
        decay = jnp.where(causal, jnp.exp(jnp.minimum(gaps, 0.0)), 0.0)
        weight[h] = decay
        probs[h] = (nt(q_ref[:, lanes(h)], k_ref[:, lanes(h)]) * decay).astype(BF16)
        att[:, lanes(h)] = nn(probs[h], v_ref[:, lanes(h)])

    for distance in range(1, Y):
        arrived(bchip.at[lax.rem(y - distance + Y, Y)], bc_recv.at[distance - 1])

    arrived(wrelay, w_recv.at[0])
    send(wrelay, wb.at[odd, :, xs(-sign), core], w_send.at[3], w_recv.at[3], (ctx, z * X + x_far))

    scan_end(0)

    gain = gain_ref[...]
    squares = jnp.zeros((tokens, 1), F32)
    for h in range(heads):
        from_state = nn(q_ref[:, lanes(h)], state[0, h]) * jnp.exp(cums[h])
        attended = att[:, lanes(h)] + from_state
        att[:, lanes(h)] = attended
        squares = squares + jnp.sum(attended * attended, axis=1, keepdims=True)
        gate_open = jax.nn.sigmoid(gate_ref[:, lanes(h)].astype(F32))
        gated = (attended * gain[:, lanes(h)] * gate_open).astype(BF16)
        for part in range(2):
            uall[z, part, :, lanes(h)] = gated[part * half_tokens : (part + 1) * half_tokens, :]

    far, near = Z // 2, Z - 1 - Z // 2
    hops = (far, near)
    ways = (sign, -sign)

    def u_part(way, step, part):
        return uall.at[zs(-ways[way] * step), part]

    def u_start(way, step, part):
        ref = u_part(way, step, part)
        send(ref, ref, u_send.at[way, step, part], u_recv.at[way, step, part], at_z(ways[way]))

    for part in range(2):
        for way in range(2):
            if hops[way] > 0:
                u_start(way, 0, part)

    def small_share(turn, value):
        small_z[turn, 0] = value
        for step in range(1, Z):
            send(small_z.at[turn, 0], small_z.at[turn, step], sz_send.at[turn, step - 1], sz_recv.at[turn, step - 1], at_z(step))

    def small_cross(turn):
        for step in range(1, Z):
            arrived(small_z.at[turn, step], sz_recv.at[turn, step - 1])
        sum_z = small_z[turn, 0]
        for step in range(1, Z):
            sum_z = sum_z + small_z[turn, step]
        small_x[turn, 0] = sum_z
        for step in range(1, X):
            send(small_x.at[turn, 0], small_x.at[turn, step], sx_send.at[turn, step - 1], sx_recv.at[turn, step - 1], at_x(step))

    def small_sum(turn):
        for step in range(1, X):
            arrived(small_x.at[turn, step], sx_recv.at[turn, step - 1])
        sum_x = small_x[turn, 0]
        for step in range(1, X):
            sum_x = sum_x + small_x[turn, step]
        return sum_x

    small_share(0, as_row(squares))

    quarter = Z // 4

    def w_span(parity, source, way):
        return wb.at[parity, pl.ds(way * quarter, quarter), source, core]

    def w_pair(parity, source, slot):
        ref = wb.at[parity, :, source, core]
        send(ref, ref, ws_send.at[slot], ws_recv.at[slot], sibling)

    for slot, source in enumerate((left, right, opp)):
        arrived(wb.at[odd, :, source, core], w_recv.at[slot + 1])
        for way in range(2):
            ref = w_span(odd, source, way)
            place = lax.rem(y + 1 - 2 * way + Y, Y)
            send(ref, ref, wy_send.at[slot, way], wy_recv.at[slot, way], at_y(place))
    for slot, source in enumerate((left, right, opp)):
        w_pair(odd, source, slot)

    def w_block(block):
        return wb[lax.rem(block, 2), lax.div(block, 2)].reshape(X * rows, width)

    def accumulate(block, part):
        yacc[part] += nt(w_block(block), uall[block, part]).reshape(yacc.shape[1:])

    def u_pass(step, part):
        for way in range(2):
            if step < hops[way]:
                arrived(u_part(way, step + 1, part), u_recv.at[way, step, part])
                if step + 1 < hops[way]:
                    u_start(way, step + 1, part)

    for step in range(far - 1):
        for part in range(2):
            u_pass(step, part)
    small_cross(0)
    for slot, source in enumerate((left, right, opp)):
        for way in range(2):
            arrived(w_span(1 - odd, source, way), wy_recv.at[slot, way])
        w_pair(1 - odd, source, 3 + slot)
    arrived(wb.at[:, :, x], w_own)
    for slot, source in enumerate((left, right, opp)):
        arrived(wb.at[odd, :, source, 1 - core], ws_recv.at[slot])
        arrived(wb.at[1 - odd, :, source, 1 - core], ws_recv.at[3 + slot])
    for part in range(2):
        yacc[part] = nt(w_block(z), uall[z, part]).reshape(yacc.shape[1:])
        for step in range(far - 1):
            for way in range(2):
                if step < hops[way]:
                    accumulate(zs(-ways[way] * (step + 1)), part)

    def y_start(part, kind, piece, value, device):
        ystage[part, kind, piece] = value.astype(BF16)
        send(
            ystage.at[part, kind, piece],
            yrecv.at[part, kind, piece],
            y_send.at[part, kind, piece],
            y_recv.at[part, kind, piece],
            device,
        )

    def y_arrived(part, kind, piece):
        arrived(yrecv.at[part, kind, piece], y_recv.at[part, kind, piece])
        return yrecv[part, kind, piece].astype(F32)

    for part in range(2):
        u_pass(far - 1, part)
        for way in range(2):
            if far == hops[way]:
                accumulate(zs(-ways[way] * far), part)
        y_start(part, 0, 0, yacc[part, opp, 0], at_x(1))
        y_start(part, 0, 1, yacc[part, opp, 1], at_x(-1))
        y_start(part, 1, 1, yacc[part, right, 1], at_x(1))
        y_start(part, 1, 0, yacc[part, left, 0], at_x(-1))
    for part in range(2):
        y_start(part, 2, 0, yacc[part, right, 0] + y_arrived(part, 0, 0), at_x(1))
        y_start(part, 2, 1, yacc[part, left, 1] + y_arrived(part, 0, 1), at_x(-1))

    inv_rms = lax.rsqrt(small_sum(0) / total_features + EPS)

    def g_start(part, source, piece, kind, device):
        ref = gx.at[part, source, piece]
        send(ref, ref, g_send.at[part, kind, piece], g_recv.at[part, kind, piece], device)

    def g_arrived(part, source, piece, kind):
        arrived(gx.at[part, source, piece], g_recv.at[part, kind, piece])

    products = []
    for part in range(2):
        span = slice(part * half_tokens, (part + 1) * half_tokens)
        product = jnp.zeros((1, half_tokens), F32)
        for piece in range(2):
            total = yacc[part, x, piece] + y_arrived(part, 1, piece) + y_arrived(part, 2, piece)
            rounded = (total * inv_rms[:, span]).astype(BF16)
            out_ref[piece * half : (piece + 1) * half, span] = rounded
            wanted = target_ref[piece * half : (piece + 1) * half, span].astype(F32)
            grad = (rounded.astype(F32) - wanted).astype(BF16)
            gx[part, x, piece] = grad
            g_start(part, x, piece, piece, at_x(1 - 2 * piece))
            product = product + jnp.sum(grad.astype(F32) * total, axis=0, keepdims=True)
        g_start(part, x, 1, 0, at_x(1))
        g_start(part, x, 0, 1, at_x(-1))
        products.append(product)
    small_share(1, jnp.concatenate(products, axis=1))
    stores = [
        pltpu.make_async_copy(src, dst, out_sems.at[index])
        for index, (src, dst) in enumerate(
            ((out_ref, out_to), (qg_ref, qg_to), (kg_ref, kg_to), (vg_ref, vg_to), (gg_ref, gg_to))
        )
    ]
    stores[0].start()
    for part in range(2):
        g_arrived(part, left, 0, 0)
        g_start(part, left, 0, 2, at_x(1))
        g_arrived(part, right, 1, 1)
        g_start(part, right, 1, 2, at_x(-1))

    eye = identity(half_tokens)

    def feature_part(block, part):
        return nn(gall[part], w_block(block))

    def f_slot(way, step):
        return way * far + step

    def f_start(way, step, part, h, value):
        slot = f_slot(way, step)
        fstage[slot, part, h] = value.astype(BF16)
        send(
            fstage.at[slot, part, h],
            frecv.at[slot, part, h],
            f_send.at[slot, part, h],
            f_recv.at[slot, part, h],
            at_z(ways[way]),
        )

    def f_arrived(way, step, part, h):
        slot = f_slot(way, step)
        arrived(frecv.at[slot, part, h], f_recv.at[slot, part, h])
        return frecv[slot, part, h].astype(F32)

    for step in range(far):
        for part in range(2):
            if step == 0:
                g_arrived(part, left, 1, 0)
                g_arrived(part, right, 0, 1)
                for piece in range(2):
                    g_arrived(part, opp, piece, 2)
                gall[part] = nt(eye, gx[part].reshape(X * rows, half_tokens)).astype(BF16)
            sums = [
                feature_part(zs(ways[way] * (hops[way] - step)), part) if step < hops[way] else None
                for way in range(2)
            ]
            for h in range(heads):
                for way in range(2):
                    if step < hops[way]:
                        value = sums[way][:, lanes(h)]
                        if step > 0:
                            value = value + f_arrived(way, step - 1, part, h)
                        f_start(way, step, part, h, value)
        if step == 0:
            small_cross(1)

    own_feature = [feature_part(z, part) for part in range(2)]
    mean_product = as_columns(small_sum(1) / total_features)
    inv = as_columns(inv_rms)

    for h in range(heads):
        pieces = []
        for part in range(2):
            value = own_feature[part][:, lanes(h)]
            for way in range(2):
                if hops[way] > 0:
                    value = value + f_arrived(way, hops[way] - 1, part, h)
            pieces.append(value)
        attended = att[:, lanes(h)]
        gate_open = jax.nn.sigmoid(gate_ref[:, lanes(h)].astype(F32))
        normed_grad = jnp.concatenate(pieces, axis=0) * gain[:, lanes(h)] * gate_open
        grad = (inv * normed_grad - inv * inv * inv * attended * mean_product).astype(BF16)
        agrad[:, lanes(h)] = grad
        decayed = (q_ref[:, lanes(h)].astype(F32) * jnp.exp(cums[h])).astype(BF16)
        scan_give(1, h, tn(decayed, grad))
        gg_ref[:, lanes(h)] = (normed_grad * attended * inv * (1.0 - gate_open)).astype(BF16)
    stores[4].start()

    for h in range(heads):
        grad = agrad[:, lanes(h)]
        score_grad = (nt(grad, v_ref[:, lanes(h)]) * weight[h]).astype(BF16)
        if h == 0:
            scan_send(1)
        qg_ref[:, lanes(h)] = (
            nn(score_grad, k_ref[:, lanes(h)]) + jnp.exp(cums[h]) * nt(grad, state[0, h])
        ).astype(BF16)
        klocal[:, lanes(h)] = tn(score_grad, q_ref[:, lanes(h)])
        vlocal[:, lanes(h)] = tn(probs[h], grad)
    stores[1].start()
    scan_end(1)
    for h in range(heads):
        later = state[1, h]
        kg_ref[:, lanes(h)] = (
            klocal[:, lanes(h)] + jnp.exp(totals[h] - cums[h]) * nt(v_ref[:, lanes(h)], later)
        ).astype(BF16)
        vg_ref[:, lanes(h)] = (vlocal[:, lanes(h)] + nn(kdec[:, lanes(h)], later)).astype(BF16)

    stores[2].start()
    stores[3].start()

    for index in range(4):
        arrived(wrelay, w_send.at[index])
    for index in range(6):
        arrived(wrelay, ws_send.at[index])
    for slot in range(3):
        for way in range(2):
            arrived(w_span(odd, x, way), wy_send.at[slot, way])
    for way in range(2):
        for step in range(hops[way]):
            for part in range(2):
                arrived(u_part(way, step, part), u_send.at[way, step, part])
                slot = f_slot(way, step)
                for h in range(heads):
                    arrived(fstage.at[slot, part, h], f_send.at[slot, part, h])
    for part in range(2):
        for kind in range(3):
            for piece in range(2):
                arrived(ystage.at[part, kind, piece], y_send.at[part, kind, piece])
                arrived(ystage.at[part, kind, piece], g_send.at[part, kind, piece])
    arrived(bown, b_send)
    for distance in range(1, Y):
        arrived(bown, bc_send.at[distance - 1])
    for turn in range(2):
        arrived(s_out.at[turn], s_send.at[turn])
        arrived(c_out.at[turn], c_send.at[turn])
        step, _ = scan_way(turn)
        for distance in range(1, Y):

            @pl.when(reaches(y + step * distance))
            def _():
                arrived(t_out.at[turn], t_send.at[turn, distance - 1])

        for distance in range(1, Z):
            arrived(small_z.at[turn, 0], sz_send.at[turn, distance - 1])
        for distance in range(1, X):
            arrived(small_x.at[turn, 0], sx_send.at[turn, distance - 1])
    for copy in stores:
        copy.wait()


def store(*refs):
    count = len(refs) // 2
    for src, dst in zip(refs[:count], refs[count:]):
        dst[...] = src[...]


def on_device(chips, queries, keys, values, log_decay, gate, norm_gain, out_weight, target):
    Y, Z = chips
    tokens, width = queries.shape
    rows, features = out_weight.shape
    half = rows // 2
    far = Z // 2
    vmem = pltpu.VMEM
    dma = pltpu.SemaphoreType.DMA
    scratch = [
        vmem((rows, tokens), BF16),
        vmem((tokens, width), BF16),
        vmem((tokens, width), BF16),
        vmem((tokens, width), BF16),
        vmem((tokens, width), BF16),
        dma((5,)),
        vmem((tokens, width), BF16),
        vmem((tokens, width), BF16),
        vmem((tokens, width), BF16),
        vmem((width // DH, tokens), F32),
        vmem((tokens, width), BF16),
        vmem((1, width), F32),
        vmem((rows, tokens), BF16),
        dma((7,)),
        vmem((2, Z // 2, X, 2, half, width), BF16),
        vmem((Z // 2, half, width), BF16),
        vmem((Z, 2, tokens // 2, width), BF16),
        vmem((2, X, 2, half, tokens // 2), F32),
        vmem((2, 3, 2, half, tokens // 2), BF16),
        vmem((2, 3, 2, half, tokens // 2), BF16),
        vmem((2, X, 2, half, tokens // 2), BF16),
        vmem((2, tokens // 2, X * rows), BF16),
        vmem((Z - 1, 2, 2, tokens // 2, DH), BF16),
        vmem((Z - 1, 2, 2, tokens // 2, DH), BF16),
        vmem((width // DH, tokens, tokens), F32),
        vmem((width // DH, tokens, tokens), BF16),
        vmem((tokens, width), BF16),
        vmem((tokens, width), F32),
        vmem((tokens, width), F32),
        vmem((tokens, width), F32),
        vmem((tokens, width), BF16),
        vmem((8, 128), F32),
        vmem((8, 128), F32),
        vmem((Y, 8, 128), F32),
        vmem((2, DH, DH), BF16),
        vmem((2, DH, DH), BF16),
        vmem((2, DH, DH), F32),
        vmem((2, DH, DH), BF16),
        vmem((2, max(Y - 1, 1), DH, DH), BF16),
        vmem((DH, DH), F32),
        vmem((8, 128), F32),
        vmem((2, DH, DH), BF16),
        vmem((2, 2, DH, DH), BF16),
        vmem((2, Z, 1, tokens), F32),
        vmem((2, X, 1, tokens), F32),
        dma((4,)),
        dma((4,)),
        dma,
        dma((6,)),
        dma((6,)),
        dma((3, 2)),
        dma((3, 2)),
        dma((2, far, 2)),
        dma((2, far, 2)),
        dma((2, 3, 2)),
        dma((2, 3, 2)),
        dma((2, 3, 2)),
        dma((2, 3, 2)),
        dma((Z - 1, 2, 2)),
        dma((Z - 1, 2, 2)),
        dma,
        dma,
        dma((max(Y - 1, 1),)),
        dma((max(Y - 1, 1),)),
        dma((2,)),
        dma((2,)),
        dma((2, max(Y - 1, 1))),
        dma((2, max(Y - 1, 1))),
        dma((2,)),
        dma((2,)),
        dma((2, Z - 1)),
        dma((2, Z - 1)),
        dma((2, X - 1)),
        dma((2, X - 1)),
    ]
    in_vmem = pl.BlockSpec(memory_space=pltpu.VMEM)
    in_hbm = pl.BlockSpec(memory_space=pltpu.HBM)
    wide = jax.ShapeDtypeStruct((tokens, width), BF16)
    out_shape = (jax.ShapeDtypeStruct((rows, tokens), BF16), wide, wide, wide, wide)
    results = pl.pallas_call(
        functools.partial(kernel, chips),
        out_shape=out_shape,
        in_specs=[in_hbm] * 8,
        out_specs=(in_hbm,) * 5,
        scratch_shapes=scratch,
        compiler_params=pltpu.CompilerParams(
            collective_id=0, has_side_effects=True, vmem_limit_bytes=63 * 1024 * 1024
        ),
        cost_estimate=pl.CostEstimate(flops=2 * 10**9, bytes_accessed=8 * 10**6, transcendentals=10**6),
        name="attention_layer",
    )(queries, keys, values, log_decay.T, gate, norm_gain.reshape(1, width), out_weight, target.T)
    output, *grads = pl.pallas_call(
        store,
        out_shape=out_shape,
        in_specs=[in_vmem] * 5,
        out_specs=(in_vmem,) * 5,
        compiler_params=pltpu.CompilerParams(vmem_limit_bytes=63 * 1024 * 1024),
        name="store",
    )(*results)
    return (output.T, *grads)


def solution(mesh):
    chips = (mesh.shape["ctx"] // 2, mesh.shape["tp"] // X)
    return jax.shard_map(
        functools.partial(on_device, chips),
        mesh=mesh,
        in_specs=(
            P("ctx", "tp"),
            P("ctx", "tp"),
            P("ctx", "tp"),
            P("ctx", "tp"),
            P("ctx", "tp"),
            P("tp"),
            P("tp", None),
            P("ctx", "tp"),
        ),
        out_specs=(P("ctx", "tp"),) * 5,
        check_vma=False,
    )
```

```python
import functools

import jax
import jax.numpy as jnp
from jax import lax
from jax.experimental import pallas as pl
from jax.experimental.pallas import tpu as pltpu
from jax.sharding import PartitionSpec as P

DH = 128
EPS = 1e-06
MESH = pl.DeviceIdType.MESH
F32 = jnp.float32
BF16 = jnp.bfloat16
X = 4


def nn(a, b):
    return lax.dot_general(a, b, (((1,), (0,)), ((), ())), preferred_element_type=F32)


def nt(a, b):
    return lax.dot_general(a, b, (((1,), (1,)), ((), ())), preferred_element_type=F32)


def tn(a, b):
    return lax.dot_general(a, b, (((0,), (0,)), ((), ())), preferred_element_type=F32)


def identity(size):
    row = lax.broadcasted_iota(jnp.int32, (size, size), 0)
    column = lax.broadcasted_iota(jnp.int32, (size, size), 1)
    return jnp.where(row == column, 1.0, 0.0).astype(BF16)


def as_row(column):
    return jnp.broadcast_to(column, (column.shape[0], 128)).T[0:1, :]


def as_columns(row):
    return jnp.broadcast_to(row, (128, row.shape[1])).T


def kernel(
    sizes,
    q_in,
    k_in,
    v_in,
    ld_in,
    gate_in,
    gain_in,
    w_ref,
    target_in,
    out_ref,
    qg_ref,
    kg_ref,
    vg_ref,
    gg_ref,
    q_ref,
    k_ref,
    v_ref,
    ld_ref,
    gate_ref,
    gain_ref,
    target_ref,
    in_sems,
    wb,
    wrelay,
    uall,
    yacc,
    ystage,
    yrecv,
    gx,
    gall,
    fstage,
    frecv,
    weight,
    probs,
    kdec,
    att,
    klocal,
    vlocal,
    agrad,
    until_end,
    from_start,
    qdec,
    scale,
    closed,
    bown,
    bsib,
    bchip,
    s_out,
    s_in,
    s_keep,
    t_out,
    t_in,
    c_acc,
    d_acc,
    c_out,
    state,
    small_z,
    small_x,
    w_send,
    w_recv,
    w_own,
    ws_send,
    ws_recv,
    u_send,
    u_recv,
    y_send,
    y_recv,
    g_send,
    g_recv,
    f_send,
    f_recv,
    b_send,
    b_recv,
    bc_send,
    bc_recv,
    s_send,
    s_recv,
    t_send,
    t_recv,
    c_send,
    c_recv,
    sz_send,
    sz_recv,
    sx_send,
    sx_recv,
):
    Y, Z = sizes
    tokens = q_ref.shape[0]
    half_tokens = tokens // 2
    rows = w_ref.shape[0]
    half = rows // 2
    width = q_ref.shape[1]
    total_features = w_ref.shape[1]
    heads = width // DH

    ctx = lax.axis_index("ctx")
    tp = lax.axis_index("tp")
    core = lax.rem(ctx, 2)
    y = lax.div(ctx, 2)
    x = lax.rem(tp, X)
    z = lax.div(tp, X)
    sibling = (y * 2 + 1 - core, tp)
    is_zero = core == 0

    def xs(step):
        return lax.rem(x + step + X, X)

    def zs(step):
        return lax.rem(z + step + 2 * Z, Z)

    def at_x(step):
        return (ctx, z * X + xs(step))

    def at_z(step):
        return (ctx, zs(step) * X + x)

    def at_y(place):
        return (place * 2 + core, tp)

    sign = 1 - 2 * core
    left, right, opp = xs(-1), xs(1), xs(2)

    def send(src, dst, send_sem, recv_sem, device):
        copy = pltpu.make_async_remote_copy(
            src_ref=src,
            dst_ref=dst,
            send_sem=send_sem,
            recv_sem=recv_sem,
            device_id=device,
            device_id_type=MESH,
        )
        copy.start()

    def arrived(ref, sem):
        pltpu.make_async_copy(ref, ref, sem).wait()

    loads = [
        pltpu.make_async_copy(src, dst, in_sems.at[index])
        for index, (src, dst) in enumerate(
            (
                (ld_in, ld_ref),
                (k_in, k_ref),
                (v_in, v_ref),
                (q_in, q_ref),
                (gate_in, gate_ref),
                (gain_in, gain_ref),
                (target_in, target_ref),
            )
        )
    ]
    for load in loads:
        load.start()
    barrier = pltpu.get_barrier_semaphore()
    partners = [sibling] + [at_x(step) for step in range(1, X)]
    partners += [at_z(step) for step in range(1, Z)]
    partners += [at_y(lax.rem(y + step, Y)) for step in range(1, Y)]
    for partner in partners:
        pl.semaphore_signal(barrier, inc=1, device_id=partner, device_id_type=MESH)

    def w_columns(block, x_to):
        start = pl.multiple_of((block * X + x_to) * width, width)
        return pl.ds(start, width)

    my_rows = pl.ds(pl.multiple_of(core * half, half), half)
    x_far = xs(sign)

    def w_far(block, carry):
        send(w_ref.at[my_rows, w_columns(block, opp)], wrelay.at[block], w_send.at[0], w_recv.at[0], (ctx, z * X + x_far))
        return carry

    def w_near(block, carry):
        send(w_ref.at[my_rows, w_columns(block, right)], wb.at[block, x, core], w_send.at[1], w_recv.at[1], at_x(1))
        send(w_ref.at[my_rows, w_columns(block, left)], wb.at[block, x, core], w_send.at[2], w_recv.at[2], at_x(-1))
        return carry

    def w_mine(block, carry):
        for part in range(2):
            pltpu.make_async_copy(
                w_ref.at[pl.ds(part * half, half), w_columns(block, x)], wb.at[block, x, part], w_own
            ).start()
        return carry

    row = lax.broadcasted_iota(jnp.int32, (tokens, tokens), 0)
    column = lax.broadcasted_iota(jnp.int32, (tokens, tokens), 1)
    causal = row >= column
    loads[0].wait()
    upto = jnp.where(row <= column, 1.0, 0.0).astype(BF16)
    rest = ld_ref[...]
    cum = jnp.zeros_like(rest)
    for _ in range(3):
        piece = rest.astype(BF16)
        cum = cum + nn(piece, upto)
        rest = rest - piece.astype(F32)
    cum_rows = [cum[h : h + 1, :] for h in range(heads)]
    cums = [as_columns(c) for c in cum_rows]
    totals = [c[tokens - 1 : tokens, :] for c in cums]
    bown[...] = jnp.zeros_like(bown)
    for h in range(heads):
        bown[h : h + 1, :] = totals[h]
    loads[1].wait()
    loads[2].wait()

    def lanes(h):
        return slice(h * DH, (h + 1) * DH)

    own = []
    for h in range(heads):
        until_end[h] = jnp.exp(totals[h] - cums[h])
        decayed = (k_ref[:, lanes(h)].astype(F32) * until_end[h]).astype(BF16)
        kdec[:, lanes(h)] = decayed
        own.append(tn(decayed, v_ref[:, lanes(h)]))

    def of_core(pair):
        return jnp.where(is_zero, pair[0], pair[1])

    def scan_give(turn, h, value):
        @pl.when(core == h)
        def _():
            s_keep[turn] = value

        @pl.when(core != h)
        def _():
            s_out[turn] = value.astype(BF16)
            send(s_out.at[turn], s_in.at[turn], s_send.at[turn], s_recv.at[turn], sibling)

    def scan_way(turn):
        step = 1 if turn == 0 else -1
        first_here = is_zero if turn == 0 else jnp.logical_not(is_zero)
        return step, first_here

    def decays(ref):
        return of_core((ref[0:1, :], ref[1:2, :]))

    def reaches(place):
        return jnp.logical_and(place >= 0, place < Y)

    def scan_send(turn):
        step, first_here = scan_way(turn)
        arrived(s_in.at[turn], s_recv.at[turn])
        mine = s_keep[turn]
        theirs = s_in[turn].astype(F32)
        first = jnp.where(first_here, mine, theirs)
        second = jnp.where(first_here, theirs, mine)
        s_keep[turn] = first
        b_second = jnp.where(first_here, decays(bsib), decays(bown))
        t_out[turn] = (jnp.exp(b_second) * first + second).astype(BF16)
        for distance in range(1, Y):
            place = y + step * distance

            @pl.when(reaches(place))
            def _():
                send(
                    t_out.at[turn],
                    t_in.at[turn, distance - 1],
                    t_send.at[turn, distance - 1],
                    t_recv.at[turn, distance - 1],
                    at_y(place),
                )

    def scan_end(turn):
        step, first_here = scan_way(turn)
        c_acc[...] = jnp.zeros_like(c_acc)
        d_acc[...] = jnp.zeros_like(d_acc)
        for distance in range(1, Y):
            place = y - step * distance

            @pl.when(reaches(place))
            def _():
                slot = t_in.at[turn, distance - 1]
                arrived(slot, t_recv.at[turn, distance - 1])
                between = d_acc[0:1, :]
                c_acc[...] += jnp.exp(between) * slot[...].astype(F32)
                d_acc[0:1, :] = between + decays(bchip.at[place])

        b_first = jnp.where(first_here, decays(bown), decays(bsib))
        carried = c_acc[...]
        after = jnp.exp(b_first) * carried + s_keep[turn]
        state[turn, core] = jnp.where(first_here, carried, after).astype(BF16)
        c_out[turn] = jnp.where(first_here, after, carried).astype(BF16)
        send(c_out.at[turn], state.at[turn, core], c_send.at[turn], c_recv.at[turn], sibling)

    def scan_take(turn):
        arrived(state.at[turn, 1 - core], c_recv.at[turn])

    pl.semaphore_wait(barrier, len(partners))
    send(bown, bsib, b_send, b_recv, sibling)
    for h in range(heads):
        scan_give(0, h, own[h])
    lax.fori_loop(0, Z, w_far, 0)
    lax.fori_loop(0, Z, w_near, 0)
    lax.fori_loop(0, Z, w_mine, 0)

    arrived(bsib, b_recv)
    bchip[y] = bown[...] + bsib[...]
    for distance in range(1, Y):
        place = lax.rem(y + distance, Y)
        send(bchip.at[y], bchip.at[y], bc_send.at[distance - 1], bc_recv.at[distance - 1], at_y(place))
    scan_send(0)

    for load in loads[3:]:
        load.wait()
    for h in range(heads):
        gaps = cums[h][:, 0:1] - cum_rows[h]
        decay = jnp.where(causal, jnp.exp(jnp.minimum(gaps, 0.0)), 0.0)
        weight[h] = decay
        probs[h] = (nt(q_ref[:, lanes(h)], k_ref[:, lanes(h)]) * decay).astype(BF16)
        att[:, lanes(h)] = nn(probs[h], v_ref[:, lanes(h)])
        from_start[h] = jnp.exp(cums[h])
        qdec[:, lanes(h)] = (q_ref[:, lanes(h)].astype(F32) * from_start[h]).astype(BF16)
        gate_open = jax.nn.sigmoid(gate_ref[:, lanes(h)].astype(F32))
        scale[:, lanes(h)] = gain_ref[:, lanes(h)] * gate_open
        closed[:, lanes(h)] = 1.0 - gate_open

    for distance in range(1, Y):
        arrived(bchip.at[lax.rem(y - distance + Y, Y)], bc_recv.at[distance - 1])

    arrived(wrelay, w_recv.at[0])
    send(wrelay, wb.at[:, xs(-sign), core], w_send.at[3], w_recv.at[3], (ctx, z * X + x_far))

    scan_end(0)
    scan_take(0)

    far, near = Z // 2, Z - 1 - Z // 2
    hops = (far, near)
    ways = (sign, -sign)

    def u_part(way, step, part):
        return uall.at[zs(-ways[way] * step), part]

    def u_start(way, step, part):
        ref = u_part(way, step, part)
        send(ref, ref, u_send.at[way, step, part], u_recv.at[way, step, part], at_z(ways[way]))

    for part in range(2):
        span = slice(part * half_tokens, (part + 1) * half_tokens)
        for h in range(heads):
            from_state = nn(q_ref[span, lanes(h)], state[0, h]) * from_start[h, span, :]
            attended = att[span, lanes(h)] + from_state
            att[span, lanes(h)] = attended
            uall[z, part, :, lanes(h)] = (attended * scale[span, lanes(h)]).astype(BF16)
        for way in range(2):
            if hops[way] > 0:
                u_start(way, 0, part)

    def small_share(turn, value):
        small_z[turn, 0] = value
        for step in range(1, Z):
            send(small_z.at[turn, 0], small_z.at[turn, step], sz_send.at[turn, step - 1], sz_recv.at[turn, step - 1], at_z(step))

    def small_cross(turn):
        for step in range(1, Z):
            arrived(small_z.at[turn, step], sz_recv.at[turn, step - 1])
        sum_z = small_z[turn, 0]
        for step in range(1, Z):
            sum_z = sum_z + small_z[turn, step]
        small_x[turn, 0] = sum_z
        for step in range(1, X):
            send(small_x.at[turn, 0], small_x.at[turn, step], sx_send.at[turn, step - 1], sx_recv.at[turn, step - 1], at_x(step))

    def small_sum(turn):
        for step in range(1, X):
            arrived(small_x.at[turn, step], sx_recv.at[turn, step - 1])
        sum_x = small_x[turn, 0]
        for step in range(1, X):
            sum_x = sum_x + small_x[turn, step]
        return sum_x

    squares = jnp.zeros((tokens, 1), F32)
    for h in range(heads):
        attended = att[:, lanes(h)]
        squares = squares + jnp.sum(attended * attended, axis=1, keepdims=True)
    small_share(0, as_row(squares))

    def w_pair(source, sem, slot):
        ref = wb.at[:, source, core]
        arrived(ref, sem)
        send(ref, ref, ws_send.at[slot], ws_recv.at[slot], sibling)

    def w_block(block):
        return wb[block].reshape(X * rows, width)

    def accumulate(block, part):
        yacc[part] += nt(w_block(block), uall[block, part]).reshape(yacc.shape[1:])

    def u_pass(step, part):
        for way in range(2):
            if step < hops[way]:
                arrived(u_part(way, step + 1, part), u_recv.at[way, step, part])
                if step + 1 < hops[way]:
                    u_start(way, step + 1, part)

    def absorb(step):
        for way in range(2):
            if step < hops[way]:
                for part in range(2):
                    accumulate(zs(-ways[way] * (step + 1)), part)

    def w_first():
        w_pair(left, w_recv.at[1], 0)
        w_pair(right, w_recv.at[2], 1)

    def w_second():
        small_cross(0)
        w_pair(opp, w_recv.at[3], 2)

    def w_third():
        for part in range(2):
            arrived(wb.at[:, x, part], w_own)
        for slot, source in enumerate((left, right, opp)):
            arrived(wb.at[:, source, 1 - core], ws_recv.at[slot])
        for part in range(2):
            yacc[part] = nt(w_block(z), uall[z, part]).reshape(yacc.shape[1:])

    stages = [w_first, w_second, w_third]
    ready = 0
    for step in range(far - 1):
        for part in range(2):
            u_pass(step, part)
        if step < len(stages) - 1:
            stages[step]()
        if step == len(stages) - 2 or step == far - 2:
            for stage in stages[min(step, len(stages) - 2) + 1 :]:
                stage()
            stages = []
        if not stages:
            while ready <= step:
                absorb(ready)
                ready += 1
    for stage in stages:
        stage()

    def y_start(part, kind, piece, value, device):
        ystage[part, kind, piece] = value.astype(BF16)
        send(
            ystage.at[part, kind, piece],
            yrecv.at[part, kind, piece],
            y_send.at[part, kind, piece],
            y_recv.at[part, kind, piece],
            device,
        )

    def y_arrived(part, kind, piece):
        arrived(yrecv.at[part, kind, piece], y_recv.at[part, kind, piece])
        return yrecv[part, kind, piece].astype(F32)

    for part in range(2):
        u_pass(far - 1, part)
        last = zs(sign * far)
        last_u = uall[last, part]

        def finish(rows_of):
            block = wb[last, rows_of].reshape(rows, width)
            yacc[part, rows_of] += nt(block, last_u).reshape(yacc.shape[2:])

        finish(opp)
        y_start(part, 0, 0, yacc[part, opp, 0], at_x(1))
        y_start(part, 0, 1, yacc[part, opp, 1], at_x(-1))
        finish(right)
        y_start(part, 1, 1, yacc[part, right, 1], at_x(1))
        finish(left)
        y_start(part, 1, 0, yacc[part, left, 0], at_x(-1))
        finish(x)
    for part in range(2):
        y_start(part, 2, 0, yacc[part, right, 0] + y_arrived(part, 0, 0), at_x(1))
        y_start(part, 2, 1, yacc[part, left, 1] + y_arrived(part, 0, 1), at_x(-1))

    inv_rms = lax.rsqrt(small_sum(0) / total_features + EPS)

    def g_start(part, source, piece, kind, device):
        ref = gx.at[part, source, piece]
        send(ref, ref, g_send.at[part, kind, piece], g_recv.at[part, kind, piece], device)

    def g_arrived(part, source, piece, kind):
        arrived(gx.at[part, source, piece], g_recv.at[part, kind, piece])

    products = []
    for part in range(2):
        span = slice(part * half_tokens, (part + 1) * half_tokens)
        product = jnp.zeros((1, half_tokens), F32)
        for piece in range(2):
            total = yacc[part, x, piece] + y_arrived(part, 1, piece) + y_arrived(part, 2, piece)
            rounded = (total * inv_rms[:, span]).astype(BF16)
            out_ref[piece * half : (piece + 1) * half, span] = rounded
            wanted = target_ref[piece * half : (piece + 1) * half, span].astype(F32)
            grad = (rounded.astype(F32) - wanted).astype(BF16)
            gx[part, x, piece] = grad
            g_start(part, x, piece, piece, at_x(1 - 2 * piece))
            product = product + jnp.sum(grad.astype(F32) * total, axis=0, keepdims=True)
        g_start(part, x, 1, 0, at_x(1))
        g_start(part, x, 0, 1, at_x(-1))
        products.append(product)
    small_share(1, jnp.concatenate(products, axis=1))
    for part in range(2):
        g_arrived(part, left, 0, 0)
        g_start(part, left, 0, 2, at_x(1))
        g_arrived(part, right, 1, 1)
        g_start(part, right, 1, 2, at_x(-1))

    eye = identity(half_tokens)

    def feature_part(block, part):
        return nn(gall[part], w_block(block))

    def f_slot(way, step):
        return way * far + step

    def f_start(way, step, part, h, value):
        slot = f_slot(way, step)
        fstage[slot, part, h] = value.astype(BF16)
        send(
            fstage.at[slot, part, h],
            frecv.at[slot, part, h],
            f_send.at[slot, part, h],
            f_recv.at[slot, part, h],
            at_z(ways[way]),
        )

    def f_arrived(way, step, part, h):
        slot = f_slot(way, step)
        arrived(frecv.at[slot, part, h], f_recv.at[slot, part, h])
        return frecv[slot, part, h].astype(F32)

    for step in range(far):
        for part in range(2):
            if step == 0:
                g_arrived(part, left, 1, 0)
                g_arrived(part, right, 0, 1)
                for piece in range(2):
                    g_arrived(part, opp, piece, 2)
                gall[part] = nt(eye, gx[part].reshape(X * rows, half_tokens)).astype(BF16)
            sums = [
                feature_part(zs(ways[way] * (hops[way] - step)), part) if step < hops[way] else None
                for way in range(2)
            ]
            for h in range(heads):
                for way in range(2):
                    if step < hops[way]:
                        value = sums[way][:, lanes(h)]
                        if step > 0:
                            value = value + f_arrived(way, step - 1, part, h)
                        f_start(way, step, part, h, value)
        if step == 0:
            small_cross(1)

    own_feature = [feature_part(z, part) for part in range(2)]
    mean_product = as_columns(small_sum(1) / total_features)
    inv = as_columns(inv_rms)

    for h in range(heads):
        pieces = []
        for part in range(2):
            value = own_feature[part][:, lanes(h)]
            for way in range(2):
                if hops[way] > 0:
                    value = value + f_arrived(way, hops[way] - 1, part, h)
            pieces.append(value)
        attended = att[:, lanes(h)]
        normed_grad = jnp.concatenate(pieces, axis=0) * scale[:, lanes(h)]
        grad = (inv * normed_grad - inv * inv * inv * attended * mean_product).astype(BF16)
        agrad[:, lanes(h)] = grad
        scan_give(1, h, tn(qdec[:, lanes(h)], grad))
        gg_ref[:, lanes(h)] = (normed_grad * attended * inv * closed[:, lanes(h)]).astype(BF16)

    for h in range(heads):
        grad = agrad[:, lanes(h)]
        score_grad = (nt(grad, v_ref[:, lanes(h)]) * weight[h]).astype(BF16)
        if h == 0:
            scan_send(1)
        qg_ref[:, lanes(h)] = (
            nn(score_grad, k_ref[:, lanes(h)]) + from_start[h] * nt(grad, state[0, h])
        ).astype(BF16)
        klocal[:, lanes(h)] = tn(score_grad, q_ref[:, lanes(h)])
        vlocal[:, lanes(h)] = tn(probs[h], grad)
    for index in range(4):
        arrived(wrelay, w_send.at[index])
    for index in range(3):
        arrived(wrelay, ws_send.at[index])
    for way in range(2):
        for step in range(hops[way]):
            for part in range(2):
                arrived(u_part(way, step, part), u_send.at[way, step, part])
                slot = f_slot(way, step)
                for h in range(heads):
                    arrived(fstage.at[slot, part, h], f_send.at[slot, part, h])
    for part in range(2):
        for kind in range(3):
            for piece in range(2):
                arrived(ystage.at[part, kind, piece], y_send.at[part, kind, piece])
                arrived(ystage.at[part, kind, piece], g_send.at[part, kind, piece])
    arrived(bown, b_send)
    for distance in range(1, Y):
        arrived(bown, bc_send.at[distance - 1])
    for turn in range(2):
        arrived(s_out.at[turn], s_send.at[turn])
        for distance in range(1, Z):
            arrived(small_z.at[turn, 0], sz_send.at[turn, distance - 1])
        for distance in range(1, X):
            arrived(small_x.at[turn, 0], sx_send.at[turn, distance - 1])

    def scan_sent(turn):
        arrived(c_out.at[turn], c_send.at[turn])
        step, _ = scan_way(turn)
        for distance in range(1, Y):

            @pl.when(reaches(y + step * distance))
            def _():
                arrived(t_out.at[turn], t_send.at[turn, distance - 1])

    scan_sent(0)

    scan_end(1)
    scan_take(1)
    for h in range(heads):
        later = state[1, h]
        kg_ref[:, lanes(h)] = (
            klocal[:, lanes(h)] + until_end[h] * nt(v_ref[:, lanes(h)], later)
        ).astype(BF16)
        vg_ref[:, lanes(h)] = (vlocal[:, lanes(h)] + nn(kdec[:, lanes(h)], later)).astype(BF16)

    scan_sent(1)


def store(*refs):
    *refs, sems = refs
    count = len(refs) // 2
    copies = [pltpu.make_async_copy(refs[i], refs[count + i], sems.at[i]) for i in range(count)]
    for copy in copies:
        copy.start()
    for copy in copies:
        copy.wait()


def on_device(chips, queries, keys, values, log_decay, gate, norm_gain, out_weight, target):
    Y, Z = chips
    tokens, width = queries.shape
    rows, features = out_weight.shape
    half = rows // 2
    far = Z // 2
    vmem = pltpu.VMEM
    dma = pltpu.SemaphoreType.DMA
    scratch = [
        vmem((tokens, width), BF16),
        vmem((tokens, width), BF16),
        vmem((tokens, width), BF16),
        vmem((width // DH, tokens), F32),
        vmem((tokens, width), BF16),
        vmem((1, width), F32),
        vmem((rows, tokens), BF16),
        dma((7,)),
        vmem((Z, X, 2, half, width), BF16),
        vmem((Z, half, width), BF16),
        vmem((Z, 2, tokens // 2, width), BF16),
        vmem((2, X, 2, half, tokens // 2), F32),
        vmem((2, 3, 2, half, tokens // 2), BF16),
        vmem((2, 3, 2, half, tokens // 2), BF16),
        vmem((2, X, 2, half, tokens // 2), BF16),
        vmem((2, tokens // 2, X * rows), BF16),
        vmem((Z - 1, 2, 2, tokens // 2, DH), BF16),
        vmem((Z - 1, 2, 2, tokens // 2, DH), BF16),
        vmem((width // DH, tokens, tokens), F32),
        vmem((width // DH, tokens, tokens), BF16),
        vmem((tokens, width), BF16),
        vmem((tokens, width), F32),
        vmem((tokens, width), F32),
        vmem((tokens, width), F32),
        vmem((tokens, width), BF16),
        vmem((width // DH, tokens, DH), F32),
        vmem((width // DH, tokens, DH), F32),
        vmem((tokens, width), BF16),
        vmem((tokens, width), F32),
        vmem((tokens, width), F32),
        vmem((8, 128), F32),
        vmem((8, 128), F32),
        vmem((Y, 8, 128), F32),
        vmem((2, DH, DH), BF16),
        vmem((2, DH, DH), BF16),
        vmem((2, DH, DH), F32),
        vmem((2, DH, DH), BF16),
        vmem((2, max(Y - 1, 1), DH, DH), BF16),
        vmem((DH, DH), F32),
        vmem((8, 128), F32),
        vmem((2, DH, DH), BF16),
        vmem((2, 2, DH, DH), BF16),
        vmem((2, Z, 1, tokens), F32),
        vmem((2, X, 1, tokens), F32),
        dma((4,)),
        dma((4,)),
        dma,
        dma((3,)),
        dma((3,)),
        dma((2, far, 2)),
        dma((2, far, 2)),
        dma((2, 3, 2)),
        dma((2, 3, 2)),
        dma((2, 3, 2)),
        dma((2, 3, 2)),
        dma((Z - 1, 2, 2)),
        dma((Z - 1, 2, 2)),
        dma,
        dma,
        dma((max(Y - 1, 1),)),
        dma((max(Y - 1, 1),)),
        dma((2,)),
        dma((2,)),
        dma((2, max(Y - 1, 1))),
        dma((2, max(Y - 1, 1))),
        dma((2,)),
        dma((2,)),
        dma((2, Z - 1)),
        dma((2, Z - 1)),
        dma((2, X - 1)),
        dma((2, X - 1)),
    ]
    in_vmem = pl.BlockSpec(memory_space=pltpu.VMEM)
    in_hbm = pl.BlockSpec(memory_space=pltpu.HBM)
    shapes = [(rows, tokens)] + [(tokens, width)] * 4
    operands = (queries, keys, values, log_decay.T, gate, norm_gain.reshape(1, width), out_weight, target.T)
    results = pl.pallas_call(
        functools.partial(kernel, chips),
        out_shape=tuple(pltpu.VMEM(shape, BF16) for shape in shapes),
        in_specs=[in_hbm] * 8,
        out_specs=(in_vmem,) * 5,
        scratch_shapes=scratch,
        compiler_params=pltpu.CompilerParams(
            collective_id=0, has_side_effects=True, vmem_limit_bytes=48 * 1024 * 1024
        ),
        cost_estimate=pl.CostEstimate(flops=2 * 10**9, bytes_accessed=8 * 10**6, transcendentals=10**6),
        name="attention_layer",
    )(*[pltpu.with_memory_space_constraint(operand, pltpu.HBM) for operand in operands])
    output, *grads = pl.pallas_call(
        store,
        out_shape=tuple(jax.ShapeDtypeStruct(shape, BF16) for shape in shapes),
        in_specs=[in_vmem] * 5,
        out_specs=(in_hbm,) * 5,
        scratch_shapes=[dma((5,))],
        name="store",
    )(*results)
    return (output.T, *grads)


def solution(mesh):
    chips = (mesh.shape["ctx"] // 2, mesh.shape["tp"] // X)
    return jax.shard_map(
        functools.partial(on_device, chips),
        mesh=mesh,
        in_specs=(
            P("ctx", "tp"),
            P("ctx", "tp"),
            P("ctx", "tp"),
            P("ctx", "tp"),
            P("ctx", "tp"),
            P("tp"),
            P("tp", None),
            P("ctx", "tp"),
        ),
        out_specs=(P("ctx", "tp"),) * 5,
        check_vma=False,
    )
```

```python
import functools

import jax
import jax.numpy as jnp
from jax import lax
from jax.experimental import pallas as pl
from jax.experimental.pallas import tpu as pltpu
from jax.sharding import PartitionSpec as P

DH = 128
EPS = 1e-06
MESH = pl.DeviceIdType.MESH
F32 = jnp.float32
BF16 = jnp.bfloat16
X = 4


def nn(a, b):
    return lax.dot_general(a, b, (((1,), (0,)), ((), ())), preferred_element_type=F32)


def nt(a, b):
    return lax.dot_general(a, b, (((1,), (1,)), ((), ())), preferred_element_type=F32)


def tn(a, b):
    return lax.dot_general(a, b, (((0,), (0,)), ((), ())), preferred_element_type=F32)


def identity(size):
    row = lax.broadcasted_iota(jnp.int32, (size, size), 0)
    column = lax.broadcasted_iota(jnp.int32, (size, size), 1)
    return jnp.where(row == column, 1.0, 0.0).astype(BF16)


def as_row(column):
    return jnp.broadcast_to(column, (column.shape[0], 128)).T[0:1, :]


def as_columns(row):
    return jnp.broadcast_to(row, (128, row.shape[1])).T


def kernel(
    sizes,
    q_in,
    k_in,
    v_in,
    ld_in,
    gate_in,
    gain_in,
    w_ref,
    target_in,
    out_ref,
    qg_ref,
    kg_ref,
    vg_ref,
    gg_ref,
    q_ref,
    k_ref,
    v_ref,
    ld_ref,
    gate_ref,
    gain_ref,
    target_ref,
    in_sems,
    wb,
    wrelay,
    uall,
    yacc,
    ystage,
    yrecv,
    gx,
    gall,
    fstage,
    frecv,
    weight,
    probs,
    kdec,
    att,
    klocal,
    vlocal,
    agrad,
    until_end,
    from_start,
    qdec,
    scale,
    closed,
    bown,
    bsib,
    bchip,
    s_out,
    s_in,
    s_keep,
    t_out,
    t_in,
    c_acc,
    d_acc,
    c_out,
    state,
    small_z,
    small_x,
    w_send,
    w_recv,
    w_own,
    ws_send,
    ws_recv,
    u_send,
    u_recv,
    y_send,
    y_recv,
    g_send,
    g_recv,
    f_send,
    f_recv,
    b_send,
    b_recv,
    bc_send,
    bc_recv,
    s_send,
    s_recv,
    t_send,
    t_recv,
    c_send,
    c_recv,
    sz_send,
    sz_recv,
    sx_send,
    sx_recv,
):
    Y, Z = sizes
    tokens = q_ref.shape[0]
    half_tokens = tokens // 2
    rows = w_ref.shape[0]
    half = rows // 2
    width = q_ref.shape[1]
    total_features = w_ref.shape[1]
    heads = width // DH

    ctx = lax.axis_index("ctx")
    tp = lax.axis_index("tp")
    core = lax.rem(ctx, 2)
    y = lax.div(ctx, 2)
    x = lax.rem(tp, X)
    z = lax.div(tp, X)
    sibling = (y * 2 + 1 - core, tp)
    is_zero = core == 0

    def xs(step):
        return lax.rem(x + step + X, X)

    def zs(step):
        return lax.rem(z + step + 2 * Z, Z)

    def at_x(step):
        return (ctx, z * X + xs(step))

    def at_z(step):
        return (ctx, zs(step) * X + x)

    def at_y(place):
        return (place * 2 + core, tp)

    sign = 1 - 2 * core
    left, right, opp = xs(-1), xs(1), xs(2)

    def send(src, dst, send_sem, recv_sem, device):
        copy = pltpu.make_async_remote_copy(
            src_ref=src,
            dst_ref=dst,
            send_sem=send_sem,
            recv_sem=recv_sem,
            device_id=device,
            device_id_type=MESH,
        )
        copy.start()

    def arrived(ref, sem):
        pltpu.make_async_copy(ref, ref, sem).wait()

    loads = [
        pltpu.make_async_copy(src, dst, in_sems.at[index])
        for index, (src, dst) in enumerate(
            (
                (ld_in, ld_ref),
                (k_in, k_ref),
                (v_in, v_ref),
                (q_in, q_ref),
                (gate_in, gate_ref),
                (gain_in, gain_ref),
                (target_in, target_ref),
            )
        )
    ]
    for load in loads:
        load.start()
    barrier = pltpu.get_barrier_semaphore()
    partners = [sibling] + [at_x(step) for step in range(1, X)]
    partners += [at_z(step) for step in range(1, Z)]
    partners += [at_y(lax.rem(y + step, Y)) for step in range(1, Y)]
    for partner in partners:
        pl.semaphore_signal(barrier, inc=1, device_id=partner, device_id_type=MESH)

    def w_columns(block, x_to):
        start = pl.multiple_of((block * X + x_to) * width, width)
        return pl.ds(start, width)

    my_rows = pl.ds(pl.multiple_of(core * half, half), half)
    x_far = xs(sign)

    def w_far(block, carry):
        send(w_ref.at[my_rows, w_columns(block, opp)], wrelay.at[block], w_send.at[0], w_recv.at[0], (ctx, z * X + x_far))
        return carry

    def w_near(block, carry):
        send(w_ref.at[my_rows, w_columns(block, right)], wb.at[block, x, core], w_send.at[1], w_recv.at[1], at_x(1))
        send(w_ref.at[my_rows, w_columns(block, left)], wb.at[block, x, core], w_send.at[2], w_recv.at[2], at_x(-1))
        return carry

    def w_mine(block, carry):
        for part in range(2):
            pltpu.make_async_copy(
                w_ref.at[pl.ds(part * half, half), w_columns(block, x)], wb.at[block, x, part], w_own
            ).start()
        return carry

    row = lax.broadcasted_iota(jnp.int32, (tokens, tokens), 0)
    column = lax.broadcasted_iota(jnp.int32, (tokens, tokens), 1)
    causal = row >= column
    loads[0].wait()
    upto = jnp.where(row <= column, 1.0, 0.0).astype(BF16)
    rest = ld_ref[...]
    cum = jnp.zeros_like(rest)
    for _ in range(3):
        piece = rest.astype(BF16)
        cum = cum + nn(piece, upto)
        rest = rest - piece.astype(F32)
    cum_rows = [cum[h : h + 1, :] for h in range(heads)]
    cums = [as_columns(c) for c in cum_rows]
    totals = [c[tokens - 1 : tokens, :] for c in cums]
    bown[...] = jnp.zeros_like(bown)
    for h in range(heads):
        bown[h : h + 1, :] = totals[h]
    loads[1].wait()
    loads[2].wait()

    def lanes(h):
        return slice(h * DH, (h + 1) * DH)

    own = []
    for h in range(heads):
        until_end[h] = jnp.exp(totals[h] - cums[h])
        decayed = (k_ref[:, lanes(h)].astype(F32) * until_end[h]).astype(BF16)
        kdec[:, lanes(h)] = decayed
        own.append(tn(decayed, v_ref[:, lanes(h)]))

    def of_core(pair):
        return jnp.where(is_zero, pair[0], pair[1])

    def scan_give(turn, h, value):
        @pl.when(core == h)
        def _():
            s_keep[turn] = value

        @pl.when(core != h)
        def _():
            s_out[turn] = value.astype(BF16)
            send(s_out.at[turn], s_in.at[turn], s_send.at[turn], s_recv.at[turn], sibling)

    def scan_way(turn):
        step = 1 if turn == 0 else -1
        first_here = is_zero if turn == 0 else jnp.logical_not(is_zero)
        return step, first_here

    def decays(ref):
        return of_core((ref[0:1, :], ref[1:2, :]))

    def reaches(place):
        return jnp.logical_and(place >= 0, place < Y)

    def scan_send(turn):
        step, first_here = scan_way(turn)
        arrived(s_in.at[turn], s_recv.at[turn])
        mine = s_keep[turn]
        theirs = s_in[turn].astype(F32)
        first = jnp.where(first_here, mine, theirs)
        second = jnp.where(first_here, theirs, mine)
        s_keep[turn] = first
        b_second = jnp.where(first_here, decays(bsib), decays(bown))
        t_out[turn] = (jnp.exp(b_second) * first + second).astype(BF16)
        for distance in range(1, Y):
            place = y + step * distance

            @pl.when(reaches(place))
            def _():
                send(
                    t_out.at[turn],
                    t_in.at[turn, distance - 1],
                    t_send.at[turn, distance - 1],
                    t_recv.at[turn, distance - 1],
                    at_y(place),
                )

    def scan_end(turn):
        step, first_here = scan_way(turn)
        c_acc[...] = jnp.zeros_like(c_acc)
        d_acc[...] = jnp.zeros_like(d_acc)
        for distance in range(1, Y):
            place = y - step * distance

            @pl.when(reaches(place))
            def _():
                slot = t_in.at[turn, distance - 1]
                arrived(slot, t_recv.at[turn, distance - 1])
                between = d_acc[0:1, :]
                c_acc[...] += jnp.exp(between) * slot[...].astype(F32)
                d_acc[0:1, :] = between + decays(bchip.at[place])

        b_first = jnp.where(first_here, decays(bown), decays(bsib))
        carried = c_acc[...]
        after = jnp.exp(b_first) * carried + s_keep[turn]
        state[turn, core] = jnp.where(first_here, carried, after).astype(BF16)
        c_out[turn] = jnp.where(first_here, after, carried).astype(BF16)
        send(c_out.at[turn], state.at[turn, core], c_send.at[turn], c_recv.at[turn], sibling)

    def scan_take(turn):
        arrived(state.at[turn, 1 - core], c_recv.at[turn])

    pl.semaphore_wait(barrier, len(partners))
    send(bown, bsib, b_send, b_recv, sibling)
    for h in range(heads):
        scan_give(0, h, own[h])
    lax.fori_loop(0, Z, w_far, 0)
    lax.fori_loop(0, Z, w_near, 0)
    lax.fori_loop(0, Z, w_mine, 0)

    arrived(bsib, b_recv)
    bchip[y] = bown[...] + bsib[...]
    for distance in range(1, Y):
        place = lax.rem(y + distance, Y)
        send(bchip.at[y], bchip.at[y], bc_send.at[distance - 1], bc_recv.at[distance - 1], at_y(place))
    scan_send(0)

    for load in loads[3:]:
        load.wait()
    for h in range(heads):
        gaps = cums[h][:, 0:1] - cum_rows[h]
        decay = jnp.where(causal, jnp.exp(jnp.minimum(gaps, 0.0)), 0.0)
        weight[h] = decay
        probs[h] = (nt(q_ref[:, lanes(h)], k_ref[:, lanes(h)]) * decay).astype(BF16)
        att[:, lanes(h)] = nn(probs[h], v_ref[:, lanes(h)])
        from_start[h] = jnp.exp(cums[h])
        qdec[:, lanes(h)] = (q_ref[:, lanes(h)].astype(F32) * from_start[h]).astype(BF16)
        gate_open = jax.nn.sigmoid(gate_ref[:, lanes(h)].astype(F32))
        scale[:, lanes(h)] = gain_ref[:, lanes(h)] * gate_open
        closed[:, lanes(h)] = 1.0 - gate_open

    for distance in range(1, Y):
        arrived(bchip.at[lax.rem(y - distance + Y, Y)], bc_recv.at[distance - 1])

    arrived(wrelay, w_recv.at[0])
    send(wrelay, wb.at[:, xs(-sign), core], w_send.at[3], w_recv.at[3], (ctx, z * X + x_far))

    scan_end(0)
    scan_take(0)

    far, near = Z // 2, Z - 1 - Z // 2
    hops = (far, near)
    ways = (sign, -sign)

    def u_part(way, step, part):
        return uall.at[zs(-ways[way] * step), part]

    def u_start(way, step, part):
        ref = u_part(way, step, part)
        send(ref, ref, u_send.at[way, step, part], u_recv.at[way, step, part], at_z(ways[way]))

    for part in range(2):
        span = slice(part * half_tokens, (part + 1) * half_tokens)
        for h in range(heads):
            from_state = nn(q_ref[span, lanes(h)], state[0, h]) * from_start[h, span, :]
            attended = att[span, lanes(h)] + from_state
            att[span, lanes(h)] = attended
            uall[z, part, :, lanes(h)] = (attended * scale[span, lanes(h)]).astype(BF16)
        for way in range(2):
            if hops[way] > 0:
                u_start(way, 0, part)

    def small_share(turn, value):
        small_z[turn, 0] = value
        for step in range(1, Z):
            send(small_z.at[turn, 0], small_z.at[turn, step], sz_send.at[turn, step - 1], sz_recv.at[turn, step - 1], at_z(step))

    def small_cross(turn):
        for step in range(1, Z):
            arrived(small_z.at[turn, step], sz_recv.at[turn, step - 1])
        sum_z = small_z[turn, 0]
        for step in range(1, Z):
            sum_z = sum_z + small_z[turn, step]
        small_x[turn, 0] = sum_z
        for step in range(1, X):
            send(small_x.at[turn, 0], small_x.at[turn, step], sx_send.at[turn, step - 1], sx_recv.at[turn, step - 1], at_x(step))

    def small_sum(turn):
        for step in range(1, X):
            arrived(small_x.at[turn, step], sx_recv.at[turn, step - 1])
        sum_x = small_x[turn, 0]
        for step in range(1, X):
            sum_x = sum_x + small_x[turn, step]
        return sum_x

    squares = jnp.zeros((tokens, 1), F32)
    for h in range(heads):
        attended = att[:, lanes(h)]
        squares = squares + jnp.sum(attended * attended, axis=1, keepdims=True)
    small_share(0, as_row(squares))

    def w_pair(source, sem, slot):
        ref = wb.at[:, source, core]
        arrived(ref, sem)
        send(ref, ref, ws_send.at[slot], ws_recv.at[slot], sibling)

    def w_block(block):
        return wb[block].reshape(X * rows, width)

    def accumulate(block, part):
        yacc[part] += nt(w_block(block), uall[block, part]).reshape(yacc.shape[1:])

    def u_pass(step, part):
        for way in range(2):
            if step < hops[way]:
                arrived(u_part(way, step + 1, part), u_recv.at[way, step, part])
                if step + 1 < hops[way]:
                    u_start(way, step + 1, part)

    def absorb(step):
        for way in range(2):
            if step < hops[way]:
                for part in range(2):
                    accumulate(zs(-ways[way] * (step + 1)), part)

    def w_first():
        w_pair(left, w_recv.at[1], 0)
        w_pair(right, w_recv.at[2], 1)

    def w_second():
        small_cross(0)
        w_pair(opp, w_recv.at[3], 2)

    def w_third():
        for part in range(2):
            arrived(wb.at[:, x, part], w_own)
        for slot, source in enumerate((left, right, opp)):
            arrived(wb.at[:, source, 1 - core], ws_recv.at[slot])
        for part in range(2):
            yacc[part] = nt(w_block(z), uall[z, part]).reshape(yacc.shape[1:])

    stages = [w_first, w_second, w_third]
    ready = 0
    for step in range(far - 1):
        for part in range(2):
            u_pass(step, part)
        if step < len(stages) - 1:
            stages[step]()
        if step == len(stages) - 2 or step == far - 2:
            for stage in stages[min(step, len(stages) - 2) + 1 :]:
                stage()
            stages = []
        if not stages:
            while ready <= step:
                absorb(ready)
                ready += 1
    for stage in stages:
        stage()

    steps = (2, 1, 3)

    def y_start(part, step):
        ystage[part, step - 1] = yacc[part, xs(step)].astype(BF16)
        send(
            ystage.at[part, step - 1],
            yrecv.at[part, step - 1],
            y_send.at[part, step - 1],
            y_recv.at[part, step - 1],
            at_x(step),
        )

    def y_arrived(part, step):
        arrived(yrecv.at[part, step - 1], y_recv.at[part, step - 1])
        return yrecv[part, step - 1].astype(F32)

    for part in range(2):
        u_pass(far - 1, part)
        last = zs(sign * far)
        last_u = uall[last, part]

        def finish(rows_of):
            block = wb[last, rows_of].reshape(rows, width)
            yacc[part, rows_of] += nt(block, last_u)

        for step in steps:
            finish(xs(step))
            y_start(part, step)
        finish(x)

    inv_rms = lax.rsqrt(small_sum(0) / total_features + EPS)

    def g_arrived(part, step):
        arrived(gx.at[part, xs(-step)], g_recv.at[part, step - 1])

    products = []
    for part in range(2):
        span = slice(part * half_tokens, (part + 1) * half_tokens)
        total = yacc[part, x]
        for step in (1, 3, 2):
            total = total + y_arrived(part, step)
        rounded = (total * inv_rms[:, span]).astype(BF16)
        grad = (rounded.astype(F32) - target_ref[:, span].astype(F32)).astype(BF16)
        gx[part, x] = grad
        for step in steps:
            ref = gx.at[part, x]
            send(ref, ref, g_send.at[part, step - 1], g_recv.at[part, step - 1], at_x(step))
        out_ref[:, span] = rounded
        products.append(jnp.sum(grad.astype(F32) * total, axis=0, keepdims=True))
    small_share(1, jnp.concatenate(products, axis=1))

    eye = identity(half_tokens)

    def feature_part(block, part):
        return nn(gall[part], w_block(block))

    def f_slot(way, step):
        return way * far + step

    def f_start(way, step, part, h, value):
        slot = f_slot(way, step)
        fstage[slot, part, h] = value.astype(BF16)
        send(
            fstage.at[slot, part, h],
            frecv.at[slot, part, h],
            f_send.at[slot, part, h],
            f_recv.at[slot, part, h],
            at_z(ways[way]),
        )

    def f_arrived(way, step, part, h):
        slot = f_slot(way, step)
        arrived(frecv.at[slot, part, h], f_recv.at[slot, part, h])
        return frecv[slot, part, h].astype(F32)

    for step in range(far):
        for part in range(2):
            if step == 0:
                for x_step in (1, 3, 2):
                    g_arrived(part, x_step)
                gall[part] = nt(eye, gx[part].reshape(X * rows, half_tokens)).astype(BF16)
            sums = [
                feature_part(zs(ways[way] * (hops[way] - step)), part) if step < hops[way] else None
                for way in range(2)
            ]
            for h in range(heads):
                for way in range(2):
                    if step < hops[way]:
                        value = sums[way][:, lanes(h)]
                        if step > 0:
                            value = value + f_arrived(way, step - 1, part, h)
                        f_start(way, step, part, h, value)
        if step == 0:
            small_cross(1)

    own_feature = [feature_part(z, part) for part in range(2)]
    mean_product = as_columns(small_sum(1) / total_features)
    inv = as_columns(inv_rms)

    for h in range(heads):
        pieces = []
        for part in range(2):
            value = own_feature[part][:, lanes(h)]
            for way in range(2):
                if hops[way] > 0:
                    value = value + f_arrived(way, hops[way] - 1, part, h)
            pieces.append(value)
        attended = att[:, lanes(h)]
        normed_grad = jnp.concatenate(pieces, axis=0) * scale[:, lanes(h)]
        grad = (inv * normed_grad - inv * inv * inv * attended * mean_product).astype(BF16)
        agrad[:, lanes(h)] = grad
        scan_give(1, h, tn(qdec[:, lanes(h)], grad))
        gg_ref[:, lanes(h)] = (normed_grad * attended * inv * closed[:, lanes(h)]).astype(BF16)

    for h in range(heads):
        grad = agrad[:, lanes(h)]
        score_grad = (nt(grad, v_ref[:, lanes(h)]) * weight[h]).astype(BF16)
        if h == 0:
            scan_send(1)
        qg_ref[:, lanes(h)] = (
            nn(score_grad, k_ref[:, lanes(h)]) + from_start[h] * nt(grad, state[0, h])
        ).astype(BF16)
        klocal[:, lanes(h)] = tn(score_grad, q_ref[:, lanes(h)])
        vlocal[:, lanes(h)] = tn(probs[h], grad)
    for index in range(4):
        arrived(wrelay, w_send.at[index])
    for index in range(3):
        arrived(wrelay, ws_send.at[index])
    for way in range(2):
        for step in range(hops[way]):
            for part in range(2):
                arrived(u_part(way, step, part), u_send.at[way, step, part])
                slot = f_slot(way, step)
                for h in range(heads):
                    arrived(fstage.at[slot, part, h], f_send.at[slot, part, h])
    for part in range(2):
        for slot in range(X - 1):
            arrived(ystage.at[part, slot], y_send.at[part, slot])
            arrived(ystage.at[part, slot], g_send.at[part, slot])
    arrived(bown, b_send)
    for distance in range(1, Y):
        arrived(bown, bc_send.at[distance - 1])
    for turn in range(2):
        arrived(s_out.at[turn], s_send.at[turn])
        for distance in range(1, Z):
            arrived(small_z.at[turn, 0], sz_send.at[turn, distance - 1])
        for distance in range(1, X):
            arrived(small_x.at[turn, 0], sx_send.at[turn, distance - 1])

    def scan_sent(turn):
        arrived(c_out.at[turn], c_send.at[turn])
        step, _ = scan_way(turn)
        for distance in range(1, Y):

            @pl.when(reaches(y + step * distance))
            def _():
                arrived(t_out.at[turn], t_send.at[turn, distance - 1])

    scan_sent(0)

    scan_end(1)
    scan_take(1)
    for h in range(heads):
        later = state[1, h]
        kg_ref[:, lanes(h)] = (
            klocal[:, lanes(h)] + until_end[h] * nt(v_ref[:, lanes(h)], later)
        ).astype(BF16)
        vg_ref[:, lanes(h)] = (vlocal[:, lanes(h)] + nn(kdec[:, lanes(h)], later)).astype(BF16)

    scan_sent(1)


def store(*refs):
    *refs, sems = refs
    count = len(refs) // 2
    copies = [pltpu.make_async_copy(refs[i], refs[count + i], sems.at[i]) for i in range(count)]
    for copy in copies:
        copy.start()
    for copy in copies:
        copy.wait()


def on_device(chips, queries, keys, values, log_decay, gate, norm_gain, out_weight, target):
    Y, Z = chips
    tokens, width = queries.shape
    rows, features = out_weight.shape
    half = rows // 2
    far = Z // 2
    vmem = pltpu.VMEM
    dma = pltpu.SemaphoreType.DMA
    scratch = [
        vmem((tokens, width), BF16),
        vmem((tokens, width), BF16),
        vmem((tokens, width), BF16),
        vmem((width // DH, tokens), F32),
        vmem((tokens, width), BF16),
        vmem((1, width), F32),
        vmem((rows, tokens), BF16),
        dma((7,)),
        vmem((Z, X, 2, half, width), BF16),
        vmem((Z, half, width), BF16),
        vmem((Z, 2, tokens // 2, width), BF16),
        vmem((2, X, rows, tokens // 2), F32),
        vmem((2, X - 1, rows, tokens // 2), BF16),
        vmem((2, X - 1, rows, tokens // 2), BF16),
        vmem((2, X, rows, tokens // 2), BF16),
        vmem((2, tokens // 2, X * rows), BF16),
        vmem((Z - 1, 2, 2, tokens // 2, DH), BF16),
        vmem((Z - 1, 2, 2, tokens // 2, DH), BF16),
        vmem((width // DH, tokens, tokens), F32),
        vmem((width // DH, tokens, tokens), BF16),
        vmem((tokens, width), BF16),
        vmem((tokens, width), F32),
        vmem((tokens, width), F32),
        vmem((tokens, width), F32),
        vmem((tokens, width), BF16),
        vmem((width // DH, tokens, DH), F32),
        vmem((width // DH, tokens, DH), F32),
        vmem((tokens, width), BF16),
        vmem((tokens, width), F32),
        vmem((tokens, width), F32),
        vmem((8, 128), F32),
        vmem((8, 128), F32),
        vmem((Y, 8, 128), F32),
        vmem((2, DH, DH), BF16),
        vmem((2, DH, DH), BF16),
        vmem((2, DH, DH), F32),
        vmem((2, DH, DH), BF16),
        vmem((2, max(Y - 1, 1), DH, DH), BF16),
        vmem((DH, DH), F32),
        vmem((8, 128), F32),
        vmem((2, DH, DH), BF16),
        vmem((2, 2, DH, DH), BF16),
        vmem((2, Z, 1, tokens), F32),
        vmem((2, X, 1, tokens), F32),
        dma((4,)),
        dma((4,)),
        dma,
        dma((3,)),
        dma((3,)),
        dma((2, far, 2)),
        dma((2, far, 2)),
        dma((2, X - 1)),
        dma((2, X - 1)),
        dma((2, X - 1)),
        dma((2, X - 1)),
        dma((Z - 1, 2, 2)),
        dma((Z - 1, 2, 2)),
        dma,
        dma,
        dma((max(Y - 1, 1),)),
        dma((max(Y - 1, 1),)),
        dma((2,)),
        dma((2,)),
        dma((2, max(Y - 1, 1))),
        dma((2, max(Y - 1, 1))),
        dma((2,)),
        dma((2,)),
        dma((2, Z - 1)),
        dma((2, Z - 1)),
        dma((2, X - 1)),
        dma((2, X - 1)),
    ]
    in_vmem = pl.BlockSpec(memory_space=pltpu.VMEM)
    in_hbm = pl.BlockSpec(memory_space=pltpu.HBM)
    shapes = [(rows, tokens)] + [(tokens, width)] * 4
    operands = (queries, keys, values, log_decay.T, gate, norm_gain.reshape(1, width), out_weight, target.T)
    results = pl.pallas_call(
        functools.partial(kernel, chips),
        out_shape=tuple(pltpu.VMEM(shape, BF16) for shape in shapes),
        in_specs=[in_hbm] * 8,
        out_specs=(in_vmem,) * 5,
        scratch_shapes=scratch,
        compiler_params=pltpu.CompilerParams(
            collective_id=0, has_side_effects=True, vmem_limit_bytes=48 * 1024 * 1024
        ),
        cost_estimate=pl.CostEstimate(flops=2 * 10**9, bytes_accessed=8 * 10**6, transcendentals=10**6),
        name="attention_layer",
    )(*[pltpu.with_memory_space_constraint(operand, pltpu.HBM) for operand in operands])
    output, *grads = pl.pallas_call(
        store,
        out_shape=tuple(jax.ShapeDtypeStruct(shape, BF16) for shape in shapes),
        in_specs=[in_vmem] * 5,
        out_specs=(in_hbm,) * 5,
        scratch_shapes=[dma((5,))],
        compiler_params=pltpu.CompilerParams(vmem_limit_bytes=4 * 1024 * 1024),
        name="store",
    )(*results)
    return (output.T, *grads)


def solution(mesh):
    chips = (mesh.shape["ctx"] // 2, mesh.shape["tp"] // X)
    return jax.shard_map(
        functools.partial(on_device, chips),
        mesh=mesh,
        in_specs=(
            P("ctx", "tp"),
            P("ctx", "tp"),
            P("ctx", "tp"),
            P("ctx", "tp"),
            P("ctx", "tp"),
            P("tp"),
            P("tp", None),
            P("ctx", "tp"),
        ),
        out_specs=(P("ctx", "tp"),) * 5,
        check_vma=False,
    )
```

```python
import functools

import jax
import jax.numpy as jnp
from jax import lax
from jax.experimental import pallas as pl
from jax.experimental.pallas import tpu as pltpu
from jax.sharding import PartitionSpec as P

DH = 128
EPS = 1e-06
MESH = pl.DeviceIdType.MESH
F32 = jnp.float32
BF16 = jnp.bfloat16
X = 4


def nn(a, b):
    return lax.dot_general(a, b, (((1,), (0,)), ((), ())), preferred_element_type=F32)


def nt(a, b):
    return lax.dot_general(a, b, (((1,), (1,)), ((), ())), preferred_element_type=F32)


def tn(a, b):
    return lax.dot_general(a, b, (((0,), (0,)), ((), ())), preferred_element_type=F32)


def identity(size):
    row = lax.broadcasted_iota(jnp.int32, (size, size), 0)
    column = lax.broadcasted_iota(jnp.int32, (size, size), 1)
    return jnp.where(row == column, 1.0, 0.0).astype(BF16)


def as_row(column):
    return jnp.broadcast_to(column, (column.shape[0], 128)).T[0:1, :]


def as_columns(row):
    return jnp.broadcast_to(row, (128, row.shape[1])).T


def kernel(
    sizes,
    q_in,
    k_in,
    v_in,
    ld_in,
    gate_in,
    gain_in,
    w_ref,
    target_in,
    out_ref,
    qg_ref,
    kg_ref,
    vg_ref,
    gg_ref,
    q_ref,
    k_ref,
    v_ref,
    ld_ref,
    gate_ref,
    gain_ref,
    target_ref,
    in_sems,
    wb,
    wrelay,
    uall,
    yacc,
    ystage,
    yrecv,
    gx,
    gall,
    fstage,
    frecv,
    weight,
    probs,
    kdec,
    att,
    klocal,
    vlocal,
    agrad,
    until_end,
    from_start,
    qdec,
    scale,
    closed,
    bown,
    bsib,
    bchip,
    s_out,
    s_in,
    s_keep,
    t_out,
    t_in,
    c_acc,
    d_acc,
    c_out,
    state,
    small_z,
    small_x,
    w_send,
    w_recv,
    w_own,
    ws_send,
    ws_recv,
    u_send,
    u_recv,
    y_send,
    y_recv,
    g_send,
    g_recv,
    f_send,
    f_recv,
    b_send,
    b_recv,
    bc_send,
    bc_recv,
    s_send,
    s_recv,
    t_send,
    t_recv,
    c_send,
    c_recv,
    sz_send,
    sz_recv,
    sx_send,
    sx_recv,
):
    Y, Z = sizes
    tokens = q_ref.shape[0]
    half_tokens = tokens // 2
    rows = w_ref.shape[0]
    half = rows // 2
    width = q_ref.shape[1]
    total_features = w_ref.shape[1]
    heads = width // DH

    ctx = lax.axis_index("ctx")
    tp = lax.axis_index("tp")
    core = lax.rem(ctx, 2)
    y = lax.div(ctx, 2)
    x = lax.rem(tp, X)
    z = lax.div(tp, X)
    sibling = (y * 2 + 1 - core, tp)
    is_zero = core == 0

    def xs(step):
        return lax.rem(x + step + X, X)

    def zs(step):
        return lax.rem(z + step + 2 * Z, Z)

    def at_x(step):
        return (ctx, z * X + xs(step))

    def at_z(step):
        return (ctx, zs(step) * X + x)

    def at_y(place):
        return (place * 2 + core, tp)

    sign = 1 - 2 * core
    left, right, opp = xs(-1), xs(1), xs(2)

    def send(src, dst, send_sem, recv_sem, device):
        copy = pltpu.make_async_remote_copy(
            src_ref=src,
            dst_ref=dst,
            send_sem=send_sem,
            recv_sem=recv_sem,
            device_id=device,
            device_id_type=MESH,
        )
        copy.start()

    def arrived(ref, sem):
        pltpu.make_async_copy(ref, ref, sem).wait()

    loads = [
        pltpu.make_async_copy(src, dst, in_sems.at[index])
        for index, (src, dst) in enumerate(
            (
                (ld_in, ld_ref),
                (k_in, k_ref),
                (v_in, v_ref),
                (q_in, q_ref),
                (gate_in, gate_ref),
                (gain_in, gain_ref),
                (target_in, target_ref),
            )
        )
    ]
    for load in loads:
        load.start()
    barrier = pltpu.get_barrier_semaphore()
    partners = [sibling] + [at_x(step) for step in range(1, X)]
    partners += [at_z(step) for step in range(1, Z)]
    partners += [at_y(lax.rem(y + step, Y)) for step in range(1, Y)]
    for partner in partners:
        pl.semaphore_signal(barrier, inc=1, device_id=partner, device_id_type=MESH)

    def w_columns(block, x_to):
        start = pl.multiple_of((block * X + x_to) * width, width)
        return pl.ds(start, width)

    my_rows = pl.ds(pl.multiple_of(core * half, half), half)
    x_far = xs(sign)

    def w_far(block, carry):
        send(w_ref.at[my_rows, w_columns(block, opp)], wrelay.at[block], w_send.at[0], w_recv.at[0], (ctx, z * X + x_far))
        return carry

    def w_near(block, carry):
        send(w_ref.at[my_rows, w_columns(block, right)], wb.at[block, x, core], w_send.at[1], w_recv.at[1], at_x(1))
        send(w_ref.at[my_rows, w_columns(block, left)], wb.at[block, x, core], w_send.at[2], w_recv.at[2], at_x(-1))
        return carry

    def w_mine(block, carry):
        for part in range(2):
            pltpu.make_async_copy(
                w_ref.at[pl.ds(part * half, half), w_columns(block, x)], wb.at[block, x, part], w_own
            ).start()
        return carry

    row = lax.broadcasted_iota(jnp.int32, (tokens, tokens), 0)
    column = lax.broadcasted_iota(jnp.int32, (tokens, tokens), 1)
    causal = row >= column
    loads[0].wait()
    upto = jnp.where(row <= column, 1.0, 0.0).astype(BF16)
    rest = ld_ref[...]
    cum = jnp.zeros_like(rest)
    for _ in range(3):
        piece = rest.astype(BF16)
        cum = cum + nn(piece, upto)
        rest = rest - piece.astype(F32)
    cum_rows = [cum[h : h + 1, :] for h in range(heads)]
    cums = [as_columns(c) for c in cum_rows]
    totals = [c[tokens - 1 : tokens, :] for c in cums]
    bown[...] = jnp.zeros_like(bown)
    for h in range(heads):
        bown[h : h + 1, :] = totals[h]
    loads[1].wait()
    loads[2].wait()

    def lanes(h):
        return slice(h * DH, (h + 1) * DH)

    own = []
    for h in range(heads):
        until_end[h] = jnp.exp(totals[h] - cums[h])
        decayed = (k_ref[:, lanes(h)].astype(F32) * until_end[h]).astype(BF16)
        kdec[:, lanes(h)] = decayed
        own.append(tn(decayed, v_ref[:, lanes(h)]))

    def of_core(pair):
        return jnp.where(is_zero, pair[0], pair[1])

    def scan_give(turn, h, value):
        @pl.when(core == h)
        def _():
            s_keep[turn] = value

        @pl.when(core != h)
        def _():
            s_out[turn] = value.astype(BF16)
            send(s_out.at[turn], s_in.at[turn], s_send.at[turn], s_recv.at[turn], sibling)

    def scan_way(turn):
        step = 1 if turn == 0 else -1
        first_here = is_zero if turn == 0 else jnp.logical_not(is_zero)
        return step, first_here

    def decays(ref):
        return of_core((ref[0:1, :], ref[1:2, :]))

    def reaches(place):
        return jnp.logical_and(place >= 0, place < Y)

    def scan_send(turn):
        step, first_here = scan_way(turn)
        arrived(s_in.at[turn], s_recv.at[turn])
        mine = s_keep[turn]
        theirs = s_in[turn].astype(F32)
        first = jnp.where(first_here, mine, theirs)
        second = jnp.where(first_here, theirs, mine)
        s_keep[turn] = first
        b_second = jnp.where(first_here, decays(bsib), decays(bown))
        t_out[turn] = (jnp.exp(b_second) * first + second).astype(BF16)
        for distance in range(1, Y):
            place = y + step * distance

            @pl.when(reaches(place))
            def _():
                send(
                    t_out.at[turn],
                    t_in.at[turn, distance - 1],
                    t_send.at[turn, distance - 1],
                    t_recv.at[turn, distance - 1],
                    at_y(place),
                )

    def scan_end(turn):
        step, first_here = scan_way(turn)
        c_acc[...] = jnp.zeros_like(c_acc)
        d_acc[...] = jnp.zeros_like(d_acc)
        for distance in range(1, Y):
            place = y - step * distance

            @pl.when(reaches(place))
            def _():
                slot = t_in.at[turn, distance - 1]
                arrived(slot, t_recv.at[turn, distance - 1])
                between = d_acc[0:1, :]
                c_acc[...] += jnp.exp(between) * slot[...].astype(F32)
                d_acc[0:1, :] = between + decays(bchip.at[place])

        b_first = jnp.where(first_here, decays(bown), decays(bsib))
        carried = c_acc[...]
        after = jnp.exp(b_first) * carried + s_keep[turn]
        state[turn, core] = jnp.where(first_here, carried, after).astype(BF16)
        c_out[turn] = jnp.where(first_here, after, carried).astype(BF16)
        send(c_out.at[turn], state.at[turn, core], c_send.at[turn], c_recv.at[turn], sibling)

    def scan_take(turn):
        arrived(state.at[turn, 1 - core], c_recv.at[turn])

    pl.semaphore_wait(barrier, len(partners))
    send(bown, bsib, b_send, b_recv, sibling)
    for h in range(heads):
        scan_give(0, h, own[h])
    lax.fori_loop(0, Z, w_far, 0)
    lax.fori_loop(0, Z, w_near, 0)
    lax.fori_loop(0, Z, w_mine, 0)

    arrived(bsib, b_recv)
    bchip[y] = bown[...] + bsib[...]
    for distance in range(1, Y):
        place = lax.rem(y + distance, Y)
        send(bchip.at[y], bchip.at[y], bc_send.at[distance - 1], bc_recv.at[distance - 1], at_y(place))
    scan_send(0)

    for load in loads[3:]:
        load.wait()
    for h in range(heads):
        gaps = cums[h][:, 0:1] - cum_rows[h]
        decay = jnp.where(causal, jnp.exp(jnp.minimum(gaps, 0.0)), 0.0)
        weight[h] = decay
        probs[h] = (nt(q_ref[:, lanes(h)], k_ref[:, lanes(h)]) * decay).astype(BF16)
        att[:, lanes(h)] = nn(probs[h], v_ref[:, lanes(h)])
        from_start[h] = jnp.exp(cums[h])
        qdec[:, lanes(h)] = (q_ref[:, lanes(h)].astype(F32) * from_start[h]).astype(BF16)
        gate_open = jax.nn.sigmoid(gate_ref[:, lanes(h)].astype(F32))
        scale[:, lanes(h)] = gain_ref[:, lanes(h)] * gate_open
        closed[:, lanes(h)] = 1.0 - gate_open

    for distance in range(1, Y):
        arrived(bchip.at[lax.rem(y - distance + Y, Y)], bc_recv.at[distance - 1])

    arrived(wrelay, w_recv.at[0])
    send(wrelay, wb.at[:, xs(-sign), core], w_send.at[3], w_recv.at[3], (ctx, z * X + x_far))

    scan_end(0)
    scan_take(0)

    far, near = Z // 2, Z - 1 - Z // 2
    hops = (far, near)
    ways = (sign, -sign)

    def u_part(way, step, part, h):
        return uall.at[zs(-ways[way] * step), part, h]

    def u_start(way, step, part, h):
        ref = u_part(way, step, part, h)
        send(ref, ref, u_send.at[way, step, part, h], u_recv.at[way, step, part, h], at_z(ways[way]))

    for part in range(2):
        span = slice(part * half_tokens, (part + 1) * half_tokens)
        for h in range(heads):
            from_state = nn(q_ref[span, lanes(h)], state[0, h]) * from_start[h, span, :]
            attended = att[span, lanes(h)] + from_state
            att[span, lanes(h)] = attended
            uall[z, part, h] = (attended * scale[span, lanes(h)]).astype(BF16)
            for way in range(2):
                if hops[way] > 0:
                    u_start(way, 0, part, h)

    def small_share(turn, value):
        small_z[turn, 0] = value
        for step in range(1, Z):
            send(small_z.at[turn, 0], small_z.at[turn, step], sz_send.at[turn, step - 1], sz_recv.at[turn, step - 1], at_z(step))

    def small_cross(turn):
        for step in range(1, Z):
            arrived(small_z.at[turn, step], sz_recv.at[turn, step - 1])
        sum_z = small_z[turn, 0]
        for step in range(1, Z):
            sum_z = sum_z + small_z[turn, step]
        small_x[turn, 0] = sum_z
        for step in range(1, X):
            send(small_x.at[turn, 0], small_x.at[turn, step], sx_send.at[turn, step - 1], sx_recv.at[turn, step - 1], at_x(step))

    def small_sum(turn):
        for step in range(1, X):
            arrived(small_x.at[turn, step], sx_recv.at[turn, step - 1])
        sum_x = small_x[turn, 0]
        for step in range(1, X):
            sum_x = sum_x + small_x[turn, step]
        return sum_x

    squares = jnp.zeros((tokens, 1), F32)
    for h in range(heads):
        attended = att[:, lanes(h)]
        squares = squares + jnp.sum(attended * attended, axis=1, keepdims=True)
    small_share(0, as_row(squares))

    def w_pair(source, sem, slot):
        ref = wb.at[:, source, core]
        arrived(ref, sem)
        send(ref, ref, ws_send.at[slot], ws_recv.at[slot], sibling)

    def w_block(block):
        return wb[block].reshape(X * rows, width)

    def u_block(block, part):
        return jnp.concatenate([uall[block, part, h] for h in range(heads)], axis=1)

    def accumulate(block, part):
        yacc[part] += nt(w_block(block), u_block(block, part)).reshape(yacc.shape[1:])

    def u_pass(step, part):
        for h in range(heads):
            for way in range(2):
                if step < hops[way]:
                    arrived(u_part(way, step + 1, part, h), u_recv.at[way, step, part, h])
                    if step + 1 < hops[way]:
                        u_start(way, step + 1, part, h)

    def absorb(step):
        for way in range(2):
            if step < hops[way]:
                for part in range(2):
                    accumulate(zs(-ways[way] * (step + 1)), part)

    for step in range(far - 1):
        for part in range(2):
            u_pass(step, part)
        if step == far - 3:
            w_pair(left, w_recv.at[1], 0)
            w_pair(right, w_recv.at[2], 1)
    if far < 3:
        w_pair(left, w_recv.at[1], 0)
        w_pair(right, w_recv.at[2], 1)
    w_pair(opp, w_recv.at[3], 2)
    small_cross(0)
    for part in range(2):
        arrived(wb.at[:, x, part], w_own)
    for slot, source in enumerate((left, right, opp)):
        arrived(wb.at[:, source, 1 - core], ws_recv.at[slot])
    for part in range(2):
        yacc[part] = nt(w_block(z), u_block(z, part)).reshape(yacc.shape[1:])
    for step in range(far - 1):
        absorb(step)

    steps = (2, 1, 3)

    def y_start(part, step):
        ystage[part, step - 1] = yacc[part, xs(step)].astype(BF16)
        send(
            ystage.at[part, step - 1],
            yrecv.at[part, step - 1],
            y_send.at[part, step - 1],
            y_recv.at[part, step - 1],
            at_x(step),
        )

    def y_arrived(part, step):
        arrived(yrecv.at[part, step - 1], y_recv.at[part, step - 1])
        return yrecv[part, step - 1].astype(F32)

    for part in range(2):
        u_pass(far - 1, part)
        last = zs(sign * far)
        last_u = u_block(last, part)

        def finish(rows_of):
            block = wb[last, rows_of].reshape(rows, width)
            yacc[part, rows_of] += nt(block, last_u)

        for step in steps:
            finish(xs(step))
            y_start(part, step)
        finish(x)

    inv_rms = lax.rsqrt(small_sum(0) / total_features + EPS)

    def g_arrived(part, step):
        arrived(gx.at[part, xs(-step)], g_recv.at[part, step - 1])

    products = []
    for part in range(2):
        span = slice(part * half_tokens, (part + 1) * half_tokens)
        total = yacc[part, x]
        for step in (1, 3, 2):
            total = total + y_arrived(part, step)
        rounded = (total * inv_rms[:, span]).astype(BF16)
        grad = (rounded.astype(F32) - target_ref[:, span].astype(F32)).astype(BF16)
        gx[part, x] = grad
        for step in steps:
            ref = gx.at[part, x]
            send(ref, ref, g_send.at[part, step - 1], g_recv.at[part, step - 1], at_x(step))
        out_ref[:, span] = rounded
        products.append(jnp.sum(grad.astype(F32) * total, axis=0, keepdims=True))
    small_share(1, jnp.concatenate(products, axis=1))

    eye = identity(half_tokens)

    def feature_part(block, part):
        return nn(gall[part], w_block(block))

    def f_slot(way, step):
        return way * far + step

    def f_start(way, step, part, h, value):
        slot = f_slot(way, step)
        fstage[slot, part, h] = value.astype(BF16)
        send(
            fstage.at[slot, part, h],
            frecv.at[slot, part, h],
            f_send.at[slot, part, h],
            f_recv.at[slot, part, h],
            at_z(ways[way]),
        )

    def f_arrived(way, step, part, h):
        slot = f_slot(way, step)
        arrived(frecv.at[slot, part, h], f_recv.at[slot, part, h])
        return frecv[slot, part, h].astype(F32)

    for step in range(far):
        for part in range(2):
            if step == 0:
                for x_step in (1, 3, 2):
                    g_arrived(part, x_step)
                gall[part] = nt(eye, gx[part].reshape(X * rows, half_tokens)).astype(BF16)
            sums = [
                feature_part(zs(ways[way] * (hops[way] - step)), part) if step < hops[way] else None
                for way in range(2)
            ]
            for h in range(heads):
                for way in range(2):
                    if step < hops[way]:
                        value = sums[way][:, lanes(h)]
                        if step > 0:
                            value = value + f_arrived(way, step - 1, part, h)
                        f_start(way, step, part, h, value)
        if step == 0:
            small_cross(1)

    own_feature = [feature_part(z, part) for part in range(2)]
    mean_product = as_columns(small_sum(1) / total_features)
    inv = as_columns(inv_rms)

    for h in range(heads):
        pieces = []
        for part in range(2):
            value = own_feature[part][:, lanes(h)]
            for way in range(2):
                if hops[way] > 0:
                    value = value + f_arrived(way, hops[way] - 1, part, h)
            pieces.append(value)
        attended = att[:, lanes(h)]
        normed_grad = jnp.concatenate(pieces, axis=0) * scale[:, lanes(h)]
        grad = (inv * normed_grad - inv * inv * inv * attended * mean_product).astype(BF16)
        agrad[:, lanes(h)] = grad
        scan_give(1, h, tn(qdec[:, lanes(h)], grad))
        gg_ref[:, lanes(h)] = (normed_grad * attended * inv * closed[:, lanes(h)]).astype(BF16)

    for h in range(heads):
        grad = agrad[:, lanes(h)]
        score_grad = (nt(grad, v_ref[:, lanes(h)]) * weight[h]).astype(BF16)
        if h == 0:
            scan_send(1)
        qg_ref[:, lanes(h)] = (
            nn(score_grad, k_ref[:, lanes(h)]) + from_start[h] * nt(grad, state[0, h])
        ).astype(BF16)
        klocal[:, lanes(h)] = tn(score_grad, q_ref[:, lanes(h)])
        vlocal[:, lanes(h)] = tn(probs[h], grad)
    for index in range(4):
        arrived(wrelay, w_send.at[index])
    for index in range(3):
        arrived(wrelay, ws_send.at[index])
    for way in range(2):
        for step in range(hops[way]):
            for part in range(2):
                slot = f_slot(way, step)
                for h in range(heads):
                    arrived(u_part(way, step, part, h), u_send.at[way, step, part, h])
                    arrived(fstage.at[slot, part, h], f_send.at[slot, part, h])
    for part in range(2):
        for slot in range(X - 1):
            arrived(ystage.at[part, slot], y_send.at[part, slot])
            arrived(ystage.at[part, slot], g_send.at[part, slot])
    arrived(bown, b_send)
    for distance in range(1, Y):
        arrived(bown, bc_send.at[distance - 1])
    for turn in range(2):
        arrived(s_out.at[turn], s_send.at[turn])
        for distance in range(1, Z):
            arrived(small_z.at[turn, 0], sz_send.at[turn, distance - 1])
        for distance in range(1, X):
            arrived(small_x.at[turn, 0], sx_send.at[turn, distance - 1])

    def scan_sent(turn):
        arrived(c_out.at[turn], c_send.at[turn])
        step, _ = scan_way(turn)
        for distance in range(1, Y):

            @pl.when(reaches(y + step * distance))
            def _():
                arrived(t_out.at[turn], t_send.at[turn, distance - 1])

    scan_sent(0)

    scan_end(1)
    scan_take(1)
    for h in range(heads):
        later = state[1, h]
        kg_ref[:, lanes(h)] = (
            klocal[:, lanes(h)] + until_end[h] * nt(v_ref[:, lanes(h)], later)
        ).astype(BF16)
        vg_ref[:, lanes(h)] = (vlocal[:, lanes(h)] + nn(kdec[:, lanes(h)], later)).astype(BF16)

    scan_sent(1)


def store(*refs):
    *refs, sems = refs
    count = len(refs) // 2
    copies = [pltpu.make_async_copy(refs[i], refs[count + i], sems.at[i]) for i in range(count)]
    for copy in copies:
        copy.start()
    for copy in copies:
        copy.wait()


def on_device(chips, queries, keys, values, log_decay, gate, norm_gain, out_weight, target):
    Y, Z = chips
    tokens, width = queries.shape
    rows, features = out_weight.shape
    half = rows // 2
    far = Z // 2
    vmem = pltpu.VMEM
    dma = pltpu.SemaphoreType.DMA
    scratch = [
        vmem((tokens, width), BF16),
        vmem((tokens, width), BF16),
        vmem((tokens, width), BF16),
        vmem((width // DH, tokens), F32),
        vmem((tokens, width), BF16),
        vmem((1, width), F32),
        vmem((rows, tokens), BF16),
        dma((7,)),
        vmem((Z, X, 2, half, width), BF16),
        vmem((Z, half, width), BF16),
        vmem((Z, 2, width // DH, tokens // 2, DH), BF16),
        vmem((2, X, rows, tokens // 2), F32),
        vmem((2, X - 1, rows, tokens // 2), BF16),
        vmem((2, X - 1, rows, tokens // 2), BF16),
        vmem((2, X, rows, tokens // 2), BF16),
        vmem((2, tokens // 2, X * rows), BF16),
        vmem((Z - 1, 2, 2, tokens // 2, DH), BF16),
        vmem((Z - 1, 2, 2, tokens // 2, DH), BF16),
        vmem((width // DH, tokens, tokens), F32),
        vmem((width // DH, tokens, tokens), BF16),
        vmem((tokens, width), BF16),
        vmem((tokens, width), F32),
        vmem((tokens, width), F32),
        vmem((tokens, width), F32),
        vmem((tokens, width), BF16),
        vmem((width // DH, tokens, DH), F32),
        vmem((width // DH, tokens, DH), F32),
        vmem((tokens, width), BF16),
        vmem((tokens, width), F32),
        vmem((tokens, width), F32),
        vmem((8, 128), F32),
        vmem((8, 128), F32),
        vmem((Y, 8, 128), F32),
        vmem((2, DH, DH), BF16),
        vmem((2, DH, DH), BF16),
        vmem((2, DH, DH), F32),
        vmem((2, DH, DH), BF16),
        vmem((2, max(Y - 1, 1), DH, DH), BF16),
        vmem((DH, DH), F32),
        vmem((8, 128), F32),
        vmem((2, DH, DH), BF16),
        vmem((2, 2, DH, DH), BF16),
        vmem((2, Z, 1, tokens), F32),
        vmem((2, X, 1, tokens), F32),
        dma((4,)),
        dma((4,)),
        dma,
        dma((3,)),
        dma((3,)),
        dma((2, far, 2, 2)),
        dma((2, far, 2, 2)),
        dma((2, X - 1)),
        dma((2, X - 1)),
        dma((2, X - 1)),
        dma((2, X - 1)),
        dma((Z - 1, 2, 2)),
        dma((Z - 1, 2, 2)),
        dma,
        dma,
        dma((max(Y - 1, 1),)),
        dma((max(Y - 1, 1),)),
        dma((2,)),
        dma((2,)),
        dma((2, max(Y - 1, 1))),
        dma((2, max(Y - 1, 1))),
        dma((2,)),
        dma((2,)),
        dma((2, Z - 1)),
        dma((2, Z - 1)),
        dma((2, X - 1)),
        dma((2, X - 1)),
    ]
    in_vmem = pl.BlockSpec(memory_space=pltpu.VMEM)
    in_hbm = pl.BlockSpec(memory_space=pltpu.HBM)
    shapes = [(rows, tokens)] + [(tokens, width)] * 4
    operands = (queries, keys, values, log_decay.T, gate, norm_gain.reshape(1, width), out_weight, target.T)
    results = pl.pallas_call(
        functools.partial(kernel, chips),
        out_shape=tuple(pltpu.VMEM(shape, BF16) for shape in shapes),
        in_specs=[in_hbm] * 8,
        out_specs=(in_vmem,) * 5,
        scratch_shapes=scratch,
        compiler_params=pltpu.CompilerParams(
            collective_id=0, has_side_effects=True, vmem_limit_bytes=48 * 1024 * 1024
        ),
        cost_estimate=pl.CostEstimate(flops=2 * 10**9, bytes_accessed=8 * 10**6, transcendentals=10**6),
        name="attention_layer",
    )(*[pltpu.with_memory_space_constraint(operand, pltpu.HBM) for operand in operands])
    output, *grads = pl.pallas_call(
        store,
        out_shape=tuple(jax.ShapeDtypeStruct(shape, BF16) for shape in shapes),
        in_specs=[in_vmem] * 5,
        out_specs=(in_hbm,) * 5,
        scratch_shapes=[dma((5,))],
        compiler_params=pltpu.CompilerParams(vmem_limit_bytes=4 * 1024 * 1024),
        name="store",
    )(*results)
    return (output.T, *grads)


def solution(mesh):
    chips = (mesh.shape["ctx"] // 2, mesh.shape["tp"] // X)
    return jax.shard_map(
        functools.partial(on_device, chips),
        mesh=mesh,
        in_specs=(
            P("ctx", "tp"),
            P("ctx", "tp"),
            P("ctx", "tp"),
            P("ctx", "tp"),
            P("ctx", "tp"),
            P("tp"),
            P("tp", None),
            P("ctx", "tp"),
        ),
        out_specs=(P("ctx", "tp"),) * 5,
        check_vma=False,
    )
```

```python
import functools

import jax
import jax.numpy as jnp
from jax import lax
from jax.experimental import pallas as pl
from jax.experimental.pallas import tpu as pltpu
from jax.sharding import PartitionSpec as P

DH = 128
EPS = 1e-06
MESH = pl.DeviceIdType.MESH
F32 = jnp.float32
BF16 = jnp.bfloat16
X = 4


def nn(a, b):
    return lax.dot_general(a, b, (((1,), (0,)), ((), ())), preferred_element_type=F32)


def nt(a, b):
    return lax.dot_general(a, b, (((1,), (1,)), ((), ())), preferred_element_type=F32)


def tn(a, b):
    return lax.dot_general(a, b, (((0,), (0,)), ((), ())), preferred_element_type=F32)


def identity(size):
    row = lax.broadcasted_iota(jnp.int32, (size, size), 0)
    column = lax.broadcasted_iota(jnp.int32, (size, size), 1)
    return jnp.where(row == column, 1.0, 0.0).astype(BF16)


def as_row(column):
    return jnp.broadcast_to(column, (column.shape[0], 128)).T[0:1, :]


def as_columns(row):
    return jnp.broadcast_to(row, (128, row.shape[1])).T


def kernel(
    sizes,
    q_in,
    k_in,
    v_in,
    ld_in,
    gate_in,
    gain_in,
    w_ref,
    target_in,
    out_ref,
    qg_ref,
    kg_ref,
    vg_ref,
    gg_ref,
    q_ref,
    k_ref,
    v_ref,
    ld_ref,
    gate_ref,
    gain_ref,
    target_ref,
    in_sems,
    wb,
    wrelay,
    uall,
    yacc,
    ystage,
    yrecv,
    gx,
    gall,
    fstage,
    frecv,
    weight,
    probs,
    kdec,
    att,
    klocal,
    vlocal,
    agrad,
    until_end,
    from_start,
    qdec,
    scale,
    closed,
    bown,
    bsib,
    bchip,
    s_out,
    s_in,
    s_keep,
    t_out,
    t_in,
    c_acc,
    d_acc,
    c_out,
    state,
    small_z,
    small_x,
    w_send,
    w_recv,
    w_own,
    ws_send,
    ws_recv,
    u_send,
    u_recv,
    y_send,
    y_recv,
    g_send,
    g_recv,
    f_send,
    f_recv,
    b_send,
    b_recv,
    bc_send,
    bc_recv,
    s_send,
    s_recv,
    t_send,
    t_recv,
    c_send,
    c_recv,
    sz_send,
    sz_recv,
    sx_send,
    sx_recv,
):
    Y, Z = sizes
    tokens = q_ref.shape[0]
    half_tokens = tokens // 2
    rows = w_ref.shape[0]
    half = rows // 2
    width = q_ref.shape[1]
    total_features = w_ref.shape[1]
    heads = width // DH

    ctx = lax.axis_index("ctx")
    tp = lax.axis_index("tp")
    core = lax.rem(ctx, 2)
    y = lax.div(ctx, 2)
    x = lax.rem(tp, X)
    z = lax.div(tp, X)
    sibling = (y * 2 + 1 - core, tp)
    is_zero = core == 0

    def xs(step):
        return lax.rem(x + step + X, X)

    def zs(step):
        return lax.rem(z + step + 2 * Z, Z)

    def at_x(step):
        return (ctx, z * X + xs(step))

    def at_z(step):
        return (ctx, zs(step) * X + x)

    def at_y(place):
        return (place * 2 + core, tp)

    sign = 1 - 2 * core
    left, right, opp = xs(-1), xs(1), xs(2)

    def send(src, dst, send_sem, recv_sem, device):
        copy = pltpu.make_async_remote_copy(
            src_ref=src,
            dst_ref=dst,
            send_sem=send_sem,
            recv_sem=recv_sem,
            device_id=device,
            device_id_type=MESH,
        )
        copy.start()

    def arrived(ref, sem):
        pltpu.make_async_copy(ref, ref, sem).wait()

    loads = [
        pltpu.make_async_copy(src, dst, in_sems.at[index])
        for index, (src, dst) in enumerate(
            (
                (ld_in, ld_ref),
                (k_in, k_ref),
                (v_in, v_ref),
                (q_in, q_ref),
                (gate_in, gate_ref),
                (gain_in, gain_ref),
                (target_in, target_ref),
            )
        )
    ]
    for load in loads:
        load.start()
    barrier = pltpu.get_barrier_semaphore()
    partners = [sibling] + [at_x(step) for step in range(1, X)]
    partners += [at_z(step) for step in range(1, Z)]
    partners += [at_y(lax.rem(y + step, Y)) for step in range(1, Y)]
    for partner in partners:
        pl.semaphore_signal(barrier, inc=1, device_id=partner, device_id_type=MESH)

    def w_columns(block, x_to):
        start = pl.multiple_of((block * X + x_to) * width, width)
        return pl.ds(start, width)

    my_rows = pl.ds(pl.multiple_of(core * half, half), half)
    x_far = xs(sign)

    def w_far(block, carry):
        send(w_ref.at[my_rows, w_columns(block, opp)], wrelay.at[block], w_send.at[0], w_recv.at[0], (ctx, z * X + x_far))
        return carry

    def w_near(block, carry):
        send(w_ref.at[my_rows, w_columns(block, right)], wb.at[block, x, core], w_send.at[1], w_recv.at[1], at_x(1))
        send(w_ref.at[my_rows, w_columns(block, left)], wb.at[block, x, core], w_send.at[2], w_recv.at[2], at_x(-1))
        return carry

    def w_mine(block, carry):
        for part in range(2):
            pltpu.make_async_copy(
                w_ref.at[pl.ds(part * half, half), w_columns(block, x)], wb.at[block, x, part], w_own
            ).start()
        return carry

    pl.semaphore_wait(barrier, len(partners))
    lax.fori_loop(0, Z, w_far, 0)
    lax.fori_loop(0, Z, w_near, 0)

    row = lax.broadcasted_iota(jnp.int32, (tokens, tokens), 0)
    column = lax.broadcasted_iota(jnp.int32, (tokens, tokens), 1)
    causal = row >= column
    loads[0].wait()
    upto = jnp.where(row <= column, 1.0, 0.0).astype(BF16)
    rest = ld_ref[...]
    cum = jnp.zeros_like(rest)
    for _ in range(3):
        piece = rest.astype(BF16)
        cum = cum + nn(piece, upto)
        rest = rest - piece.astype(F32)
    cum_rows = [cum[h : h + 1, :] for h in range(heads)]
    cums = [as_columns(c) for c in cum_rows]
    totals = [c[tokens - 1 : tokens, :] for c in cums]
    bown[...] = jnp.zeros_like(bown)
    for h in range(heads):
        bown[h : h + 1, :] = totals[h]
    loads[1].wait()
    loads[2].wait()

    def lanes(h):
        return slice(h * DH, (h + 1) * DH)

    own = []
    for h in range(heads):
        until_end[h] = jnp.exp(totals[h] - cums[h])
        decayed = (k_ref[:, lanes(h)].astype(F32) * until_end[h]).astype(BF16)
        kdec[:, lanes(h)] = decayed
        own.append(tn(decayed, v_ref[:, lanes(h)]))

    def of_core(pair):
        return jnp.where(is_zero, pair[0], pair[1])

    def scan_give(turn, h, value):
        @pl.when(core == h)
        def _():
            s_keep[turn] = value

        @pl.when(core != h)
        def _():
            s_out[turn] = value.astype(BF16)
            send(s_out.at[turn], s_in.at[turn], s_send.at[turn], s_recv.at[turn], sibling)

    def scan_way(turn):
        step = 1 if turn == 0 else -1
        first_here = is_zero if turn == 0 else jnp.logical_not(is_zero)
        return step, first_here

    def decays(ref):
        return of_core((ref[0:1, :], ref[1:2, :]))

    def reaches(place):
        return jnp.logical_and(place >= 0, place < Y)

    def scan_send(turn):
        step, first_here = scan_way(turn)
        arrived(s_in.at[turn], s_recv.at[turn])
        mine = s_keep[turn]
        theirs = s_in[turn].astype(F32)
        first = jnp.where(first_here, mine, theirs)
        second = jnp.where(first_here, theirs, mine)
        s_keep[turn] = first
        b_second = jnp.where(first_here, decays(bsib), decays(bown))
        t_out[turn] = (jnp.exp(b_second) * first + second).astype(BF16)
        for distance in range(1, Y):
            place = y + step * distance

            @pl.when(reaches(place))
            def _():
                send(
                    t_out.at[turn],
                    t_in.at[turn, distance - 1],
                    t_send.at[turn, distance - 1],
                    t_recv.at[turn, distance - 1],
                    at_y(place),
                )

    def scan_end(turn):
        step, first_here = scan_way(turn)
        c_acc[...] = jnp.zeros_like(c_acc)
        d_acc[...] = jnp.zeros_like(d_acc)
        for distance in range(1, Y):
            place = y - step * distance

            @pl.when(reaches(place))
            def _():
                slot = t_in.at[turn, distance - 1]
                arrived(slot, t_recv.at[turn, distance - 1])
                between = d_acc[0:1, :]
                c_acc[...] += jnp.exp(between) * slot[...].astype(F32)
                d_acc[0:1, :] = between + decays(bchip.at[place])

        b_first = jnp.where(first_here, decays(bown), decays(bsib))
        carried = c_acc[...]
        after = jnp.exp(b_first) * carried + s_keep[turn]
        state[turn, core] = jnp.where(first_here, carried, after).astype(BF16)
        c_out[turn] = jnp.where(first_here, after, carried).astype(BF16)
        send(c_out.at[turn], state.at[turn, core], c_send.at[turn], c_recv.at[turn], sibling)

    def scan_take(turn):
        arrived(state.at[turn, 1 - core], c_recv.at[turn])

    send(bown, bsib, b_send, b_recv, sibling)
    for h in range(heads):
        scan_give(0, h, own[h])
    lax.fori_loop(0, Z, w_mine, 0)

    arrived(bsib, b_recv)
    bchip[y] = bown[...] + bsib[...]
    for distance in range(1, Y):
        place = lax.rem(y + distance, Y)
        send(bchip.at[y], bchip.at[y], bc_send.at[distance - 1], bc_recv.at[distance - 1], at_y(place))
    scan_send(0)

    for load in loads[3:]:
        load.wait()
    for h in range(heads):
        gaps = cums[h][:, 0:1] - cum_rows[h]
        decay = jnp.where(causal, jnp.exp(jnp.minimum(gaps, 0.0)), 0.0)
        weight[h] = decay
        probs[h] = (nt(q_ref[:, lanes(h)], k_ref[:, lanes(h)]) * decay).astype(BF16)
        att[:, lanes(h)] = nn(probs[h], v_ref[:, lanes(h)])
        from_start[h] = jnp.exp(cums[h])
        qdec[:, lanes(h)] = (q_ref[:, lanes(h)].astype(F32) * from_start[h]).astype(BF16)
        gate_open = jax.nn.sigmoid(gate_ref[:, lanes(h)].astype(F32))
        scale[:, lanes(h)] = gain_ref[:, lanes(h)] * gate_open
        closed[:, lanes(h)] = 1.0 - gate_open

    for distance in range(1, Y):
        arrived(bchip.at[lax.rem(y - distance + Y, Y)], bc_recv.at[distance - 1])

    arrived(wrelay, w_recv.at[0])
    send(wrelay, wb.at[:, xs(-sign), core], w_send.at[3], w_recv.at[3], (ctx, z * X + x_far))

    scan_end(0)
    scan_take(0)

    far, near = Z // 2, Z - 1 - Z // 2
    hops = (far, near)
    ways = (sign, -sign)

    def u_part(way, step, part):
        return uall.at[zs(-ways[way] * step), part]

    def u_start(way, step, part):
        ref = u_part(way, step, part)
        send(ref, ref, u_send.at[way, step, part], u_recv.at[way, step, part], at_z(ways[way]))

    for part in range(2):
        span = slice(part * half_tokens, (part + 1) * half_tokens)
        for h in range(heads):
            from_state = nn(q_ref[span, lanes(h)], state[0, h]) * from_start[h, span, :]
            attended = att[span, lanes(h)] + from_state
            att[span, lanes(h)] = attended
            uall[z, part, :, lanes(h)] = (attended * scale[span, lanes(h)]).astype(BF16)
        for way in range(2):
            if hops[way] > 0:
                u_start(way, 0, part)

    def small_share(turn, value):
        small_z[turn, 0] = value
        for step in range(1, Z):
            send(small_z.at[turn, 0], small_z.at[turn, step], sz_send.at[turn, step - 1], sz_recv.at[turn, step - 1], at_z(step))

    def small_cross(turn):
        for step in range(1, Z):
            arrived(small_z.at[turn, step], sz_recv.at[turn, step - 1])
        sum_z = small_z[turn, 0]
        for step in range(1, Z):
            sum_z = sum_z + small_z[turn, step]
        small_x[turn, 0] = sum_z
        for step in range(1, X):
            send(small_x.at[turn, 0], small_x.at[turn, step], sx_send.at[turn, step - 1], sx_recv.at[turn, step - 1], at_x(step))

    def small_sum(turn):
        for step in range(1, X):
            arrived(small_x.at[turn, step], sx_recv.at[turn, step - 1])
        sum_x = small_x[turn, 0]
        for step in range(1, X):
            sum_x = sum_x + small_x[turn, step]
        return sum_x

    squares = jnp.zeros((tokens, 1), F32)
    for h in range(heads):
        attended = att[:, lanes(h)]
        squares = squares + jnp.sum(attended * attended, axis=1, keepdims=True)
    small_share(0, as_row(squares))

    def w_pair(source, sem, slot):
        ref = wb.at[:, source, core]
        arrived(ref, sem)
        send(ref, ref, ws_send.at[slot], ws_recv.at[slot], sibling)

    def w_block(block):
        return wb[block].reshape(X * rows, width)

    def w_rows(block, rows_of):
        return wb[block, rows_of].reshape(rows, width)

    def absorb(rows_of):
        blocks = [z] + [zs(-ways[way] * (step + 1)) for step in range(far - 1) for way in range(2) if step < hops[way]]
        for part in range(2):
            total = nt(w_rows(z, rows_of), uall[z, part])
            for block in blocks[1:]:
                total = total + nt(w_rows(block, rows_of), uall[block, part])
            yacc[part, rows_of] = total

    def u_pass(step, part):
        for way in range(2):
            if step < hops[way]:
                arrived(u_part(way, step + 1, part), u_recv.at[way, step, part])
                if step + 1 < hops[way]:
                    u_start(way, step + 1, part)

    for step in range(far - 1):
        for part in range(2):
            u_pass(step, part)
        if step == max(far - 3, 0):
            w_pair(left, w_recv.at[1], 0)
            w_pair(right, w_recv.at[2], 1)
    if far < 2:
        w_pair(left, w_recv.at[1], 0)
        w_pair(right, w_recv.at[2], 1)
    for part in range(2):
        arrived(wb.at[:, x, part], w_own)
    absorb(x)
    w_pair(opp, w_recv.at[3], 2)
    for slot, source in enumerate((left, right, opp)):
        arrived(wb.at[:, source, 1 - core], ws_recv.at[slot])
        absorb(source)
    small_cross(0)

    steps = (2, 1, 3)

    def y_start(part, step):
        ystage[part, step - 1] = yacc[part, xs(step)].astype(BF16)
        send(
            ystage.at[part, step - 1],
            yrecv.at[part, step - 1],
            y_send.at[part, step - 1],
            y_recv.at[part, step - 1],
            at_x(step),
        )

    def y_arrived(part, step):
        arrived(yrecv.at[part, step - 1], y_recv.at[part, step - 1])
        return yrecv[part, step - 1].astype(F32)

    for part in range(2):
        u_pass(far - 1, part)
        last = zs(sign * far)
        last_u = uall[last, part]

        def finish(rows_of):
            yacc[part, rows_of] += nt(w_rows(last, rows_of), last_u)

        for step in steps:
            finish(xs(step))
            y_start(part, step)
        finish(x)

    inv_rms = lax.rsqrt(small_sum(0) / total_features + EPS)

    def g_arrived(part, step):
        arrived(gx.at[part, xs(-step)], g_recv.at[part, step - 1])

    products = []
    for part in range(2):
        span = slice(part * half_tokens, (part + 1) * half_tokens)
        total = yacc[part, x]
        for step in (1, 3, 2):
            total = total + y_arrived(part, step)
        rounded = (total * inv_rms[:, span]).astype(BF16)
        grad = (rounded.astype(F32) - target_ref[:, span].astype(F32)).astype(BF16)
        gx[part, x] = grad
        for step in steps:
            ref = gx.at[part, x]
            send(ref, ref, g_send.at[part, step - 1], g_recv.at[part, step - 1], at_x(step))
        out_ref[:, span] = rounded
        products.append(jnp.sum(grad.astype(F32) * total, axis=0, keepdims=True))
    small_share(1, jnp.concatenate(products, axis=1))

    eye = identity(half_tokens)

    def feature_part(block, part):
        return nn(gall[part], w_block(block))

    def f_slot(way, step):
        return way * far + step

    def f_start(way, step, part, h, value):
        slot = f_slot(way, step)
        fstage[slot, part, h] = value.astype(BF16)
        send(
            fstage.at[slot, part, h],
            frecv.at[slot, part, h],
            f_send.at[slot, part, h],
            f_recv.at[slot, part, h],
            at_z(ways[way]),
        )

    def f_arrived(way, step, part, h):
        slot = f_slot(way, step)
        arrived(frecv.at[slot, part, h], f_recv.at[slot, part, h])
        return frecv[slot, part, h].astype(F32)

    for step in range(far):
        for part in range(2):
            if step == 0:
                for x_step in (1, 3, 2):
                    g_arrived(part, x_step)
                gall[part] = nt(eye, gx[part].reshape(X * rows, half_tokens)).astype(BF16)
            sums = [
                feature_part(zs(ways[way] * (hops[way] - step)), part) if step < hops[way] else None
                for way in range(2)
            ]
            for h in range(heads):
                for way in range(2):
                    if step < hops[way]:
                        value = sums[way][:, lanes(h)]
                        if step > 0:
                            value = value + f_arrived(way, step - 1, part, h)
                        f_start(way, step, part, h, value)
        if step == 0:
            small_cross(1)

    own_feature = [feature_part(z, part) for part in range(2)]
    mean_product = as_columns(small_sum(1) / total_features)
    inv = as_columns(inv_rms)

    for h in range(heads):
        pieces = []
        for part in range(2):
            value = own_feature[part][:, lanes(h)]
            for way in range(2):
                if hops[way] > 0:
                    value = value + f_arrived(way, hops[way] - 1, part, h)
            pieces.append(value)
        attended = att[:, lanes(h)]
        normed_grad = jnp.concatenate(pieces, axis=0) * scale[:, lanes(h)]
        grad = (inv * normed_grad - inv * inv * inv * attended * mean_product).astype(BF16)
        agrad[:, lanes(h)] = grad
        scan_give(1, h, tn(qdec[:, lanes(h)], grad))
        gg_ref[:, lanes(h)] = (normed_grad * attended * inv * closed[:, lanes(h)]).astype(BF16)

    for h in range(heads):
        grad = agrad[:, lanes(h)]
        score_grad = (nt(grad, v_ref[:, lanes(h)]) * weight[h]).astype(BF16)
        if h == 0:
            scan_send(1)
        qg_ref[:, lanes(h)] = (
            nn(score_grad, k_ref[:, lanes(h)]) + from_start[h] * nt(grad, state[0, h])
        ).astype(BF16)
        klocal[:, lanes(h)] = tn(score_grad, q_ref[:, lanes(h)])
        vlocal[:, lanes(h)] = tn(probs[h], grad)
    for index in range(4):
        arrived(wrelay, w_send.at[index])
    for index in range(3):
        arrived(wrelay, ws_send.at[index])
    for way in range(2):
        for step in range(hops[way]):
            for part in range(2):
                arrived(u_part(way, step, part), u_send.at[way, step, part])
                slot = f_slot(way, step)
                for h in range(heads):
                    arrived(fstage.at[slot, part, h], f_send.at[slot, part, h])
    for part in range(2):
        for slot in range(X - 1):
            arrived(ystage.at[part, slot], y_send.at[part, slot])
            arrived(ystage.at[part, slot], g_send.at[part, slot])
    arrived(bown, b_send)
    for distance in range(1, Y):
        arrived(bown, bc_send.at[distance - 1])
    for turn in range(2):
        arrived(s_out.at[turn], s_send.at[turn])
        for distance in range(1, Z):
            arrived(small_z.at[turn, 0], sz_send.at[turn, distance - 1])
        for distance in range(1, X):
            arrived(small_x.at[turn, 0], sx_send.at[turn, distance - 1])

    def scan_sent(turn):
        arrived(c_out.at[turn], c_send.at[turn])
        step, _ = scan_way(turn)
        for distance in range(1, Y):

            @pl.when(reaches(y + step * distance))
            def _():
                arrived(t_out.at[turn], t_send.at[turn, distance - 1])

    scan_sent(0)

    scan_end(1)
    scan_take(1)
    for h in range(heads):
        later = state[1, h]
        kg_ref[:, lanes(h)] = (
            klocal[:, lanes(h)] + until_end[h] * nt(v_ref[:, lanes(h)], later)
        ).astype(BF16)
        vg_ref[:, lanes(h)] = (vlocal[:, lanes(h)] + nn(kdec[:, lanes(h)], later)).astype(BF16)

    scan_sent(1)


def store(*refs):
    *refs, sems = refs
    count = len(refs) // 2
    copies = [pltpu.make_async_copy(refs[i], refs[count + i], sems.at[i]) for i in range(count)]
    for copy in copies:
        copy.start()
    for copy in copies:
        copy.wait()


def on_device(chips, queries, keys, values, log_decay, gate, norm_gain, out_weight, target):
    Y, Z = chips
    tokens, width = queries.shape
    rows, features = out_weight.shape
    half = rows // 2
    far = Z // 2
    vmem = pltpu.VMEM
    dma = pltpu.SemaphoreType.DMA
    scratch = [
        vmem((tokens, width), BF16),
        vmem((tokens, width), BF16),
        vmem((tokens, width), BF16),
        vmem((width // DH, tokens), F32),
        vmem((tokens, width), BF16),
        vmem((1, width), F32),
        vmem((rows, tokens), BF16),
        dma((7,)),
        vmem((Z, X, 2, half, width), BF16),
        vmem((Z, half, width), BF16),
        vmem((Z, 2, tokens // 2, width), BF16),
        vmem((2, X, rows, tokens // 2), F32),
        vmem((2, X - 1, rows, tokens // 2), BF16),
        vmem((2, X - 1, rows, tokens // 2), BF16),
        vmem((2, X, rows, tokens // 2), BF16),
        vmem((2, tokens // 2, X * rows), BF16),
        vmem((Z - 1, 2, 2, tokens // 2, DH), BF16),
        vmem((Z - 1, 2, 2, tokens // 2, DH), BF16),
        vmem((width // DH, tokens, tokens), F32),
        vmem((width // DH, tokens, tokens), BF16),
        vmem((tokens, width), BF16),
        vmem((tokens, width), F32),
        vmem((tokens, width), F32),
        vmem((tokens, width), F32),
        vmem((tokens, width), BF16),
        vmem((width // DH, tokens, DH), F32),
        vmem((width // DH, tokens, DH), F32),
        vmem((tokens, width), BF16),
        vmem((tokens, width), F32),
        vmem((tokens, width), F32),
        vmem((8, 128), F32),
        vmem((8, 128), F32),
        vmem((Y, 8, 128), F32),
        vmem((2, DH, DH), BF16),
        vmem((2, DH, DH), BF16),
        vmem((2, DH, DH), F32),
        vmem((2, DH, DH), BF16),
        vmem((2, max(Y - 1, 1), DH, DH), BF16),
        vmem((DH, DH), F32),
        vmem((8, 128), F32),
        vmem((2, DH, DH), BF16),
        vmem((2, 2, DH, DH), BF16),
        vmem((2, Z, 1, tokens), F32),
        vmem((2, X, 1, tokens), F32),
        dma((4,)),
        dma((4,)),
        dma,
        dma((3,)),
        dma((3,)),
        dma((2, far, 2)),
        dma((2, far, 2)),
        dma((2, X - 1)),
        dma((2, X - 1)),
        dma((2, X - 1)),
        dma((2, X - 1)),
        dma((Z - 1, 2, 2)),
        dma((Z - 1, 2, 2)),
        dma,
        dma,
        dma((max(Y - 1, 1),)),
        dma((max(Y - 1, 1),)),
        dma((2,)),
        dma((2,)),
        dma((2, max(Y - 1, 1))),
        dma((2, max(Y - 1, 1))),
        dma((2,)),
        dma((2,)),
        dma((2, Z - 1)),
        dma((2, Z - 1)),
        dma((2, X - 1)),
        dma((2, X - 1)),
    ]
    in_vmem = pl.BlockSpec(memory_space=pltpu.VMEM)
    in_hbm = pl.BlockSpec(memory_space=pltpu.HBM)
    shapes = [(rows, tokens)] + [(tokens, width)] * 4
    operands = (queries, keys, values, log_decay.T, gate, norm_gain.reshape(1, width), out_weight, target.T)
    results = pl.pallas_call(
        functools.partial(kernel, chips),
        out_shape=tuple(pltpu.VMEM(shape, BF16) for shape in shapes),
        in_specs=[in_hbm] * 8,
        out_specs=(in_vmem,) * 5,
        scratch_shapes=scratch,
        compiler_params=pltpu.CompilerParams(
            collective_id=0, has_side_effects=True, vmem_limit_bytes=48 * 1024 * 1024
        ),
        cost_estimate=pl.CostEstimate(flops=2 * 10**9, bytes_accessed=8 * 10**6, transcendentals=10**6),
        name="attention_layer",
    )(*[pltpu.with_memory_space_constraint(operand, pltpu.HBM) for operand in operands])
    output, *grads = pl.pallas_call(
        store,
        out_shape=tuple(jax.ShapeDtypeStruct(shape, BF16) for shape in shapes),
        in_specs=[in_vmem] * 5,
        out_specs=(in_hbm,) * 5,
        scratch_shapes=[dma((5,))],
        compiler_params=pltpu.CompilerParams(vmem_limit_bytes=4 * 1024 * 1024),
        name="store",
    )(*results)
    return (output.T, *grads)


def solution(mesh):
    chips = (mesh.shape["ctx"] // 2, mesh.shape["tp"] // X)
    return jax.shard_map(
        functools.partial(on_device, chips),
        mesh=mesh,
        in_specs=(
            P("ctx", "tp"),
            P("ctx", "tp"),
            P("ctx", "tp"),
            P("ctx", "tp"),
            P("ctx", "tp"),
            P("tp"),
            P("tp", None),
            P("ctx", "tp"),
        ),
        out_specs=(P("ctx", "tp"),) * 5,
        check_vma=False,
    )
```

```python
import functools

import jax
import jax.numpy as jnp
from jax import lax
from jax.experimental import pallas as pl
from jax.experimental.pallas import tpu as pltpu
from jax.sharding import PartitionSpec as P

DH = 128
EPS = 1e-06
MESH = pl.DeviceIdType.MESH
F32 = jnp.float32
BF16 = jnp.bfloat16
X = 4


def nn(a, b):
    return lax.dot_general(a, b, (((1,), (0,)), ((), ())), preferred_element_type=F32)


def nt(a, b):
    return lax.dot_general(a, b, (((1,), (1,)), ((), ())), preferred_element_type=F32)


def tn(a, b):
    return lax.dot_general(a, b, (((0,), (0,)), ((), ())), preferred_element_type=F32)


def identity(size):
    row = lax.broadcasted_iota(jnp.int32, (size, size), 0)
    column = lax.broadcasted_iota(jnp.int32, (size, size), 1)
    return jnp.where(row == column, 1.0, 0.0).astype(BF16)


def as_row(column):
    return jnp.broadcast_to(column, (column.shape[0], 128)).T[0:1, :]


def as_columns(row):
    return jnp.broadcast_to(row, (128, row.shape[1])).T


def kernel(
    sizes,
    q_in,
    k_in,
    v_in,
    ld_in,
    gate_in,
    gain_in,
    w_ref,
    target_in,
    out_ref,
    qg_ref,
    kg_ref,
    vg_ref,
    gg_ref,
    q_ref,
    k_ref,
    v_ref,
    ld_ref,
    gate_ref,
    gain_ref,
    target_ref,
    in_sems,
    wb,
    wrelay,
    uall,
    yacc,
    ystage,
    yrecv,
    gx,
    gall,
    fstage,
    frecv,
    weight,
    probs,
    kdec,
    att,
    klocal,
    vlocal,
    agrad,
    until_end,
    from_start,
    qdec,
    scale,
    closed,
    bown,
    bsib,
    bchip,
    s_out,
    s_in,
    s_keep,
    t_out,
    t_in,
    c_acc,
    d_acc,
    c_out,
    state,
    small_z,
    small_x,
    w_send,
    w_recv,
    w_own,
    ws_send,
    ws_recv,
    u_send,
    u_recv,
    y_send,
    y_recv,
    g_send,
    g_recv,
    f_send,
    f_recv,
    b_send,
    b_recv,
    bc_send,
    bc_recv,
    s_send,
    s_recv,
    t_send,
    t_recv,
    c_send,
    c_recv,
    sz_send,
    sz_recv,
    sx_send,
    sx_recv,
):
    Y, Z = sizes
    tokens = q_ref.shape[0]
    half_tokens = tokens // 2
    rows = w_ref.shape[0]
    half = rows // 2
    width = q_ref.shape[1]
    total_features = w_ref.shape[1]
    heads = width // DH

    ctx = lax.axis_index("ctx")
    tp = lax.axis_index("tp")
    core = lax.rem(ctx, 2)
    y = lax.div(ctx, 2)
    x = lax.rem(tp, X)
    z = lax.div(tp, X)
    sibling = (y * 2 + 1 - core, tp)
    is_zero = core == 0

    def xs(step):
        return lax.rem(x + step + X, X)

    def zs(step):
        return lax.rem(z + step + 2 * Z, Z)

    def at_x(step):
        return (ctx, z * X + xs(step))

    def at_z(step):
        return (ctx, zs(step) * X + x)

    def at_y(place):
        return (place * 2 + core, tp)

    sign = 1 - 2 * core
    left, right, opp = xs(-1), xs(1), xs(2)

    def send(src, dst, send_sem, recv_sem, device):
        copy = pltpu.make_async_remote_copy(
            src_ref=src,
            dst_ref=dst,
            send_sem=send_sem,
            recv_sem=recv_sem,
            device_id=device,
            device_id_type=MESH,
        )
        copy.start()

    def arrived(ref, sem):
        pltpu.make_async_copy(ref, ref, sem).wait()

    loads = [
        pltpu.make_async_copy(src, dst, in_sems.at[index])
        for index, (src, dst) in enumerate(
            (
                (ld_in, ld_ref),
                (k_in, k_ref),
                (v_in, v_ref),
                (q_in, q_ref),
                (gate_in, gate_ref),
                (gain_in, gain_ref),
                (target_in, target_ref),
            )
        )
    ]
    for load in loads:
        load.start()
    barrier = pltpu.get_barrier_semaphore()
    partners = [sibling] + [at_x(step) for step in range(1, X)]
    partners += [at_z(step) for step in range(1, Z)]
    partners += [at_y(lax.rem(y + step, Y)) for step in range(1, Y)]
    for partner in partners:
        pl.semaphore_signal(barrier, inc=1, device_id=partner, device_id_type=MESH)

    def w_columns(block, x_to):
        start = pl.multiple_of((block * X + x_to) * width, width)
        return pl.ds(start, width)

    my_rows = pl.ds(pl.multiple_of(core * half, half), half)
    x_far = xs(sign)

    def w_far(block, carry):
        send(w_ref.at[my_rows, w_columns(block, opp)], wrelay.at[block], w_send.at[0], w_recv.at[0], (ctx, z * X + x_far))
        return carry

    def w_near(block, carry):
        send(w_ref.at[my_rows, w_columns(block, right)], wb.at[block, x, core], w_send.at[1], w_recv.at[1], at_x(1))
        send(w_ref.at[my_rows, w_columns(block, left)], wb.at[block, x, core], w_send.at[2], w_recv.at[2], at_x(-1))
        return carry

    def w_mine(block, carry):
        for part in range(2):
            pltpu.make_async_copy(
                w_ref.at[pl.ds(part * half, half), w_columns(block, x)], wb.at[block, x, part], w_own
            ).start()
        return carry

    row = lax.broadcasted_iota(jnp.int32, (tokens, tokens), 0)
    column = lax.broadcasted_iota(jnp.int32, (tokens, tokens), 1)
    causal = row >= column
    loads[0].wait()
    upto = jnp.where(row <= column, 1.0, 0.0).astype(BF16)
    rest = ld_ref[...]
    cum = jnp.zeros_like(rest)
    for _ in range(3):
        piece = rest.astype(BF16)
        cum = cum + nn(piece, upto)
        rest = rest - piece.astype(F32)
    cum_rows = [cum[h : h + 1, :] for h in range(heads)]
    cums = [as_columns(c) for c in cum_rows]
    totals = [c[tokens - 1 : tokens, :] for c in cums]
    bown[...] = jnp.zeros_like(bown)
    for h in range(heads):
        bown[h : h + 1, :] = totals[h]
    loads[1].wait()
    loads[2].wait()

    def lanes(h):
        return slice(h * DH, (h + 1) * DH)

    own = []
    for h in range(heads):
        until_end[h] = jnp.exp(totals[h] - cums[h])
        decayed = (k_ref[:, lanes(h)].astype(F32) * until_end[h]).astype(BF16)
        kdec[:, lanes(h)] = decayed
        own.append(tn(decayed, v_ref[:, lanes(h)]))

    def of_core(pair):
        return jnp.where(is_zero, pair[0], pair[1])

    def scan_give(turn, h, value):
        @pl.when(core == h)
        def _():
            s_keep[turn] = value

        @pl.when(core != h)
        def _():
            s_out[turn] = value.astype(BF16)
            send(s_out.at[turn], s_in.at[turn], s_send.at[turn], s_recv.at[turn], sibling)

    def scan_way(turn):
        step = 1 if turn == 0 else -1
        first_here = is_zero if turn == 0 else jnp.logical_not(is_zero)
        return step, first_here

    def decays(ref):
        return of_core((ref[0:1, :], ref[1:2, :]))

    def reaches(place):
        return jnp.logical_and(place >= 0, place < Y)

    def scan_send(turn):
        step, first_here = scan_way(turn)
        arrived(s_in.at[turn], s_recv.at[turn])
        mine = s_keep[turn]
        theirs = s_in[turn].astype(F32)
        first = jnp.where(first_here, mine, theirs)
        second = jnp.where(first_here, theirs, mine)
        s_keep[turn] = first
        b_second = jnp.where(first_here, decays(bsib), decays(bown))
        t_out[turn] = (jnp.exp(b_second) * first + second).astype(BF16)
        for distance in range(1, Y):
            place = y + step * distance

            @pl.when(reaches(place))
            def _():
                send(
                    t_out.at[turn],
                    t_in.at[turn, distance - 1],
                    t_send.at[turn, distance - 1],
                    t_recv.at[turn, distance - 1],
                    at_y(place),
                )

    def scan_end(turn):
        step, first_here = scan_way(turn)
        c_acc[...] = jnp.zeros_like(c_acc)
        d_acc[...] = jnp.zeros_like(d_acc)
        for distance in range(1, Y):
            place = y - step * distance

            @pl.when(reaches(place))
            def _():
                slot = t_in.at[turn, distance - 1]
                arrived(slot, t_recv.at[turn, distance - 1])
                between = d_acc[0:1, :]
                c_acc[...] += jnp.exp(between) * slot[...].astype(F32)
                d_acc[0:1, :] = between + decays(bchip.at[place])

        b_first = jnp.where(first_here, decays(bown), decays(bsib))
        carried = c_acc[...]
        after = jnp.exp(b_first) * carried + s_keep[turn]
        c_out[turn] = jnp.where(first_here, after, carried).astype(BF16)
        send(c_out.at[turn], state.at[turn, core], c_send.at[turn], c_recv.at[turn], sibling)
        state[turn, core] = jnp.where(first_here, carried, after).astype(BF16)

    def scan_take(turn):
        arrived(state.at[turn, 1 - core], c_recv.at[turn])

    pl.semaphore_wait(barrier, len(partners))
    send(bown, bsib, b_send, b_recv, sibling)
    for h in range(heads):
        scan_give(0, h, own[h])
    lax.fori_loop(0, Z, w_far, 0)
    lax.fori_loop(0, Z, w_near, 0)
    lax.fori_loop(0, Z, w_mine, 0)

    arrived(bsib, b_recv)
    bchip[y] = bown[...] + bsib[...]
    for distance in range(1, Y):
        place = lax.rem(y + distance, Y)
        send(bchip.at[y], bchip.at[y], bc_send, bc_recv.at[distance - 1], at_y(place))
    scan_send(0)

    for load in loads[3:]:
        load.wait()
    for h in range(heads):
        gaps = cums[h][:, 0:1] - cum_rows[h]
        decay = jnp.where(causal, jnp.exp(jnp.minimum(gaps, 0.0)), 0.0)
        weight[h] = decay
        probs[h] = (nt(q_ref[:, lanes(h)], k_ref[:, lanes(h)]) * decay).astype(BF16)
        att[:, lanes(h)] = nn(probs[h], v_ref[:, lanes(h)])
        from_start[h] = jnp.exp(cums[h])
        gate_open = jax.nn.sigmoid(gate_ref[:, lanes(h)].astype(F32))
        scale[:, lanes(h)] = gain_ref[:, lanes(h)] * gate_open

    for distance in range(1, Y):
        arrived(bchip.at[lax.rem(y - distance + Y, Y)], bc_recv.at[distance - 1])

    scan_end(0)

    far, near = Z // 2, Z - 1 - Z // 2
    hops = (far, near)
    ways = (sign, -sign)

    def u_part(way, step, part, h):
        return uall.at[zs(-ways[way] * step), part, h]

    def u_start(way, step, part, h):
        ref = u_part(way, step, part, h)
        send(ref, ref, u_send, u_recv.at[way, step, part, h], at_z(ways[way]))

    order = (core, 1 - core)

    def any_lanes(h):
        return pl.ds(pl.multiple_of(h * DH, DH), DH)

    for turn, h in enumerate(order):
        if turn == 1:
            scan_take(0)
        for part in range(2):
            span = slice(part * half_tokens, (part + 1) * half_tokens)
            from_state = nn(q_ref[span, any_lanes(h)], state[0, h]) * from_start[h, span, :]
            attended = att[span, any_lanes(h)] + from_state
            att[span, any_lanes(h)] = attended
            uall[z, part, h] = (attended * scale[span, any_lanes(h)]).astype(BF16)
            for way in range(2):
                if hops[way] > 0:
                    u_start(way, 0, part, h)

    def small_share(turn, value):
        small_z[turn, 0] = value
        for step in range(1, Z):
            send(small_z.at[turn, 0], small_z.at[turn, step], sz_send, sz_recv.at[turn, step - 1], at_z(step))

    def small_cross(turn):
        for step in range(1, Z):
            arrived(small_z.at[turn, step], sz_recv.at[turn, step - 1])
        sum_z = small_z[turn, 0]
        for step in range(1, Z):
            sum_z = sum_z + small_z[turn, step]
        small_x[turn, 0] = sum_z
        for step in range(1, X):
            send(small_x.at[turn, 0], small_x.at[turn, step], sx_send, sx_recv.at[turn, step - 1], at_x(step))

    def small_sum(turn):
        for step in range(1, X):
            arrived(small_x.at[turn, step], sx_recv.at[turn, step - 1])
        sum_x = small_x[turn, 0]
        for step in range(1, X):
            sum_x = sum_x + small_x[turn, step]
        return sum_x

    squares = jnp.zeros((tokens, 1), F32)
    for h in range(heads):
        attended = att[:, lanes(h)]
        squares = squares + jnp.sum(attended * attended, axis=1, keepdims=True)
    small_share(0, as_row(squares))

    arrived(wrelay, w_recv.at[0])
    send(wrelay, wb.at[:, xs(-sign), core], w_send.at[3], w_recv.at[3], (ctx, z * X + x_far))

    for h in range(heads):
        qdec[:, lanes(h)] = (q_ref[:, lanes(h)].astype(F32) * from_start[h]).astype(BF16)
        closed[:, lanes(h)] = 1.0 - jax.nn.sigmoid(gate_ref[:, lanes(h)].astype(F32))

    def w_pair(source, sem, slot):
        ref = wb.at[:, source, core]
        arrived(ref, sem)
        send(ref, ref, ws_send.at[slot], ws_recv.at[slot], sibling)

    def w_block(block):
        return wb[block].reshape(X * rows, width)

    def u_block(block, part):
        return jnp.concatenate([uall[block, part, h] for h in range(heads)], axis=1)

    def accumulate(block, part):
        yacc[part] += nt(w_block(block), u_block(block, part)).reshape(yacc.shape[1:])

    def u_pass(step, part, some):
        for h in some:
            for way in range(2):
                if step < hops[way]:
                    arrived(u_part(way, step + 1, part, h), u_recv.at[way, step, part, h])
                    if step + 1 < hops[way]:
                        u_start(way, step + 1, part, h)

    def absorb(step):
        for way in range(2):
            if step < hops[way]:
                for part in range(2):
                    accumulate(zs(-ways[way] * (step + 1)), part)

    for step in range(far - 1):
        for h in order:
            for part in range(2):
                u_pass(step, part, (h,))
        if step == far - 3:
            w_pair(left, w_recv.at[1], 0)
            w_pair(right, w_recv.at[2], 1)
    if far < 3:
        w_pair(left, w_recv.at[1], 0)
        w_pair(right, w_recv.at[2], 1)
    w_pair(opp, w_recv.at[3], 2)
    small_cross(0)
    for part in range(2):
        arrived(wb.at[:, x, part], w_own)
    for slot, source in enumerate((left, right, opp)):
        arrived(wb.at[:, source, 1 - core], ws_recv.at[slot])
    for part in range(2):
        yacc[part] = nt(w_block(z), u_block(z, part)).reshape(yacc.shape[1:])
    for step in range(far - 1):
        absorb(step)

    steps = (2, 1, 3)

    def y_start(part, step):
        ystage[part, step - 1] = yacc[part, xs(step)].astype(BF16)
        send(
            ystage.at[part, step - 1],
            yrecv.at[part, step - 1],
            y_send,
            y_recv.at[part, step - 1],
            at_x(step),
        )

    def y_arrived(part, step):
        arrived(yrecv.at[part, step - 1], y_recv.at[part, step - 1])
        return yrecv[part, step - 1].astype(F32)

    for part in range(2):
        u_pass(far - 1, part, order)
        last = zs(sign * far)
        last_u = u_block(last, part)

        def finish(rows_of):
            block = wb[last, rows_of].reshape(rows, width)
            yacc[part, rows_of] += nt(block, last_u)

        for step in steps:
            finish(xs(step))
            y_start(part, step)
        finish(x)

    inv_rms = lax.rsqrt(small_sum(0) / total_features + EPS)

    def g_arrived(part, step):
        arrived(gx.at[part, xs(-step)], g_recv.at[part, step - 1])

    products = []
    for part in range(2):
        span = slice(part * half_tokens, (part + 1) * half_tokens)
        total = yacc[part, x]
        for step in (1, 3, 2):
            total = total + y_arrived(part, step)
        rounded = (total * inv_rms[:, span]).astype(BF16)
        grad = (rounded.astype(F32) - target_ref[:, span].astype(F32)).astype(BF16)
        gx[part, x] = grad
        for step in steps:
            ref = gx.at[part, x]
            send(ref, ref, g_send, g_recv.at[part, step - 1], at_x(step))
        out_ref[:, span] = rounded
        products.append(jnp.sum(grad.astype(F32) * total, axis=0, keepdims=True))
    small_share(1, jnp.concatenate(products, axis=1))

    eye = identity(half_tokens)

    def feature_part(block, part):
        return nn(gall[part], w_block(block))

    def f_slot(way, step):
        return way * far + step

    def f_start(way, step, part, h, value):
        slot = f_slot(way, step)
        fstage[slot, part, h] = value.astype(BF16)
        send(
            fstage.at[slot, part, h],
            frecv.at[slot, part, h],
            f_send,
            f_recv.at[slot, part, h],
            at_z(ways[way]),
        )

    def f_arrived(way, step, part, h):
        slot = f_slot(way, step)
        arrived(frecv.at[slot, part, h], f_recv.at[slot, part, h])
        return frecv[slot, part, h].astype(F32)

    for step in range(far):
        for part in range(2):
            if step == 0:
                for x_step in (1, 3, 2):
                    g_arrived(part, x_step)
                gall[part] = nt(eye, gx[part].reshape(X * rows, half_tokens)).astype(BF16)
            sums = [
                feature_part(zs(ways[way] * (hops[way] - step)), part) if step < hops[way] else None
                for way in range(2)
            ]
            for h in range(heads):
                for way in range(2):
                    if step < hops[way]:
                        value = sums[way][:, lanes(h)]
                        if step > 0:
                            value = value + f_arrived(way, step - 1, part, h)
                        f_start(way, step, part, h, value)
        if step == 0:
            small_cross(1)

    own_feature = [feature_part(z, part) for part in range(2)]
    mean_product = as_columns(small_sum(1) / total_features)
    inv = as_columns(inv_rms)

    for h in range(heads):
        pieces = []
        for part in range(2):
            value = own_feature[part][:, lanes(h)]
            for way in range(2):
                if hops[way] > 0:
                    value = value + f_arrived(way, hops[way] - 1, part, h)
            pieces.append(value)
        attended = att[:, lanes(h)]
        normed_grad = jnp.concatenate(pieces, axis=0) * scale[:, lanes(h)]
        grad = (inv * normed_grad - inv * inv * inv * attended * mean_product).astype(BF16)
        agrad[:, lanes(h)] = grad
        scan_give(1, h, tn(qdec[:, lanes(h)], grad))
        gg_ref[:, lanes(h)] = (normed_grad * attended * inv * closed[:, lanes(h)]).astype(BF16)

    for h in range(heads):
        grad = agrad[:, lanes(h)]
        score_grad = (nt(grad, v_ref[:, lanes(h)]) * weight[h]).astype(BF16)
        if h == 0:
            scan_send(1)
        qg_ref[:, lanes(h)] = (
            nn(score_grad, k_ref[:, lanes(h)]) + from_start[h] * nt(grad, state[0, h])
        ).astype(BF16)
        klocal[:, lanes(h)] = tn(score_grad, q_ref[:, lanes(h)])
        vlocal[:, lanes(h)] = tn(probs[h], grad)
    for index in range(4):
        arrived(wrelay, w_send.at[index])
    for index in range(3):
        arrived(wrelay, ws_send.at[index])
    arrived(uall.at[pl.ds(0, Z - 1)], u_send)
    arrived(fstage, f_send)
    arrived(ystage, y_send)
    arrived(ystage, g_send)
    arrived(bown, b_send)
    if Y > 1:
        arrived(bchip.at[pl.ds(0, Y - 1)], bc_send)
    arrived(small_z.at[:, pl.ds(0, Z - 1)], sz_send)
    arrived(small_x.at[:, pl.ds(0, X - 1)], sx_send)
    for turn in range(2):
        arrived(s_out.at[turn], s_send.at[turn])

    def scan_sent(turn):
        arrived(c_out.at[turn], c_send.at[turn])
        step, _ = scan_way(turn)
        for distance in range(1, Y):

            @pl.when(reaches(y + step * distance))
            def _():
                arrived(t_out.at[turn], t_send.at[turn, distance - 1])

    scan_sent(0)

    scan_end(1)
    for turn, h in enumerate(order):
        if turn == 1:
            scan_take(1)
        at = any_lanes(h)
        later = state[1, h]
        kg_ref[:, at] = (klocal[:, at] + until_end[h] * nt(v_ref[:, at], later)).astype(BF16)
        vg_ref[:, at] = (vlocal[:, at] + nn(kdec[:, at], later)).astype(BF16)

    scan_sent(1)


def store(*refs):
    *refs, sems = refs
    count = len(refs) // 2
    copies = [pltpu.make_async_copy(refs[i], refs[count + i], sems.at[i]) for i in range(count)]
    for copy in copies:
        copy.start()
    for copy in copies:
        copy.wait()


def on_device(chips, queries, keys, values, log_decay, gate, norm_gain, out_weight, target):
    Y, Z = chips
    tokens, width = queries.shape
    rows, features = out_weight.shape
    half = rows // 2
    far = Z // 2
    vmem = pltpu.VMEM
    dma = pltpu.SemaphoreType.DMA
    scratch = [
        vmem((tokens, width), BF16),
        vmem((tokens, width), BF16),
        vmem((tokens, width), BF16),
        vmem((width // DH, tokens), F32),
        vmem((tokens, width), BF16),
        vmem((1, width), F32),
        vmem((rows, tokens), BF16),
        dma((7,)),
        vmem((Z, X, 2, half, width), BF16),
        vmem((Z, half, width), BF16),
        vmem((Z, 2, width // DH, tokens // 2, DH), BF16),
        vmem((2, X, rows, tokens // 2), F32),
        vmem((2, X - 1, rows, tokens // 2), BF16),
        vmem((2, X - 1, rows, tokens // 2), BF16),
        vmem((2, X, rows, tokens // 2), BF16),
        vmem((2, tokens // 2, X * rows), BF16),
        vmem((Z - 1, 2, 2, tokens // 2, DH), BF16),
        vmem((Z - 1, 2, 2, tokens // 2, DH), BF16),
        vmem((width // DH, tokens, tokens), F32),
        vmem((width // DH, tokens, tokens), BF16),
        vmem((tokens, width), BF16),
        vmem((tokens, width), F32),
        vmem((tokens, width), F32),
        vmem((tokens, width), F32),
        vmem((tokens, width), BF16),
        vmem((width // DH, tokens, DH), F32),
        vmem((width // DH, tokens, DH), F32),
        vmem((tokens, width), BF16),
        vmem((tokens, width), F32),
        vmem((tokens, width), F32),
        vmem((8, 128), F32),
        vmem((8, 128), F32),
        vmem((Y, 8, 128), F32),
        vmem((2, DH, DH), BF16),
        vmem((2, DH, DH), BF16),
        vmem((2, DH, DH), F32),
        vmem((2, DH, DH), BF16),
        vmem((2, max(Y - 1, 1), DH, DH), BF16),
        vmem((DH, DH), F32),
        vmem((8, 128), F32),
        vmem((2, DH, DH), BF16),
        vmem((2, 2, DH, DH), BF16),
        vmem((2, Z, 1, tokens), F32),
        vmem((2, X, 1, tokens), F32),
        dma((4,)),
        dma((4,)),
        dma,
        dma((3,)),
        dma((3,)),
        dma,
        dma((2, far, 2, 2)),
        dma,
        dma((2, X - 1)),
        dma,
        dma((2, X - 1)),
        dma,
        dma((Z - 1, 2, 2)),
        dma,
        dma,
        dma,
        dma((max(Y - 1, 1),)),
        dma((2,)),
        dma((2,)),
        dma((2, max(Y - 1, 1))),
        dma((2, max(Y - 1, 1))),
        dma((2,)),
        dma((2,)),
        dma,
        dma((2, Z - 1)),
        dma,
        dma((2, X - 1)),
    ]
    in_vmem = pl.BlockSpec(memory_space=pltpu.VMEM)
    in_hbm = pl.BlockSpec(memory_space=pltpu.HBM)
    shapes = [(rows, tokens)] + [(tokens, width)] * 4
    operands = (queries, keys, values, log_decay.T, gate, norm_gain.reshape(1, width), out_weight, target.T)
    results = pl.pallas_call(
        functools.partial(kernel, chips),
        out_shape=tuple(pltpu.VMEM(shape, BF16) for shape in shapes),
        in_specs=[in_hbm] * 8,
        out_specs=(in_vmem,) * 5,
        scratch_shapes=scratch,
        compiler_params=pltpu.CompilerParams(
            collective_id=0, has_side_effects=True, vmem_limit_bytes=48 * 1024 * 1024
        ),
        cost_estimate=pl.CostEstimate(flops=2 * 10**9, bytes_accessed=8 * 10**6, transcendentals=10**6),
        name="attention_layer",
    )(*[pltpu.with_memory_space_constraint(operand, pltpu.HBM) for operand in operands])
    output, *grads = pl.pallas_call(
        store,
        out_shape=tuple(jax.ShapeDtypeStruct(shape, BF16) for shape in shapes),
        in_specs=[in_vmem] * 5,
        out_specs=(in_hbm,) * 5,
        scratch_shapes=[dma((5,))],
        compiler_params=pltpu.CompilerParams(vmem_limit_bytes=4 * 1024 * 1024),
        name="store",
    )(*results)
    return (output.T, *grads)


def solution(mesh):
    chips = (mesh.shape["ctx"] // 2, mesh.shape["tp"] // X)
    return jax.shard_map(
        functools.partial(on_device, chips),
        mesh=mesh,
        in_specs=(
            P("ctx", "tp"),
            P("ctx", "tp"),
            P("ctx", "tp"),
            P("ctx", "tp"),
            P("ctx", "tp"),
            P("tp"),
            P("tp", None),
            P("ctx", "tp"),
        ),
        out_specs=(P("ctx", "tp"),) * 5,
        check_vma=False,
    )
```

```python
import functools

import jax
import jax.numpy as jnp
from jax import lax
from jax.experimental import pallas as pl
from jax.experimental.pallas import tpu as pltpu
from jax.sharding import PartitionSpec as P

DH = 128
EPS = 1e-06
MESH = pl.DeviceIdType.MESH
F32 = jnp.float32
BF16 = jnp.bfloat16
X = 4


def nn(a, b):
    return lax.dot_general(a, b, (((1,), (0,)), ((), ())), preferred_element_type=F32)


def nt(a, b):
    return lax.dot_general(a, b, (((1,), (1,)), ((), ())), preferred_element_type=F32)


def tn(a, b):
    return lax.dot_general(a, b, (((0,), (0,)), ((), ())), preferred_element_type=F32)


def identity(size):
    row = lax.broadcasted_iota(jnp.int32, (size, size), 0)
    column = lax.broadcasted_iota(jnp.int32, (size, size), 1)
    return jnp.where(row == column, 1.0, 0.0).astype(BF16)


def as_row(column):
    return jnp.broadcast_to(column, (column.shape[0], 128)).T[0:1, :]


def as_columns(row):
    return jnp.broadcast_to(row, (128, row.shape[1])).T


def kernel(
    sizes,
    q_in,
    k_in,
    v_in,
    ld_in,
    gate_in,
    gain_in,
    w_ref,
    target_in,
    out_ref,
    qg_ref,
    kg_ref,
    vg_ref,
    gg_ref,
    q_ref,
    k_ref,
    v_ref,
    ld_ref,
    gate_ref,
    gain_ref,
    target_ref,
    in_sems,
    wb,
    wrelay,
    uall,
    yacc,
    ystage,
    yrecv,
    gx,
    gall,
    fstage,
    frecv,
    weight,
    probs,
    kdec,
    att,
    klocal,
    vlocal,
    agrad,
    until_end,
    from_start,
    qdec,
    scale,
    closed,
    bown,
    bsib,
    bchip,
    s_out,
    s_in,
    s_keep,
    t_out,
    t_in,
    c_acc,
    d_acc,
    c_out,
    state,
    small_z,
    small_x,
    w_send,
    w_recv,
    w_own,
    ws_send,
    ws_recv,
    u_send,
    u_recv,
    y_send,
    y_recv,
    g_send,
    g_recv,
    f_send,
    f_recv,
    b_send,
    b_recv,
    bc_send,
    bc_recv,
    s_send,
    s_recv,
    t_send,
    t_recv,
    c_send,
    c_recv,
    sz_send,
    sz_recv,
    sx_send,
    sx_recv,
):
    Y, Z = sizes
    tokens = q_ref.shape[0]
    half_tokens = tokens // 2
    rows = w_ref.shape[0]
    half = rows // 2
    width = q_ref.shape[1]
    total_features = w_ref.shape[1]
    heads = width // DH

    ctx = lax.axis_index("ctx")
    tp = lax.axis_index("tp")
    core = lax.rem(ctx, 2)
    y = lax.div(ctx, 2)
    x = lax.rem(tp, X)
    z = lax.div(tp, X)
    sibling = (y * 2 + 1 - core, tp)
    is_zero = core == 0

    def xs(step):
        return lax.rem(x + step + X, X)

    def zs(step):
        return lax.rem(z + step + 2 * Z, Z)

    def at_x(step):
        return (ctx, z * X + xs(step))

    def at_z(step):
        return (ctx, zs(step) * X + x)

    def at_y(place):
        return (place * 2 + core, tp)

    sign = 1 - 2 * core
    left, right, opp = xs(-1), xs(1), xs(2)

    def send(src, dst, send_sem, recv_sem, device):
        copy = pltpu.make_async_remote_copy(
            src_ref=src,
            dst_ref=dst,
            send_sem=send_sem,
            recv_sem=recv_sem,
            device_id=device,
            device_id_type=MESH,
        )
        copy.start()

    def arrived(ref, sem):
        pltpu.make_async_copy(ref, ref, sem).wait()

    loads = [
        pltpu.make_async_copy(src, dst, in_sems.at[index])
        for index, (src, dst) in enumerate(
            (
                (ld_in, ld_ref),
                (k_in, k_ref),
                (v_in, v_ref),
                (q_in, q_ref),
                (gate_in, gate_ref),
                (gain_in, gain_ref),
                (target_in, target_ref),
            )
        )
    ]
    for load in loads:
        load.start()
    barrier = pltpu.get_barrier_semaphore()
    partners = [sibling] + [at_x(step) for step in range(1, X)]
    partners += [at_z(step) for step in range(1, Z)]
    partners += [at_y(lax.rem(y + step, Y)) for step in range(1, Y)]
    for partner in partners:
        pl.semaphore_signal(barrier, inc=1, device_id=partner, device_id_type=MESH)

    def w_columns(block, x_to):
        start = pl.multiple_of((block * X + x_to) * width, width)
        return pl.ds(start, width)

    my_rows = pl.ds(pl.multiple_of(core * half, half), half)
    x_far = xs(sign)

    def w_far(block, carry):
        send(w_ref.at[my_rows, w_columns(block, opp)], wrelay.at[block], w_send.at[0], w_recv.at[0], (ctx, z * X + x_far))
        return carry

    def w_near(block, carry):
        send(w_ref.at[my_rows, w_columns(block, right)], wb.at[block, x, core], w_send.at[1], w_recv.at[1], at_x(1))
        send(w_ref.at[my_rows, w_columns(block, left)], wb.at[block, x, core], w_send.at[2], w_recv.at[2], at_x(-1))
        return carry

    def w_mine(block, carry):
        for part in range(2):
            pltpu.make_async_copy(
                w_ref.at[pl.ds(part * half, half), w_columns(block, x)], wb.at[block, x, part], w_own
            ).start()
        return carry

    row = lax.broadcasted_iota(jnp.int32, (tokens, tokens), 0)
    column = lax.broadcasted_iota(jnp.int32, (tokens, tokens), 1)
    causal = row >= column
    loads[0].wait()
    upto = jnp.where(row <= column, 1.0, 0.0).astype(BF16)
    rest = ld_ref[...]
    cum = jnp.zeros_like(rest)
    for _ in range(3):
        piece = rest.astype(BF16)
        cum = cum + nn(piece, upto)
        rest = rest - piece.astype(F32)
    cum_rows = [cum[h : h + 1, :] for h in range(heads)]
    cums = [as_columns(c) for c in cum_rows]
    totals = [c[tokens - 1 : tokens, :] for c in cums]
    bown[...] = jnp.zeros_like(bown)
    for h in range(heads):
        bown[h : h + 1, :] = totals[h]
    loads[1].wait()
    loads[2].wait()

    def lanes(h):
        return slice(h * DH, (h + 1) * DH)

    for h in range(heads):
        until_end[h] = jnp.exp(totals[h] - cums[h])
    order = (core, 1 - core)
    others = (1 - core, core)

    def any_lanes(h):
        return pl.ds(pl.multiple_of(h * DH, DH), DH)

    def of_core(pair):
        return jnp.where(is_zero, pair[0], pair[1])

    def scan_give(turn, mine, value):
        if mine:
            s_keep[turn] = value
        else:
            s_out[turn] = value.astype(BF16)
            send(s_out.at[turn], s_in.at[turn], s_send.at[turn], s_recv.at[turn], sibling)

    def scan_way(turn):
        step = 1 if turn == 0 else -1
        first_here = is_zero if turn == 0 else jnp.logical_not(is_zero)
        return step, first_here

    def decays(ref):
        return of_core((ref[0:1, :], ref[1:2, :]))

    def reaches(place):
        return jnp.logical_and(place >= 0, place < Y)

    def scan_send(turn):
        step, first_here = scan_way(turn)
        arrived(s_in.at[turn], s_recv.at[turn])
        mine = s_keep[turn]
        theirs = s_in[turn].astype(F32)
        first = jnp.where(first_here, mine, theirs)
        second = jnp.where(first_here, theirs, mine)
        s_keep[turn] = first
        b_second = jnp.where(first_here, decays(bsib), decays(bown))
        t_out[turn] = (jnp.exp(b_second) * first + second).astype(BF16)
        for distance in range(1, Y):
            place = y + step * distance

            @pl.when(reaches(place))
            def _():
                send(
                    t_out.at[turn],
                    t_in.at[turn, distance - 1],
                    t_send.at[turn, distance - 1],
                    t_recv.at[turn, distance - 1],
                    at_y(place),
                )

    def scan_end(turn):
        step, first_here = scan_way(turn)
        c_acc[...] = jnp.zeros_like(c_acc)
        d_acc[...] = jnp.zeros_like(d_acc)
        for distance in range(1, Y):
            place = y - step * distance

            @pl.when(reaches(place))
            def _():
                slot = t_in.at[turn, distance - 1]
                arrived(slot, t_recv.at[turn, distance - 1])
                between = d_acc[0:1, :]
                c_acc[...] += jnp.exp(between) * slot[...].astype(F32)
                d_acc[0:1, :] = between + decays(bchip.at[place])

        b_first = jnp.where(first_here, decays(bown), decays(bsib))
        carried = c_acc[...]
        after = jnp.exp(b_first) * carried + s_keep[turn]
        c_out[turn] = jnp.where(first_here, after, carried).astype(BF16)
        send(c_out.at[turn], state.at[turn, core], c_send.at[turn], c_recv.at[turn], sibling)
        state[turn, core] = jnp.where(first_here, carried, after).astype(BF16)

    def scan_take(turn):
        arrived(state.at[turn, 1 - core], c_recv.at[turn])

    pl.semaphore_wait(barrier, len(partners))
    send(bown, bsib, b_send, b_recv, sibling)
    for mine, h in enumerate(others):
        at = any_lanes(h)
        decayed = (k_ref[:, at].astype(F32) * until_end[h]).astype(BF16)
        kdec[:, at] = decayed
        scan_give(0, mine, tn(decayed, v_ref[:, at]))
    lax.fori_loop(0, Z, w_far, 0)
    lax.fori_loop(0, Z, w_near, 0)
    lax.fori_loop(0, Z, w_mine, 0)

    arrived(bsib, b_recv)
    bchip[y] = bown[...] + bsib[...]
    for distance in range(1, Y):
        place = lax.rem(y + distance, Y)
        send(bchip.at[y], bchip.at[y], bc_send, bc_recv.at[distance - 1], at_y(place))
    scan_send(0)

    for load in loads[3:]:
        load.wait()
    for h in range(heads):
        gaps = cums[h][:, 0:1] - cum_rows[h]
        decay = jnp.where(causal, jnp.exp(jnp.minimum(gaps, 0.0)), 0.0)
        weight[h] = decay
        probs[h] = (nt(q_ref[:, lanes(h)], k_ref[:, lanes(h)]) * decay).astype(BF16)
        att[:, lanes(h)] = nn(probs[h], v_ref[:, lanes(h)])
        from_start[h] = jnp.exp(cums[h])
        gate_open = jax.nn.sigmoid(gate_ref[:, lanes(h)].astype(F32))
        scale[:, lanes(h)] = gain_ref[:, lanes(h)] * gate_open

    for distance in range(1, Y):
        arrived(bchip.at[lax.rem(y - distance + Y, Y)], bc_recv.at[distance - 1])

    scan_end(0)

    far, near = Z // 2, Z - 1 - Z // 2
    hops = (far, near)
    ways = (sign, -sign)

    def u_part(way, step, part, h):
        return uall.at[zs(-ways[way] * step), part, h]

    def u_start(way, step, part, h):
        ref = u_part(way, step, part, h)
        send(ref, ref, u_send, u_recv.at[way, step, part, h], at_z(ways[way]))

    for turn, h in enumerate(order):
        if turn == 1:
            scan_take(0)
        for part in range(2):
            span = slice(part * half_tokens, (part + 1) * half_tokens)
            from_state = nn(q_ref[span, any_lanes(h)], state[0, h]) * from_start[h, span, :]
            attended = att[span, any_lanes(h)] + from_state
            att[span, any_lanes(h)] = attended
            uall[z, part, h] = (attended * scale[span, any_lanes(h)]).astype(BF16)
            for way in range(2):
                if hops[way] > 0:
                    u_start(way, 0, part, h)

    def small_share(turn, value):
        small_z[turn, 0] = value
        for step in range(1, Z):
            send(small_z.at[turn, 0], small_z.at[turn, step], sz_send, sz_recv.at[turn, step - 1], at_z(step))

    def small_cross(turn):
        for step in range(1, Z):
            arrived(small_z.at[turn, step], sz_recv.at[turn, step - 1])
        sum_z = small_z[turn, 0]
        for step in range(1, Z):
            sum_z = sum_z + small_z[turn, step]
        small_x[turn, 0] = sum_z
        for step in range(1, X):
            send(small_x.at[turn, 0], small_x.at[turn, step], sx_send, sx_recv.at[turn, step - 1], at_x(step))

    def small_sum(turn):
        for step in range(1, X):
            arrived(small_x.at[turn, step], sx_recv.at[turn, step - 1])
        sum_x = small_x[turn, 0]
        for step in range(1, X):
            sum_x = sum_x + small_x[turn, step]
        return sum_x

    squares = jnp.zeros((tokens, 1), F32)
    for h in range(heads):
        attended = att[:, lanes(h)]
        squares = squares + jnp.sum(attended * attended, axis=1, keepdims=True)
    small_share(0, as_row(squares))

    arrived(wrelay, w_recv.at[0])
    send(wrelay, wb.at[:, xs(-sign), core], w_send.at[3], w_recv.at[3], (ctx, z * X + x_far))

    for h in range(heads):
        qdec[:, lanes(h)] = (q_ref[:, lanes(h)].astype(F32) * from_start[h]).astype(BF16)
        closed[:, lanes(h)] = 1.0 - jax.nn.sigmoid(gate_ref[:, lanes(h)].astype(F32))

    def w_pair(source, sem, slot):
        ref = wb.at[:, source, core]
        arrived(ref, sem)
        send(ref, ref, ws_send.at[slot], ws_recv.at[slot], sibling)

    def w_block(block):
        return wb[block].reshape(X * rows, width)

    def u_block(block, part):
        return jnp.concatenate([uall[block, part, h] for h in range(heads)], axis=1)

    def accumulate(block, part):
        yacc[part] += nt(w_block(block), u_block(block, part)).reshape(yacc.shape[1:])

    def u_pass(step, part, some):
        for h in some:
            for way in range(2):
                if step < hops[way]:
                    arrived(u_part(way, step + 1, part, h), u_recv.at[way, step, part, h])
                    if step + 1 < hops[way]:
                        u_start(way, step + 1, part, h)

    def absorb(step):
        for way in range(2):
            if step < hops[way]:
                for part in range(2):
                    accumulate(zs(-ways[way] * (step + 1)), part)

    for step in range(far - 1):
        for h in order:
            for part in range(2):
                u_pass(step, part, (h,))
        if step == far - 3:
            w_pair(left, w_recv.at[1], 0)
            w_pair(right, w_recv.at[2], 1)
    if far < 3:
        w_pair(left, w_recv.at[1], 0)
        w_pair(right, w_recv.at[2], 1)
    w_pair(opp, w_recv.at[3], 2)
    small_cross(0)
    for part in range(2):
        arrived(wb.at[:, x, part], w_own)
    for slot, source in enumerate((left, right, opp)):
        arrived(wb.at[:, source, 1 - core], ws_recv.at[slot])
    for part in range(2):
        yacc[part] = nt(w_block(z), u_block(z, part)).reshape(yacc.shape[1:])
    for step in range(far - 1):
        absorb(step)

    steps = (2, 1, 3)

    def y_start(part, step):
        ystage[part, step - 1] = yacc[part, xs(step)].astype(BF16)
        send(
            ystage.at[part, step - 1],
            yrecv.at[part, step - 1],
            y_send,
            y_recv.at[part, step - 1],
            at_x(step),
        )

    def y_arrived(part, step):
        arrived(yrecv.at[part, step - 1], y_recv.at[part, step - 1])
        return yrecv[part, step - 1].astype(F32)

    for part in range(2):
        u_pass(far - 1, part, order)
        last = zs(sign * far)
        last_u = u_block(last, part)

        def finish(rows_of):
            block = wb[last, rows_of].reshape(rows, width)
            yacc[part, rows_of] += nt(block, last_u)

        for step in steps:
            finish(xs(step))
            y_start(part, step)
        finish(x)

    inv_rms = lax.rsqrt(small_sum(0) / total_features + EPS)

    def g_arrived(part, step):
        arrived(gx.at[part, xs(-step)], g_recv.at[part, step - 1])

    products = []
    for part in range(2):
        span = slice(part * half_tokens, (part + 1) * half_tokens)
        total = yacc[part, x]
        for step in (1, 3, 2):
            total = total + y_arrived(part, step)
        rounded = (total * inv_rms[:, span]).astype(BF16)
        grad = (rounded.astype(F32) - target_ref[:, span].astype(F32)).astype(BF16)
        gx[part, x] = grad
        for step in steps:
            ref = gx.at[part, x]
            send(ref, ref, g_send, g_recv.at[part, step - 1], at_x(step))
        out_ref[:, span] = rounded
        products.append(jnp.sum(grad.astype(F32) * total, axis=0, keepdims=True))
    small_share(1, jnp.concatenate(products, axis=1))

    eye = identity(half_tokens)

    def feature_part(block, part):
        return nn(gall[part], w_block(block))

    def f_slot(way, step):
        return way * far + step

    def f_start(way, step, part, h, value):
        slot = f_slot(way, step)
        fstage[slot, part, h] = value.astype(BF16)
        send(
            fstage.at[slot, part, h],
            frecv.at[slot, part, h],
            f_send,
            f_recv.at[slot, part, h],
            at_z(ways[way]),
        )

    def f_arrived(way, step, part, h):
        slot = f_slot(way, step)
        arrived(frecv.at[slot, part, h], f_recv.at[slot, part, h])
        return frecv[slot, part, h].astype(F32)

    def by_head(value):
        first, second = value[:, lanes(0)], value[:, lanes(1)]
        return jnp.where(is_zero, second, first), jnp.where(is_zero, first, second)

    for part in range(2):
        for x_step in (1, 3, 2):
            g_arrived(part, x_step)
        gall[part] = nt(eye, gx[part].reshape(X * rows, half_tokens)).astype(BF16)
        sums = [by_head(feature_part(zs(ways[way] * hops[way]), part)) if hops[way] > 0 else None for way in range(2)]
        for turn in range(heads):
            for way in range(2):
                if hops[way] > 0:
                    f_start(way, 0, part, turn, sums[way][turn])
    small_cross(1)

    def feature_both(block):
        return by_head(nn(gall[...].reshape(tokens, X * rows), w_block(block)))

    for step in range(1, far):
        sums = [feature_both(zs(ways[way] * (hops[way] - step))) if step < hops[way] else None for way in range(2)]
        for part in range(2):
            span = slice(part * half_tokens, (part + 1) * half_tokens)
            for turn in range(heads):
                for way in range(2):
                    if step < hops[way]:
                        value = sums[way][turn][span, :] + f_arrived(way, step - 1, part, turn)
                        f_start(way, step, part, turn, value)

    own_feature = feature_both(z)
    mean_product = as_columns(small_sum(1) / total_features)
    inv = as_columns(inv_rms)

    for turn, h in enumerate(others):
        at = any_lanes(h)
        pieces = []
        for part in range(2):
            value = own_feature[turn][part * half_tokens : (part + 1) * half_tokens, :]
            for way in range(2):
                if hops[way] > 0:
                    value = value + f_arrived(way, hops[way] - 1, part, turn)
            pieces.append(value)
        attended = att[:, at]
        normed_grad = jnp.concatenate(pieces, axis=0) * scale[:, at]
        grad = (inv * normed_grad - inv * inv * inv * attended * mean_product).astype(BF16)
        agrad[:, at] = grad
        scan_give(1, turn, tn(qdec[:, at], grad))
        gg_ref[:, at] = (normed_grad * attended * inv * closed[:, at]).astype(BF16)

    for h in range(heads):
        grad = agrad[:, lanes(h)]
        score_grad = (nt(grad, v_ref[:, lanes(h)]) * weight[h]).astype(BF16)
        if h == 0:
            scan_send(1)
        qg_ref[:, lanes(h)] = (
            nn(score_grad, k_ref[:, lanes(h)]) + from_start[h] * nt(grad, state[0, h])
        ).astype(BF16)
        klocal[:, lanes(h)] = tn(score_grad, q_ref[:, lanes(h)])
        vlocal[:, lanes(h)] = tn(probs[h], grad)
    for index in range(4):
        arrived(wrelay, w_send.at[index])
    for index in range(3):
        arrived(wrelay, ws_send.at[index])
    arrived(uall.at[pl.ds(0, Z - 1)], u_send)
    arrived(fstage, f_send)
    arrived(ystage, y_send)
    arrived(ystage, g_send)
    arrived(bown, b_send)
    if Y > 1:
        arrived(bchip.at[pl.ds(0, Y - 1)], bc_send)
    arrived(small_z.at[:, pl.ds(0, Z - 1)], sz_send)
    arrived(small_x.at[:, pl.ds(0, X - 1)], sx_send)
    for turn in range(2):
        arrived(s_out.at[turn], s_send.at[turn])

    def scan_sent(turn):
        step, _ = scan_way(turn)
        for distance in range(1, Y):

            @pl.when(reaches(y + step * distance))
            def _():
                arrived(t_out.at[turn], t_send.at[turn, distance - 1])

    scan_sent(0)
    arrived(c_out.at[0], c_send.at[0])

    scan_end(1)
    for turn, h in enumerate(order):
        if turn == 1:
            scan_sent(1)
            scan_take(1)
        at = any_lanes(h)
        later = state[1, h]
        kg_ref[:, at] = (klocal[:, at] + until_end[h] * nt(v_ref[:, at], later)).astype(BF16)
        vg_ref[:, at] = (vlocal[:, at] + nn(kdec[:, at], later)).astype(BF16)

    arrived(c_out.at[1], c_send.at[1])


def store(*refs):
    *refs, sems = refs
    count = len(refs) // 2
    copies = [pltpu.make_async_copy(refs[i], refs[count + i], sems.at[i]) for i in range(count)]
    for copy in copies:
        copy.start()
    for copy in copies:
        copy.wait()


def on_device(chips, queries, keys, values, log_decay, gate, norm_gain, out_weight, target):
    Y, Z = chips
    tokens, width = queries.shape
    rows, features = out_weight.shape
    half = rows // 2
    far = Z // 2
    vmem = pltpu.VMEM
    dma = pltpu.SemaphoreType.DMA
    scratch = [
        vmem((tokens, width), BF16),
        vmem((tokens, width), BF16),
        vmem((tokens, width), BF16),
        vmem((width // DH, tokens), F32),
        vmem((tokens, width), BF16),
        vmem((1, width), F32),
        vmem((rows, tokens), BF16),
        dma((7,)),
        vmem((Z, X, 2, half, width), BF16),
        vmem((Z, half, width), BF16),
        vmem((Z, 2, width // DH, tokens // 2, DH), BF16),
        vmem((2, X, rows, tokens // 2), F32),
        vmem((2, X - 1, rows, tokens // 2), BF16),
        vmem((2, X - 1, rows, tokens // 2), BF16),
        vmem((2, X, rows, tokens // 2), BF16),
        vmem((2, tokens // 2, X * rows), BF16),
        vmem((Z - 1, 2, 2, tokens // 2, DH), BF16),
        vmem((Z - 1, 2, 2, tokens // 2, DH), BF16),
        vmem((width // DH, tokens, tokens), F32),
        vmem((width // DH, tokens, tokens), BF16),
        vmem((tokens, width), BF16),
        vmem((tokens, width), F32),
        vmem((tokens, width), F32),
        vmem((tokens, width), F32),
        vmem((tokens, width), BF16),
        vmem((width // DH, tokens, DH), F32),
        vmem((width // DH, tokens, DH), F32),
        vmem((tokens, width), BF16),
        vmem((tokens, width), F32),
        vmem((tokens, width), F32),
        vmem((8, 128), F32),
        vmem((8, 128), F32),
        vmem((Y, 8, 128), F32),
        vmem((2, DH, DH), BF16),
        vmem((2, DH, DH), BF16),
        vmem((2, DH, DH), F32),
        vmem((2, DH, DH), BF16),
        vmem((2, max(Y - 1, 1), DH, DH), BF16),
        vmem((DH, DH), F32),
        vmem((8, 128), F32),
        vmem((2, DH, DH), BF16),
        vmem((2, 2, DH, DH), BF16),
        vmem((2, Z, 1, tokens), F32),
        vmem((2, X, 1, tokens), F32),
        dma((4,)),
        dma((4,)),
        dma,
        dma((3,)),
        dma((3,)),
        dma,
        dma((2, far, 2, 2)),
        dma,
        dma((2, X - 1)),
        dma,
        dma((2, X - 1)),
        dma,
        dma((Z - 1, 2, 2)),
        dma,
        dma,
        dma,
        dma((max(Y - 1, 1),)),
        dma((2,)),
        dma((2,)),
        dma((2, max(Y - 1, 1))),
        dma((2, max(Y - 1, 1))),
        dma((2,)),
        dma((2,)),
        dma,
        dma((2, Z - 1)),
        dma,
        dma((2, X - 1)),
    ]
    in_vmem = pl.BlockSpec(memory_space=pltpu.VMEM)
    in_hbm = pl.BlockSpec(memory_space=pltpu.HBM)
    shapes = [(rows, tokens)] + [(tokens, width)] * 4
    operands = (queries, keys, values, log_decay.T, gate, norm_gain.reshape(1, width), out_weight, target.T)
    results = pl.pallas_call(
        functools.partial(kernel, chips),
        out_shape=tuple(pltpu.VMEM(shape, BF16) for shape in shapes),
        in_specs=[in_hbm] * 8,
        out_specs=(in_vmem,) * 5,
        scratch_shapes=scratch,
        compiler_params=pltpu.CompilerParams(
            collective_id=0, has_side_effects=True, vmem_limit_bytes=48 * 1024 * 1024
        ),
        cost_estimate=pl.CostEstimate(flops=2 * 10**9, bytes_accessed=8 * 10**6, transcendentals=10**6),
        name="attention_layer",
    )(*[pltpu.with_memory_space_constraint(operand, pltpu.HBM) for operand in operands])
    output, *grads = pl.pallas_call(
        store,
        out_shape=tuple(jax.ShapeDtypeStruct(shape, BF16) for shape in shapes),
        in_specs=[in_vmem] * 5,
        out_specs=(in_hbm,) * 5,
        scratch_shapes=[dma((5,))],
        compiler_params=pltpu.CompilerParams(vmem_limit_bytes=4 * 1024 * 1024),
        name="store",
    )(*results)
    return (output.T, *grads)


def solution(mesh):
    chips = (mesh.shape["ctx"] // 2, mesh.shape["tp"] // X)
    return jax.shard_map(
        functools.partial(on_device, chips),
        mesh=mesh,
        in_specs=(
            P("ctx", "tp"),
            P("ctx", "tp"),
            P("ctx", "tp"),
            P("ctx", "tp"),
            P("ctx", "tp"),
            P("tp"),
            P("tp", None),
            P("ctx", "tp"),
        ),
        out_specs=(P("ctx", "tp"),) * 5,
        check_vma=False,
    )
```

```python
import functools

import jax
import jax.numpy as jnp
from jax import lax
from jax.experimental import pallas as pl
from jax.experimental.pallas import tpu as pltpu
from jax.sharding import PartitionSpec as P

DH = 128
EPS = 1e-06
MESH = pl.DeviceIdType.MESH
F32 = jnp.float32
BF16 = jnp.bfloat16
X = 4


def nn(a, b):
    return lax.dot_general(a, b, (((1,), (0,)), ((), ())), preferred_element_type=F32)


def nt(a, b):
    return lax.dot_general(a, b, (((1,), (1,)), ((), ())), preferred_element_type=F32)


def tn(a, b):
    return lax.dot_general(a, b, (((0,), (0,)), ((), ())), preferred_element_type=F32)


def identity(size):
    row = lax.broadcasted_iota(jnp.int32, (size, size), 0)
    column = lax.broadcasted_iota(jnp.int32, (size, size), 1)
    return jnp.where(row == column, 1.0, 0.0).astype(BF16)


def as_row(column):
    return jnp.broadcast_to(column, (column.shape[0], 128)).T[0:1, :]


def as_columns(row):
    return jnp.broadcast_to(row, (128, row.shape[1])).T


def kernel(
    sizes,
    q_in,
    k_in,
    v_in,
    ld_in,
    gate_in,
    gain_in,
    w_ref,
    target_in,
    out_ref,
    qg_ref,
    kg_ref,
    vg_ref,
    gg_ref,
    q_ref,
    k_ref,
    v_ref,
    ld_ref,
    gate_ref,
    gain_ref,
    target_ref,
    in_sems,
    wb,
    wrelay,
    uall,
    yacc,
    ystage,
    yrecv,
    gx,
    gall,
    fstage,
    frecv,
    weight,
    probs,
    kdec,
    att,
    klocal,
    vlocal,
    agrad,
    until_end,
    from_start,
    qdec,
    scale,
    closed,
    bown,
    bsib,
    bchip,
    s_out,
    s_in,
    s_keep,
    t_out,
    t_in,
    c_acc,
    d_acc,
    c_out,
    state,
    small_z,
    small_x,
    w_send,
    w_recv,
    w_own,
    ws_send,
    ws_recv,
    u_send,
    u_recv,
    y_send,
    y_recv,
    g_send,
    g_recv,
    f_send,
    f_recv,
    b_send,
    b_recv,
    bc_send,
    bc_recv,
    s_send,
    s_recv,
    t_send,
    t_recv,
    c_send,
    c_recv,
    sz_send,
    sz_recv,
    sx_send,
    sx_recv,
):
    Y, Z = sizes
    tokens = q_ref.shape[0]
    half_tokens = tokens // 2
    rows = w_ref.shape[0]
    half = rows // 2
    width = q_ref.shape[1]
    total_features = w_ref.shape[1]
    heads = width // DH

    ctx = lax.axis_index("ctx")
    tp = lax.axis_index("tp")
    core = lax.rem(ctx, 2)
    y = lax.div(ctx, 2)
    x = lax.rem(tp, X)
    z = lax.div(tp, X)
    sibling = (y * 2 + 1 - core, tp)
    is_zero = core == 0

    def xs(step):
        return lax.rem(x + step + X, X)

    def zs(step):
        return lax.rem(z + step + 2 * Z, Z)

    def at_x(step):
        return (ctx, z * X + xs(step))

    def at_z(step):
        return (ctx, zs(step) * X + x)

    def at_y(place):
        return (place * 2 + core, tp)

    sign = 1 - 2 * core
    left, right, opp = xs(-1), xs(1), xs(2)

    def send(src, dst, send_sem, recv_sem, device):
        copy = pltpu.make_async_remote_copy(
            src_ref=src,
            dst_ref=dst,
            send_sem=send_sem,
            recv_sem=recv_sem,
            device_id=device,
            device_id_type=MESH,
        )
        copy.start()

    def arrived(ref, sem):
        pltpu.make_async_copy(ref, ref, sem).wait()

    loads = [
        pltpu.make_async_copy(src, dst, in_sems.at[index])
        for index, (src, dst) in enumerate(
            (
                (ld_in, ld_ref),
                (k_in, k_ref),
                (v_in, v_ref),
                (q_in, q_ref),
                (gate_in, gate_ref),
                (gain_in, gain_ref),
                (target_in, target_ref),
            )
        )
    ]
    for load in loads:
        load.start()
    barrier = pltpu.get_barrier_semaphore()
    partners = [sibling] + [at_x(step) for step in range(1, X)]
    partners += [at_z(step) for step in range(1, Z)]
    partners += [at_y(lax.rem(y + step, Y)) for step in range(1, Y)]
    for partner in partners:
        pl.semaphore_signal(barrier, inc=1, device_id=partner, device_id_type=MESH)

    def w_columns(block, x_to):
        start = pl.multiple_of((block * X + x_to) * width, width)
        return pl.ds(start, width)

    my_rows = pl.ds(pl.multiple_of(core * half, half), half)
    x_far = xs(sign)

    def w_far(block, carry):
        send(w_ref.at[my_rows, w_columns(block, opp)], wrelay.at[block], w_send.at[0], w_recv.at[0], (ctx, z * X + x_far))
        return carry

    def w_near(block, carry):
        send(w_ref.at[my_rows, w_columns(block, right)], wb.at[block, x, core], w_send.at[1], w_recv.at[1], at_x(1))
        send(w_ref.at[my_rows, w_columns(block, left)], wb.at[block, x, core], w_send.at[2], w_recv.at[2], at_x(-1))
        return carry

    def w_mine(block, carry):
        for part in range(2):
            pltpu.make_async_copy(
                w_ref.at[pl.ds(part * half, half), w_columns(block, x)], wb.at[block, x, part], w_own
            ).start()
        return carry

    row = lax.broadcasted_iota(jnp.int32, (tokens, tokens), 0)
    column = lax.broadcasted_iota(jnp.int32, (tokens, tokens), 1)
    causal = row >= column
    loads[0].wait()
    upto = jnp.where(row <= column, 1.0, 0.0).astype(BF16)
    rest = ld_ref[...]
    cum = jnp.zeros_like(rest)
    for _ in range(3):
        piece = rest.astype(BF16)
        cum = cum + nn(piece, upto)
        rest = rest - piece.astype(F32)
    cum_rows = [cum[h : h + 1, :] for h in range(heads)]
    cums = [as_columns(c) for c in cum_rows]
    totals = [c[tokens - 1 : tokens, :] for c in cums]
    bown[...] = jnp.zeros_like(bown)
    for h in range(heads):
        bown[h : h + 1, :] = totals[h]
    loads[1].wait()
    loads[2].wait()

    def lanes(h):
        return slice(h * DH, (h + 1) * DH)

    for h in range(heads):
        until_end[h] = jnp.exp(totals[h] - cums[h])
    order = (core, 1 - core)
    others = (1 - core, core)

    def any_lanes(h):
        return pl.ds(pl.multiple_of(h * DH, DH), DH)

    def of_core(pair):
        return jnp.where(is_zero, pair[0], pair[1])

    def scan_give(turn, mine, value):
        if mine:
            s_keep[turn] = value
        else:
            s_out[turn] = value.astype(BF16)
            send(s_out.at[turn], s_in.at[turn], s_send.at[turn], s_recv.at[turn], sibling)

    def scan_way(turn):
        step = 1 if turn == 0 else -1
        first_here = is_zero if turn == 0 else jnp.logical_not(is_zero)
        return step, first_here

    def decays(ref):
        return of_core((ref[0:1, :], ref[1:2, :]))

    def reaches(place):
        return jnp.logical_and(place >= 0, place < Y)

    def scan_send(turn):
        step, first_here = scan_way(turn)
        arrived(s_in.at[turn], s_recv.at[turn])
        mine = s_keep[turn]
        theirs = s_in[turn].astype(F32)
        first = jnp.where(first_here, mine, theirs)
        second = jnp.where(first_here, theirs, mine)
        s_keep[turn] = first
        b_second = jnp.where(first_here, decays(bsib), decays(bown))
        t_out[turn] = (jnp.exp(b_second) * first + second).astype(BF16)
        for distance in range(1, Y):
            place = y + step * distance

            @pl.when(reaches(place))
            def _():
                send(
                    t_out.at[turn],
                    t_in.at[turn, distance - 1],
                    t_send.at[turn, distance - 1],
                    t_recv.at[turn, distance - 1],
                    at_y(place),
                )

    def scan_end(turn):
        step, first_here = scan_way(turn)
        c_acc[...] = jnp.zeros_like(c_acc)
        d_acc[...] = jnp.zeros_like(d_acc)
        for distance in range(1, Y):
            place = y - step * distance

            @pl.when(reaches(place))
            def _():
                slot = t_in.at[turn, distance - 1]
                arrived(slot, t_recv.at[turn, distance - 1])
                between = d_acc[0:1, :]
                c_acc[...] += jnp.exp(between) * slot[...].astype(F32)
                d_acc[0:1, :] = between + decays(bchip.at[place])

        b_first = jnp.where(first_here, decays(bown), decays(bsib))
        carried = c_acc[...]
        after = jnp.exp(b_first) * carried + s_keep[turn]
        c_out[turn] = jnp.where(first_here, after, carried).astype(BF16)
        send(c_out.at[turn], state.at[turn, core], c_send.at[turn], c_recv.at[turn], sibling)
        state[turn, core] = jnp.where(first_here, carried, after).astype(BF16)

    def scan_take(turn):
        arrived(state.at[turn, 1 - core], c_recv.at[turn])

    pl.semaphore_wait(barrier, len(partners))
    send(bown, bsib, b_send, b_recv, sibling)
    for mine, h in enumerate(others):
        at = any_lanes(h)
        decayed = (k_ref[:, at].astype(F32) * until_end[h]).astype(BF16)
        kdec[:, at] = decayed
        scan_give(0, mine, tn(decayed, v_ref[:, at]))
    lax.fori_loop(0, Z, w_far, 0)
    lax.fori_loop(0, Z, w_near, 0)
    lax.fori_loop(0, Z, w_mine, 0)

    arrived(bsib, b_recv)
    bchip[y] = bown[...] + bsib[...]
    for distance in range(1, Y):
        place = lax.rem(y + distance, Y)
        send(bchip.at[y], bchip.at[y], bc_send, bc_recv.at[distance - 1], at_y(place))
    scan_send(0)

    for load in loads[3:]:
        load.wait()
    for h in range(heads):
        gaps = cums[h][:, 0:1] - cum_rows[h]
        decay = jnp.where(causal, jnp.exp(jnp.minimum(gaps, 0.0)), 0.0)
        weight[h] = decay
        probs[h] = (nt(q_ref[:, lanes(h)], k_ref[:, lanes(h)]) * decay).astype(BF16)
        att[:, lanes(h)] = nn(probs[h], v_ref[:, lanes(h)])
        from_start[h] = jnp.exp(cums[h])
        gate_open = jax.nn.sigmoid(gate_ref[:, lanes(h)].astype(F32))
        scale[:, lanes(h)] = gain_ref[:, lanes(h)] * gate_open

    for distance in range(1, Y):
        arrived(bchip.at[lax.rem(y - distance + Y, Y)], bc_recv.at[distance - 1])

    scan_end(0)

    far, near = Z // 2, Z - 1 - Z // 2
    hops = (far, near)
    ways = (sign, -sign)

    def u_part(way, step, part, h):
        return uall.at[zs(-ways[way] * step), part, h]

    def u_start(way, step, part, h):
        ref = u_part(way, step, part, h)
        send(ref, ref, u_send, u_recv.at[way, step, part, h], at_z(ways[way]))

    for turn, h in enumerate(order):
        if turn == 1:
            scan_take(0)
        for part in range(2):
            span = slice(part * half_tokens, (part + 1) * half_tokens)
            from_state = nn(q_ref[span, any_lanes(h)], state[0, h]) * from_start[h, span, :]
            attended = att[span, any_lanes(h)] + from_state
            att[span, any_lanes(h)] = attended
            uall[z, part, h] = (attended * scale[span, any_lanes(h)]).astype(BF16)
            for way in range(2):
                if hops[way] > 0:
                    u_start(way, 0, part, h)

    def small_share(turn, value):
        small_z[turn, 0] = value
        for step in range(1, Z):
            send(small_z.at[turn, 0], small_z.at[turn, step], sz_send, sz_recv.at[turn, step - 1], at_z(step))

    def small_cross(turn):
        for step in range(1, Z):
            arrived(small_z.at[turn, step], sz_recv.at[turn, step - 1])
        sum_z = small_z[turn, 0]
        for step in range(1, Z):
            sum_z = sum_z + small_z[turn, step]
        small_x[turn, 0] = sum_z
        for step in range(1, X):
            send(small_x.at[turn, 0], small_x.at[turn, step], sx_send, sx_recv.at[turn, step - 1], at_x(step))

    def small_sum(turn):
        for step in range(1, X):
            arrived(small_x.at[turn, step], sx_recv.at[turn, step - 1])
        sum_x = small_x[turn, 0]
        for step in range(1, X):
            sum_x = sum_x + small_x[turn, step]
        return sum_x

    squares = jnp.zeros((tokens, 1), F32)
    for h in range(heads):
        attended = att[:, lanes(h)]
        squares = squares + jnp.sum(attended * attended, axis=1, keepdims=True)
    small_share(0, as_row(squares))

    arrived(wrelay, w_recv.at[0])
    send(wrelay, wb.at[:, xs(-sign), core], w_send.at[3], w_recv.at[3], (ctx, z * X + x_far))

    for h in range(heads):
        qdec[:, lanes(h)] = (q_ref[:, lanes(h)].astype(F32) * from_start[h]).astype(BF16)
        closed[:, lanes(h)] = 1.0 - jax.nn.sigmoid(gate_ref[:, lanes(h)].astype(F32))

    def w_pair(source, sem, slot):
        ref = wb.at[:, source, core]
        arrived(ref, sem)
        send(ref, ref, ws_send.at[slot], ws_recv.at[slot], sibling)

    def w_block(block):
        return wb[block].reshape(X * rows, width)

    def u_block(block, part):
        return jnp.concatenate([uall[block, part, h] for h in range(heads)], axis=1)

    def accumulate(block, part):
        yacc[part] += nt(w_block(block), u_block(block, part)).reshape(yacc.shape[1:])

    def u_pass(step, part, some):
        for h in some:
            for way in range(2):
                if step < hops[way]:
                    arrived(u_part(way, step + 1, part, h), u_recv.at[way, step, part, h])
                    if step + 1 < hops[way]:
                        u_start(way, step + 1, part, h)

    def absorb(step):
        for way in range(2):
            if step < hops[way]:
                for part in range(2):
                    accumulate(zs(-ways[way] * (step + 1)), part)

    def w_forward():
        small_cross(0)
        w_pair(left, w_recv.at[1], 0)
        w_pair(right, w_recv.at[2], 1)
        w_pair(opp, w_recv.at[3], 2)

    for step in range(far - 1):
        if step == far - 2:
            w_forward()
        for h in order:
            for part in range(2):
                u_pass(step, part, (h,))
    if far < 2:
        w_forward()
    for part in range(2):
        arrived(wb.at[:, x, part], w_own)
    for slot, source in enumerate((left, right, opp)):
        arrived(wb.at[:, source, 1 - core], ws_recv.at[slot])
    for part in range(2):
        yacc[part] = nt(w_block(z), u_block(z, part)).reshape(yacc.shape[1:])
    for step in range(far - 1):
        absorb(step)

    steps = (2, 1, 3)

    def y_start(part, step):
        ystage[part, step - 1] = yacc[part, xs(step)].astype(BF16)
        send(
            ystage.at[part, step - 1],
            yrecv.at[part, step - 1],
            y_send,
            y_recv.at[part, step - 1],
            at_x(step),
        )

    def y_arrived(part, step):
        arrived(yrecv.at[part, step - 1], y_recv.at[part, step - 1])
        return yrecv[part, step - 1].astype(F32)

    for part in range(2):
        u_pass(far - 1, part, order)
        last = zs(sign * far)
        last_u = u_block(last, part)

        def finish(rows_of):
            block = wb[last, rows_of].reshape(rows, width)
            yacc[part, rows_of] += nt(block, last_u)

        for step in steps:
            finish(xs(step))
            y_start(part, step)
        finish(x)

    inv_rms = lax.rsqrt(small_sum(0) / total_features + EPS)

    def g_arrived(part, step):
        arrived(gx.at[part, xs(-step)], g_recv.at[part, step - 1])

    products = []
    for part in range(2):
        span = slice(part * half_tokens, (part + 1) * half_tokens)
        total = yacc[part, x]
        for step in (1, 3, 2):
            total = total + y_arrived(part, step)
        rounded = (total * inv_rms[:, span]).astype(BF16)
        grad = (rounded.astype(F32) - target_ref[:, span].astype(F32)).astype(BF16)
        gx[part, x] = grad
        for step in steps:
            ref = gx.at[part, x]
            send(ref, ref, g_send, g_recv.at[part, step - 1], at_x(step))
        out_ref[:, span] = rounded
        products.append(jnp.sum(grad.astype(F32) * total, axis=0, keepdims=True))
    small_share(1, jnp.concatenate(products, axis=1))

    eye = identity(half_tokens)

    def feature_part(block, part):
        return nn(gall[part], w_block(block))

    def f_slot(way, step):
        return way * far + step

    def f_start(way, step, part, h, value):
        slot = f_slot(way, step)
        fstage[slot, part, h] = value.astype(BF16)
        send(
            fstage.at[slot, part, h],
            frecv.at[slot, part, h],
            f_send,
            f_recv.at[slot, part, h],
            at_z(ways[way]),
        )

    def f_arrived(way, step, part, h):
        slot = f_slot(way, step)
        arrived(frecv.at[slot, part, h], f_recv.at[slot, part, h])
        return frecv[slot, part, h].astype(F32)

    def by_head(value):
        first, second = value[:, lanes(0)], value[:, lanes(1)]
        return jnp.where(is_zero, second, first), jnp.where(is_zero, first, second)

    for part in range(2):
        for x_step in (1, 3, 2):
            g_arrived(part, x_step)
        gall[part] = nt(eye, gx[part].reshape(X * rows, half_tokens)).astype(BF16)
        sums = [by_head(feature_part(zs(ways[way] * hops[way]), part)) if hops[way] > 0 else None for way in range(2)]
        for turn in range(heads):
            for way in range(2):
                if hops[way] > 0:
                    f_start(way, 0, part, turn, sums[way][turn])
    small_cross(1)

    def feature_both(block):
        return by_head(nn(gall[...].reshape(tokens, X * rows), w_block(block)))

    for step in range(1, far):
        sums = [feature_both(zs(ways[way] * (hops[way] - step))) if step < hops[way] else None for way in range(2)]
        for part in range(2):
            span = slice(part * half_tokens, (part + 1) * half_tokens)
            for turn in range(heads):
                for way in range(2):
                    if step < hops[way]:
                        value = sums[way][turn][span, :] + f_arrived(way, step - 1, part, turn)
                        f_start(way, step, part, turn, value)

    own_feature = feature_both(z)
    mean_product = as_columns(small_sum(1) / total_features)
    inv = as_columns(inv_rms)

    for turn, h in enumerate(others):
        at = any_lanes(h)
        pieces = []
        for part in range(2):
            value = own_feature[turn][part * half_tokens : (part + 1) * half_tokens, :]
            for way in range(2):
                if hops[way] > 0:
                    value = value + f_arrived(way, hops[way] - 1, part, turn)
            pieces.append(value)
        attended = att[:, at]
        normed_grad = jnp.concatenate(pieces, axis=0) * scale[:, at]
        grad = (inv * normed_grad - inv * inv * inv * attended * mean_product).astype(BF16)
        agrad[:, at] = grad
        scan_give(1, turn, tn(qdec[:, at], grad))
        gg_ref[:, at] = (normed_grad * attended * inv * closed[:, at]).astype(BF16)

    for h in range(heads):
        grad = agrad[:, lanes(h)]
        score_grad = (nt(grad, v_ref[:, lanes(h)]) * weight[h]).astype(BF16)
        if h == 0:
            scan_send(1)
        qg_ref[:, lanes(h)] = (
            nn(score_grad, k_ref[:, lanes(h)]) + from_start[h] * nt(grad, state[0, h])
        ).astype(BF16)
        klocal[:, lanes(h)] = tn(score_grad, q_ref[:, lanes(h)])
        vlocal[:, lanes(h)] = tn(probs[h], grad)
    for index in range(4):
        arrived(wrelay, w_send.at[index])
    for index in range(3):
        arrived(wrelay, ws_send.at[index])
    arrived(uall.at[pl.ds(0, Z - 1)], u_send)
    arrived(fstage, f_send)
    arrived(ystage, y_send)
    arrived(ystage, g_send)
    arrived(bown, b_send)
    if Y > 1:
        arrived(bchip.at[pl.ds(0, Y - 1)], bc_send)
    arrived(small_z.at[:, pl.ds(0, Z - 1)], sz_send)
    arrived(small_x.at[:, pl.ds(0, X - 1)], sx_send)
    for turn in range(2):
        arrived(s_out.at[turn], s_send.at[turn])

    def scan_sent(turn):
        step, _ = scan_way(turn)
        for distance in range(1, Y):

            @pl.when(reaches(y + step * distance))
            def _():
                arrived(t_out.at[turn], t_send.at[turn, distance - 1])

    scan_sent(0)
    arrived(c_out.at[0], c_send.at[0])

    scan_end(1)
    for turn, h in enumerate(order):
        if turn == 1:
            scan_sent(1)
            scan_take(1)
        at = any_lanes(h)
        later = state[1, h]
        kg_ref[:, at] = (klocal[:, at] + until_end[h] * nt(v_ref[:, at], later)).astype(BF16)
        vg_ref[:, at] = (vlocal[:, at] + nn(kdec[:, at], later)).astype(BF16)

    arrived(c_out.at[1], c_send.at[1])


def store(*refs):
    *refs, sems = refs
    count = len(refs) // 2
    copies = [pltpu.make_async_copy(refs[i], refs[count + i], sems.at[i]) for i in range(count)]
    for copy in copies:
        copy.start()
    for copy in copies:
        copy.wait()


def on_device(chips, queries, keys, values, log_decay, gate, norm_gain, out_weight, target):
    Y, Z = chips
    tokens, width = queries.shape
    rows, features = out_weight.shape
    half = rows // 2
    far = Z // 2
    vmem = pltpu.VMEM
    dma = pltpu.SemaphoreType.DMA
    scratch = [
        vmem((tokens, width), BF16),
        vmem((tokens, width), BF16),
        vmem((tokens, width), BF16),
        vmem((width // DH, tokens), F32),
        vmem((tokens, width), BF16),
        vmem((1, width), F32),
        vmem((rows, tokens), BF16),
        dma((7,)),
        vmem((Z, X, 2, half, width), BF16),
        vmem((Z, half, width), BF16),
        vmem((Z, 2, width // DH, tokens // 2, DH), BF16),
        vmem((2, X, rows, tokens // 2), F32),
        vmem((2, X - 1, rows, tokens // 2), BF16),
        vmem((2, X - 1, rows, tokens // 2), BF16),
        vmem((2, X, rows, tokens // 2), BF16),
        vmem((2, tokens // 2, X * rows), BF16),
        vmem((Z - 1, 2, 2, tokens // 2, DH), BF16),
        vmem((Z - 1, 2, 2, tokens // 2, DH), BF16),
        vmem((width // DH, tokens, tokens), F32),
        vmem((width // DH, tokens, tokens), BF16),
        vmem((tokens, width), BF16),
        vmem((tokens, width), F32),
        vmem((tokens, width), F32),
        vmem((tokens, width), F32),
        vmem((tokens, width), BF16),
        vmem((width // DH, tokens, DH), F32),
        vmem((width // DH, tokens, DH), F32),
        vmem((tokens, width), BF16),
        vmem((tokens, width), F32),
        vmem((tokens, width), F32),
        vmem((8, 128), F32),
        vmem((8, 128), F32),
        vmem((Y, 8, 128), F32),
        vmem((2, DH, DH), BF16),
        vmem((2, DH, DH), BF16),
        vmem((2, DH, DH), F32),
        vmem((2, DH, DH), BF16),
        vmem((2, max(Y - 1, 1), DH, DH), BF16),
        vmem((DH, DH), F32),
        vmem((8, 128), F32),
        vmem((2, DH, DH), BF16),
        vmem((2, 2, DH, DH), BF16),
        vmem((2, Z, 1, tokens), F32),
        vmem((2, X, 1, tokens), F32),
        dma((4,)),
        dma((4,)),
        dma,
        dma((3,)),
        dma((3,)),
        dma,
        dma((2, far, 2, 2)),
        dma,
        dma((2, X - 1)),
        dma,
        dma((2, X - 1)),
        dma,
        dma((Z - 1, 2, 2)),
        dma,
        dma,
        dma,
        dma((max(Y - 1, 1),)),
        dma((2,)),
        dma((2,)),
        dma((2, max(Y - 1, 1))),
        dma((2, max(Y - 1, 1))),
        dma((2,)),
        dma((2,)),
        dma,
        dma((2, Z - 1)),
        dma,
        dma((2, X - 1)),
    ]
    in_vmem = pl.BlockSpec(memory_space=pltpu.VMEM)
    in_hbm = pl.BlockSpec(memory_space=pltpu.HBM)
    shapes = [(rows, tokens)] + [(tokens, width)] * 4
    operands = (queries, keys, values, log_decay.T, gate, norm_gain.reshape(1, width), out_weight, target.T)
    results = pl.pallas_call(
        functools.partial(kernel, chips),
        out_shape=tuple(pltpu.VMEM(shape, BF16) for shape in shapes),
        in_specs=[in_hbm] * 8,
        out_specs=(in_vmem,) * 5,
        scratch_shapes=scratch,
        compiler_params=pltpu.CompilerParams(
            collective_id=0, has_side_effects=True, vmem_limit_bytes=48 * 1024 * 1024
        ),
        cost_estimate=pl.CostEstimate(flops=2 * 10**9, bytes_accessed=8 * 10**6, transcendentals=10**6),
        name="attention_layer",
    )(*[pltpu.with_memory_space_constraint(operand, pltpu.HBM) for operand in operands])
    output, *grads = pl.pallas_call(
        store,
        out_shape=tuple(jax.ShapeDtypeStruct(shape, BF16) for shape in shapes),
        in_specs=[in_vmem] * 5,
        out_specs=(in_hbm,) * 5,
        scratch_shapes=[dma((5,))],
        compiler_params=pltpu.CompilerParams(vmem_limit_bytes=4 * 1024 * 1024),
        name="store",
    )(*results)
    return (output.T, *grads)


def solution(mesh):
    chips = (mesh.shape["ctx"] // 2, mesh.shape["tp"] // X)
    return jax.shard_map(
        functools.partial(on_device, chips),
        mesh=mesh,
        in_specs=(
            P("ctx", "tp"),
            P("ctx", "tp"),
            P("ctx", "tp"),
            P("ctx", "tp"),
            P("ctx", "tp"),
            P("tp"),
            P("tp", None),
            P("ctx", "tp"),
        ),
        out_specs=(P("ctx", "tp"),) * 5,
        check_vma=False,
    )
```

```python
import functools

import jax
import jax.numpy as jnp
from jax import lax
from jax.experimental import pallas as pl
from jax.experimental.pallas import tpu as pltpu
from jax.sharding import PartitionSpec as P

DH = 128
EPS = 1e-06
MESH = pl.DeviceIdType.MESH
F32 = jnp.float32
BF16 = jnp.bfloat16
X = 4


def nn(a, b):
    return lax.dot_general(a, b, (((1,), (0,)), ((), ())), preferred_element_type=F32)


def nt(a, b):
    return lax.dot_general(a, b, (((1,), (1,)), ((), ())), preferred_element_type=F32)


def tn(a, b):
    return lax.dot_general(a, b, (((0,), (0,)), ((), ())), preferred_element_type=F32)


def identity(size):
    row = lax.broadcasted_iota(jnp.int32, (size, size), 0)
    column = lax.broadcasted_iota(jnp.int32, (size, size), 1)
    return jnp.where(row == column, 1.0, 0.0).astype(BF16)


def as_row(column):
    return jnp.broadcast_to(column, (column.shape[0], 128)).T[0:1, :]


def as_columns(row):
    return jnp.broadcast_to(row, (128, row.shape[1])).T


def kernel(
    sizes,
    q_in,
    k_in,
    v_in,
    ld_in,
    gate_in,
    gain_in,
    w_ref,
    target_in,
    out_ref,
    qg_ref,
    kg_ref,
    vg_ref,
    gg_ref,
    q_ref,
    k_ref,
    v_ref,
    ld_ref,
    gate_ref,
    gain_ref,
    target_ref,
    in_sems,
    wb,
    wrelay,
    uall,
    yacc,
    ystage,
    yrecv,
    gx,
    gall,
    fstage,
    frecv,
    weight,
    probs,
    kdec,
    att,
    klocal,
    vlocal,
    agrad,
    until_end,
    from_start,
    qdec,
    scale,
    closed,
    bown,
    bsib,
    bchip,
    s_out,
    s_in,
    s_keep,
    t_out,
    t_in,
    c_acc,
    d_acc,
    c_out,
    state,
    small_z,
    small_x,
    w_send,
    w_recv,
    w_own,
    ws_send,
    ws_recv,
    u_send,
    u_recv,
    y_send,
    y_recv,
    g_send,
    g_recv,
    f_send,
    f_recv,
    b_send,
    b_recv,
    bc_send,
    bc_recv,
    s_send,
    s_recv,
    t_send,
    t_recv,
    c_send,
    c_recv,
    sz_send,
    sz_recv,
    sx_send,
    sx_recv,
):
    Y, Z = sizes
    tokens = q_ref.shape[0]
    half_tokens = tokens // 2
    rows = w_ref.shape[0]
    half = rows // 2
    width = q_ref.shape[1]
    total_features = w_ref.shape[1]
    heads = width // DH

    ctx = lax.axis_index("ctx")
    tp = lax.axis_index("tp")
    core = lax.rem(ctx, 2)
    y = lax.div(ctx, 2)
    x = lax.rem(tp, X)
    z = lax.div(tp, X)
    sibling = (y * 2 + 1 - core, tp)
    is_zero = core == 0

    def xs(step):
        return lax.rem(x + step + X, X)

    def zs(step):
        return lax.rem(z + step + 2 * Z, Z)

    def at_x(step):
        return (ctx, z * X + xs(step))

    def at_z(step):
        return (ctx, zs(step) * X + x)

    def at_y(place):
        return (place * 2 + core, tp)

    sign = 1 - 2 * core
    left, right, opp = xs(-1), xs(1), xs(2)

    def send(src, dst, send_sem, recv_sem, device):
        copy = pltpu.make_async_remote_copy(
            src_ref=src,
            dst_ref=dst,
            send_sem=send_sem,
            recv_sem=recv_sem,
            device_id=device,
            device_id_type=MESH,
        )
        copy.start()

    def arrived(ref, sem):
        pltpu.make_async_copy(ref, ref, sem).wait()

    loads = [
        pltpu.make_async_copy(src, dst, in_sems.at[index])
        for index, (src, dst) in enumerate(
            (
                (ld_in, ld_ref),
                (k_in, k_ref),
                (v_in, v_ref),
                (q_in, q_ref),
                (gate_in, gate_ref),
                (gain_in, gain_ref),
                (target_in, target_ref),
            )
        )
    ]
    for load in loads:
        load.start()
    barrier = pltpu.get_barrier_semaphore()
    partners = [sibling] + [at_x(step) for step in range(1, X)]
    partners += [at_z(step) for step in range(1, Z)]
    partners += [at_y(lax.rem(y + step, Y)) for step in range(1, Y)]
    for partner in partners:
        pl.semaphore_signal(barrier, inc=1, device_id=partner, device_id_type=MESH)

    def w_columns(block, x_to):
        start = pl.multiple_of((block * X + x_to) * width, width)
        return pl.ds(start, width)

    my_rows = pl.ds(pl.multiple_of(core * half, half), half)
    x_far = xs(sign)

    def w_far(block, carry):
        send(w_ref.at[my_rows, w_columns(block, opp)], wrelay.at[block], w_send.at[0], w_recv.at[0], (ctx, z * X + x_far))
        return carry

    def w_near(block, carry):
        send(w_ref.at[my_rows, w_columns(block, right)], wb.at[block, x, core], w_send.at[1], w_recv.at[1], at_x(1))
        send(w_ref.at[my_rows, w_columns(block, left)], wb.at[block, x, core], w_send.at[2], w_recv.at[2], at_x(-1))
        return carry

    def w_mine(block, carry):
        for part in range(2):
            pltpu.make_async_copy(
                w_ref.at[pl.ds(part * half, half), w_columns(block, x)], wb.at[block, x, part], w_own
            ).start()
        return carry

    row = lax.broadcasted_iota(jnp.int32, (tokens, tokens), 0)
    column = lax.broadcasted_iota(jnp.int32, (tokens, tokens), 1)
    causal = row >= column
    loads[0].wait()
    upto = jnp.where(row <= column, 1.0, 0.0).astype(BF16)
    rest = ld_ref[...]
    cum = jnp.zeros_like(rest)
    for _ in range(3):
        piece = rest.astype(BF16)
        cum = cum + nn(piece, upto)
        rest = rest - piece.astype(F32)
    cum_rows = [cum[h : h + 1, :] for h in range(heads)]
    cums = [as_columns(c) for c in cum_rows]
    totals = [c[tokens - 1 : tokens, :] for c in cums]
    bown[...] = jnp.zeros_like(bown)
    for h in range(heads):
        bown[h : h + 1, :] = totals[h]
    loads[1].wait()
    loads[2].wait()

    def lanes(h):
        return slice(h * DH, (h + 1) * DH)

    for h in range(heads):
        until_end[h] = jnp.exp(totals[h] - cums[h])
    order = (core, 1 - core)
    others = (1 - core, core)

    def any_lanes(h):
        return pl.ds(pl.multiple_of(h * DH, DH), DH)

    def of_core(pair):
        return jnp.where(is_zero, pair[0], pair[1])

    def scan_give(turn, mine, value):
        if mine:
            s_keep[turn] = value
        else:
            s_out[turn] = value.astype(BF16)
            send(s_out.at[turn], s_in.at[turn], s_send.at[turn], s_recv.at[turn], sibling)

    def scan_way(turn):
        step = 1 if turn == 0 else -1
        first_here = is_zero if turn == 0 else jnp.logical_not(is_zero)
        return step, first_here

    def decays(ref):
        return of_core((ref[0:1, :], ref[1:2, :]))

    def reaches(place):
        return jnp.logical_and(place >= 0, place < Y)

    def scan_send(turn):
        step, first_here = scan_way(turn)
        arrived(s_in.at[turn], s_recv.at[turn])
        mine = s_keep[turn]
        theirs = s_in[turn].astype(F32)
        first = jnp.where(first_here, mine, theirs)
        second = jnp.where(first_here, theirs, mine)
        s_keep[turn] = first
        b_second = jnp.where(first_here, decays(bsib), decays(bown))
        t_out[turn] = (jnp.exp(b_second) * first + second).astype(BF16)
        for distance in range(1, Y):
            place = y + step * distance

            @pl.when(reaches(place))
            def _():
                send(
                    t_out.at[turn],
                    t_in.at[turn, distance - 1],
                    t_send.at[turn, distance - 1],
                    t_recv.at[turn, distance - 1],
                    at_y(place),
                )

    def scan_end(turn):
        step, first_here = scan_way(turn)
        c_acc[...] = jnp.zeros_like(c_acc)
        d_acc[...] = jnp.zeros_like(d_acc)
        for distance in range(1, Y):
            place = y - step * distance

            @pl.when(reaches(place))
            def _():
                slot = t_in.at[turn, distance - 1]
                arrived(slot, t_recv.at[turn, distance - 1])
                between = d_acc[0:1, :]
                c_acc[...] += jnp.exp(between) * slot[...].astype(F32)
                d_acc[0:1, :] = between + decays(bchip.at[place])

        b_first = jnp.where(first_here, decays(bown), decays(bsib))
        carried = c_acc[...]
        after = jnp.exp(b_first) * carried + s_keep[turn]
        c_out[turn] = jnp.where(first_here, after, carried).astype(BF16)
        send(c_out.at[turn], state.at[turn, core], c_send.at[turn], c_recv.at[turn], sibling)
        state[turn, core] = jnp.where(first_here, carried, after).astype(BF16)

    def scan_take(turn):
        arrived(state.at[turn, 1 - core], c_recv.at[turn])

    pl.semaphore_wait(barrier, len(partners))
    send(bown, bsib, b_send, b_recv, sibling)
    for mine, h in enumerate(others):
        at = any_lanes(h)
        decayed = (k_ref[:, at].astype(F32) * until_end[h]).astype(BF16)
        kdec[:, at] = decayed
        scan_give(0, mine, tn(decayed, v_ref[:, at]))
    lax.fori_loop(0, Z, w_far, 0)
    lax.fori_loop(0, Z, w_near, 0)

    arrived(bsib, b_recv)
    bchip[y] = bown[...] + bsib[...]
    for distance in range(1, Y):
        place = lax.rem(y + distance, Y)
        send(bchip.at[y], bchip.at[y], bc_send, bc_recv.at[distance - 1], at_y(place))
    scan_send(0)

    for load in loads[3:]:
        load.wait()
    for h in range(heads):
        gaps = cums[h][:, 0:1] - cum_rows[h]
        decay = jnp.where(causal, jnp.exp(jnp.minimum(gaps, 0.0)), 0.0)
        weight[h] = decay
        probs[h] = (nt(q_ref[:, lanes(h)], k_ref[:, lanes(h)]) * decay).astype(BF16)
        att[:, lanes(h)] = nn(probs[h], v_ref[:, lanes(h)])
        from_start[h] = jnp.exp(cums[h])
        gate_open = jax.nn.sigmoid(gate_ref[:, lanes(h)].astype(F32))
        scale[:, lanes(h)] = gain_ref[:, lanes(h)] * gate_open

    for distance in range(1, Y):
        arrived(bchip.at[lax.rem(y - distance + Y, Y)], bc_recv.at[distance - 1])

    scan_end(0)

    far, near = Z // 2, Z - 1 - Z // 2
    hops = (far, near)
    ways = (sign, -sign)

    def u_part(way, step, part, h):
        return uall.at[zs(-ways[way] * step), part, h]

    def u_start(way, step, part, h):
        ref = u_part(way, step, part, h)
        send(ref, ref, u_send, u_recv.at[way, step, part, h], at_z(ways[way]))

    for turn, h in enumerate(order):
        if turn == 1:
            scan_take(0)
        for part in range(2):
            span = slice(part * half_tokens, (part + 1) * half_tokens)
            from_state = nn(q_ref[span, any_lanes(h)], state[0, h]) * from_start[h, span, :]
            attended = att[span, any_lanes(h)] + from_state
            att[span, any_lanes(h)] = attended
            uall[z, part, h] = (attended * scale[span, any_lanes(h)]).astype(BF16)
            for way in range(2):
                if hops[way] > 0:
                    u_start(way, 0, part, h)

    def small_share(turn, value):
        small_z[turn, 0] = value
        for step in range(1, Z):
            send(small_z.at[turn, 0], small_z.at[turn, step], sz_send, sz_recv.at[turn, step - 1], at_z(step))

    def small_cross(turn):
        for step in range(1, Z):
            arrived(small_z.at[turn, step], sz_recv.at[turn, step - 1])
        sum_z = small_z[turn, 0]
        for step in range(1, Z):
            sum_z = sum_z + small_z[turn, step]
        small_x[turn, 0] = sum_z
        for step in range(1, X):
            send(small_x.at[turn, 0], small_x.at[turn, step], sx_send, sx_recv.at[turn, step - 1], at_x(step))

    def small_sum(turn):
        for step in range(1, X):
            arrived(small_x.at[turn, step], sx_recv.at[turn, step - 1])
        sum_x = small_x[turn, 0]
        for step in range(1, X):
            sum_x = sum_x + small_x[turn, step]
        return sum_x

    squares = jnp.zeros((tokens, 1), F32)
    for h in range(heads):
        attended = att[:, lanes(h)]
        squares = squares + jnp.sum(attended * attended, axis=1, keepdims=True)
    small_share(0, as_row(squares))
    lax.fori_loop(0, Z, w_mine, 0)

    arrived(wrelay, w_recv.at[0])
    send(wrelay, wb.at[:, xs(-sign), core], w_send.at[3], w_recv.at[3], (ctx, z * X + x_far))

    for h in range(heads):
        qdec[:, lanes(h)] = (q_ref[:, lanes(h)].astype(F32) * from_start[h]).astype(BF16)
        closed[:, lanes(h)] = 1.0 - jax.nn.sigmoid(gate_ref[:, lanes(h)].astype(F32))

    def w_pair(source, sem, slot):
        ref = wb.at[:, source, core]
        arrived(ref, sem)
        send(ref, ref, ws_send.at[slot], ws_recv.at[slot], sibling)

    def w_block(block):
        return wb[block].reshape(X * rows, width)

    def u_block(block, part):
        return jnp.concatenate([uall[block, part, h] for h in range(heads)], axis=1)

    def product(block):
        both = nt(w_block(block), jnp.concatenate([u_block(block, part) for part in range(2)], axis=0))
        return [both[:, part * half_tokens : (part + 1) * half_tokens].reshape(yacc.shape[1:]) for part in range(2)]

    def u_pass(step, part, some):
        for h in some:
            for way in range(2):
                if step < hops[way]:
                    arrived(u_part(way, step + 1, part, h), u_recv.at[way, step, part, h])
                    if step + 1 < hops[way]:
                        u_start(way, step + 1, part, h)

    def absorb(step):
        for way in range(2):
            if step < hops[way]:
                for part, value in enumerate(product(zs(-ways[way] * (step + 1)))):
                    yacc[part] += value

    def w_forward():
        small_cross(0)
        w_pair(left, w_recv.at[1], 0)
        w_pair(right, w_recv.at[2], 1)
        w_pair(opp, w_recv.at[3], 2)

    for step in range(far - 1):
        if step == far - 2:
            w_forward()
        for h in order:
            for part in range(2):
                u_pass(step, part, (h,))
    if far < 2:
        w_forward()
    for part in range(2):
        arrived(wb.at[:, x, part], w_own)
    for slot, source in enumerate((left, right, opp)):
        arrived(wb.at[:, source, 1 - core], ws_recv.at[slot])
    for part, value in enumerate(product(z)):
        yacc[part] = value
    for step in range(far - 1):
        absorb(step)

    steps = (2, 1, 3)

    def y_start(part, step):
        ystage[part, step - 1] = yacc[part, xs(step)].astype(BF16)
        send(
            ystage.at[part, step - 1],
            yrecv.at[part, step - 1],
            y_send,
            y_recv.at[part, step - 1],
            at_x(step),
        )

    def y_arrived(part, step):
        arrived(yrecv.at[part, step - 1], y_recv.at[part, step - 1])
        return yrecv[part, step - 1].astype(F32)

    for part in range(2):
        u_pass(far - 1, part, order)
        last = zs(sign * far)
        last_u = u_block(last, part)

        def finish(rows_of):
            block = wb[last, rows_of].reshape(rows, width)
            yacc[part, rows_of] += nt(block, last_u)

        for step in steps:
            finish(xs(step))
            y_start(part, step)
        finish(x)

    inv_rms = lax.rsqrt(small_sum(0) / total_features + EPS)

    def g_arrived(part, step):
        arrived(gx.at[part, xs(-step)], g_recv.at[part, step - 1])

    products = []
    for part in range(2):
        span = slice(part * half_tokens, (part + 1) * half_tokens)
        total = yacc[part, x]
        for step in (1, 3, 2):
            total = total + y_arrived(part, step)
        rounded = (total * inv_rms[:, span]).astype(BF16)
        grad = (rounded.astype(F32) - target_ref[:, span].astype(F32)).astype(BF16)
        gx[part, x] = grad
        for step in steps:
            ref = gx.at[part, x]
            send(ref, ref, g_send, g_recv.at[part, step - 1], at_x(step))
        out_ref[:, span] = rounded
        products.append(jnp.sum(grad.astype(F32) * total, axis=0, keepdims=True))
    small_share(1, jnp.concatenate(products, axis=1))

    eye = identity(half_tokens)

    def feature_part(block, part):
        return nn(gall[part], w_block(block))

    def f_slot(way, step):
        return way * far + step

    def f_start(way, step, part, h, value):
        slot = f_slot(way, step)
        fstage[slot, part, h] = value.astype(BF16)
        send(
            fstage.at[slot, part, h],
            frecv.at[slot, part, h],
            f_send,
            f_recv.at[slot, part, h],
            at_z(ways[way]),
        )

    def f_arrived(way, step, part, h):
        slot = f_slot(way, step)
        arrived(frecv.at[slot, part, h], f_recv.at[slot, part, h])
        return frecv[slot, part, h].astype(F32)

    def by_head(value):
        first, second = value[:, lanes(0)], value[:, lanes(1)]
        return jnp.where(is_zero, second, first), jnp.where(is_zero, first, second)

    for part in range(2):
        for x_step in (1, 3, 2):
            g_arrived(part, x_step)
        gall[part] = nt(eye, gx[part].reshape(X * rows, half_tokens)).astype(BF16)
        sums = [by_head(feature_part(zs(ways[way] * hops[way]), part)) if hops[way] > 0 else None for way in range(2)]
        for turn in range(heads):
            for way in range(2):
                if hops[way] > 0:
                    f_start(way, 0, part, turn, sums[way][turn])
    small_cross(1)

    def feature_both(block):
        return by_head(nn(gall[...].reshape(tokens, X * rows), w_block(block)))

    for step in range(1, far):
        sums = [feature_both(zs(ways[way] * (hops[way] - step))) if step < hops[way] else None for way in range(2)]
        for part in range(2):
            span = slice(part * half_tokens, (part + 1) * half_tokens)
            for turn in range(heads):
                for way in range(2):
                    if step < hops[way]:
                        value = sums[way][turn][span, :] + f_arrived(way, step - 1, part, turn)
                        f_start(way, step, part, turn, value)

    own_feature = feature_both(z)
    mean_product = as_columns(small_sum(1) / total_features)
    inv = as_columns(inv_rms)

    for turn, h in enumerate(others):
        at = any_lanes(h)
        pieces = []
        for part in range(2):
            value = own_feature[turn][part * half_tokens : (part + 1) * half_tokens, :]
            for way in range(2):
                if hops[way] > 0:
                    value = value + f_arrived(way, hops[way] - 1, part, turn)
            pieces.append(value)
        attended = att[:, at]
        normed_grad = jnp.concatenate(pieces, axis=0) * scale[:, at]
        grad = (inv * normed_grad - inv * inv * inv * attended * mean_product).astype(BF16)
        agrad[:, at] = grad
        scan_give(1, turn, tn(qdec[:, at], grad))
        gg_ref[:, at] = (normed_grad * attended * inv * closed[:, at]).astype(BF16)

    for h in range(heads):
        grad = agrad[:, lanes(h)]
        score_grad = (nt(grad, v_ref[:, lanes(h)]) * weight[h]).astype(BF16)
        if h == 0:
            scan_send(1)
        qg_ref[:, lanes(h)] = (
            nn(score_grad, k_ref[:, lanes(h)]) + from_start[h] * nt(grad, state[0, h])
        ).astype(BF16)
        klocal[:, lanes(h)] = tn(score_grad, q_ref[:, lanes(h)])
        vlocal[:, lanes(h)] = tn(probs[h], grad)
    for index in range(4):
        arrived(wrelay, w_send.at[index])
    for index in range(3):
        arrived(wrelay, ws_send.at[index])
    arrived(uall.at[pl.ds(0, Z - 1)], u_send)
    arrived(fstage, f_send)
    arrived(ystage, y_send)
    arrived(ystage, g_send)
    arrived(bown, b_send)
    if Y > 1:
        arrived(bchip.at[pl.ds(0, Y - 1)], bc_send)
    arrived(small_z.at[:, pl.ds(0, Z - 1)], sz_send)
    arrived(small_x.at[:, pl.ds(0, X - 1)], sx_send)
    for turn in range(2):
        arrived(s_out.at[turn], s_send.at[turn])

    def scan_sent(turn):
        step, _ = scan_way(turn)
        for distance in range(1, Y):

            @pl.when(reaches(y + step * distance))
            def _():
                arrived(t_out.at[turn], t_send.at[turn, distance - 1])

    scan_sent(0)
    arrived(c_out.at[0], c_send.at[0])

    scan_end(1)
    for turn, h in enumerate(order):
        if turn == 1:
            scan_sent(1)
            scan_take(1)
        at = any_lanes(h)
        later = state[1, h]
        kg_ref[:, at] = (klocal[:, at] + until_end[h] * nt(v_ref[:, at], later)).astype(BF16)
        vg_ref[:, at] = (vlocal[:, at] + nn(kdec[:, at], later)).astype(BF16)

    arrived(c_out.at[1], c_send.at[1])


def store(*refs):
    *refs, sems = refs
    count = len(refs) // 2
    copies = [pltpu.make_async_copy(refs[i], refs[count + i], sems.at[i]) for i in range(count)]
    for copy in copies:
        copy.start()
    for copy in copies:
        copy.wait()


def on_device(chips, queries, keys, values, log_decay, gate, norm_gain, out_weight, target):
    Y, Z = chips
    tokens, width = queries.shape
    rows, features = out_weight.shape
    half = rows // 2
    far = Z // 2
    vmem = pltpu.VMEM
    dma = pltpu.SemaphoreType.DMA
    scratch = [
        vmem((tokens, width), BF16),
        vmem((tokens, width), BF16),
        vmem((tokens, width), BF16),
        vmem((width // DH, tokens), F32),
        vmem((tokens, width), BF16),
        vmem((1, width), F32),
        vmem((rows, tokens), BF16),
        dma((7,)),
        vmem((Z, X, 2, half, width), BF16),
        vmem((Z, half, width), BF16),
        vmem((Z, 2, width // DH, tokens // 2, DH), BF16),
        vmem((2, X, rows, tokens // 2), F32),
        vmem((2, X - 1, rows, tokens // 2), BF16),
        vmem((2, X - 1, rows, tokens // 2), BF16),
        vmem((2, X, rows, tokens // 2), BF16),
        vmem((2, tokens // 2, X * rows), BF16),
        vmem((Z - 1, 2, 2, tokens // 2, DH), BF16),
        vmem((Z - 1, 2, 2, tokens // 2, DH), BF16),
        vmem((width // DH, tokens, tokens), F32),
        vmem((width // DH, tokens, tokens), BF16),
        vmem((tokens, width), BF16),
        vmem((tokens, width), F32),
        vmem((tokens, width), F32),
        vmem((tokens, width), F32),
        vmem((tokens, width), BF16),
        vmem((width // DH, tokens, DH), F32),
        vmem((width // DH, tokens, DH), F32),
        vmem((tokens, width), BF16),
        vmem((tokens, width), F32),
        vmem((tokens, width), F32),
        vmem((8, 128), F32),
        vmem((8, 128), F32),
        vmem((Y, 8, 128), F32),
        vmem((2, DH, DH), BF16),
        vmem((2, DH, DH), BF16),
        vmem((2, DH, DH), F32),
        vmem((2, DH, DH), BF16),
        vmem((2, max(Y - 1, 1), DH, DH), BF16),
        vmem((DH, DH), F32),
        vmem((8, 128), F32),
        vmem((2, DH, DH), BF16),
        vmem((2, 2, DH, DH), BF16),
        vmem((2, Z, 1, tokens), F32),
        vmem((2, X, 1, tokens), F32),
        dma((4,)),
        dma((4,)),
        dma,
        dma((3,)),
        dma((3,)),
        dma,
        dma((2, far, 2, 2)),
        dma,
        dma((2, X - 1)),
        dma,
        dma((2, X - 1)),
        dma,
        dma((Z - 1, 2, 2)),
        dma,
        dma,
        dma,
        dma((max(Y - 1, 1),)),
        dma((2,)),
        dma((2,)),
        dma((2, max(Y - 1, 1))),
        dma((2, max(Y - 1, 1))),
        dma((2,)),
        dma((2,)),
        dma,
        dma((2, Z - 1)),
        dma,
        dma((2, X - 1)),
    ]
    in_vmem = pl.BlockSpec(memory_space=pltpu.VMEM)
    in_hbm = pl.BlockSpec(memory_space=pltpu.HBM)
    shapes = [(rows, tokens)] + [(tokens, width)] * 4
    operands = (queries, keys, values, log_decay.T, gate, norm_gain.reshape(1, width), out_weight, target.T)
    results = pl.pallas_call(
        functools.partial(kernel, chips),
        out_shape=tuple(pltpu.VMEM(shape, BF16) for shape in shapes),
        in_specs=[in_hbm] * 8,
        out_specs=(in_vmem,) * 5,
        scratch_shapes=scratch,
        compiler_params=pltpu.CompilerParams(
            collective_id=0, has_side_effects=True, vmem_limit_bytes=48 * 1024 * 1024
        ),
        cost_estimate=pl.CostEstimate(flops=2 * 10**9, bytes_accessed=8 * 10**6, transcendentals=10**6),
        name="attention_layer",
    )(*[pltpu.with_memory_space_constraint(operand, pltpu.HBM) for operand in operands])
    output, *grads = pl.pallas_call(
        store,
        out_shape=tuple(jax.ShapeDtypeStruct(shape, BF16) for shape in shapes),
        in_specs=[in_vmem] * 5,
        out_specs=(in_hbm,) * 5,
        scratch_shapes=[dma((5,))],
        compiler_params=pltpu.CompilerParams(vmem_limit_bytes=4 * 1024 * 1024),
        name="store",
    )(*results)
    return (output.T, *grads)


def solution(mesh):
    chips = (mesh.shape["ctx"] // 2, mesh.shape["tp"] // X)
    return jax.shard_map(
        functools.partial(on_device, chips),
        mesh=mesh,
        in_specs=(
            P("ctx", "tp"),
            P("ctx", "tp"),
            P("ctx", "tp"),
            P("ctx", "tp"),
            P("ctx", "tp"),
            P("tp"),
            P("tp", None),
            P("ctx", "tp"),
        ),
        out_specs=(P("ctx", "tp"),) * 5,
        check_vma=False,
    )
```

```python
import functools

import jax
import jax.numpy as jnp
from jax import lax
from jax.experimental import pallas as pl
from jax.experimental.pallas import tpu as pltpu
from jax.sharding import PartitionSpec as P

DH = 128
EPS = 1e-06
MESH = pl.DeviceIdType.MESH
F32 = jnp.float32
BF16 = jnp.bfloat16
X = 4


def nn(a, b):
    return lax.dot_general(a, b, (((1,), (0,)), ((), ())), preferred_element_type=F32)


def nt(a, b):
    return lax.dot_general(a, b, (((1,), (1,)), ((), ())), preferred_element_type=F32)


def tn(a, b):
    return lax.dot_general(a, b, (((0,), (0,)), ((), ())), preferred_element_type=F32)


def identity(size):
    row = lax.broadcasted_iota(jnp.int32, (size, size), 0)
    column = lax.broadcasted_iota(jnp.int32, (size, size), 1)
    return jnp.where(row == column, 1.0, 0.0).astype(BF16)


def as_row(column):
    return jnp.broadcast_to(column, (column.shape[0], 128)).T[0:1, :]


def as_columns(row):
    return jnp.broadcast_to(row, (128, row.shape[1])).T


def kernel(
    sizes,
    q_in,
    k_in,
    v_in,
    ld_in,
    gate_in,
    gain_in,
    w_ref,
    target_in,
    out_ref,
    qg_ref,
    kg_ref,
    vg_ref,
    gg_ref,
    q_ref,
    k_ref,
    v_ref,
    ld_ref,
    gate_ref,
    gain_ref,
    target_ref,
    in_sems,
    wb,
    wrelay,
    uall,
    yacc,
    ystage,
    yrecv,
    gx,
    gall,
    fstage,
    frecv,
    weight,
    probs,
    kdec,
    att,
    klocal,
    vlocal,
    agrad,
    until_end,
    from_start,
    qdec,
    scale,
    closed,
    bown,
    bsib,
    bchip,
    s_out,
    s_in,
    s_keep,
    t_out,
    t_in,
    c_acc,
    d_acc,
    c_out,
    state,
    small_z,
    small_x,
    w_send,
    w_recv,
    w_own,
    ws_send,
    ws_recv,
    u_send,
    u_recv,
    y_send,
    y_recv,
    g_send,
    g_recv,
    f_send,
    f_recv,
    b_send,
    b_recv,
    bc_send,
    bc_recv,
    s_send,
    s_recv,
    t_send,
    t_recv,
    c_send,
    c_recv,
    sz_send,
    sz_recv,
    sx_send,
    sx_recv,
):
    Y, Z = sizes
    tokens = q_ref.shape[0]
    half_tokens = tokens // 2
    rows = w_ref.shape[0]
    half = rows // 2
    width = q_ref.shape[1]
    total_features = w_ref.shape[1]
    heads = width // DH

    ctx = lax.axis_index("ctx")
    tp = lax.axis_index("tp")
    core = lax.rem(ctx, 2)
    y = lax.div(ctx, 2)
    x = lax.rem(tp, X)
    z = lax.div(tp, X)
    sibling = (y * 2 + 1 - core, tp)
    is_zero = core == 0

    def xs(step):
        return lax.rem(x + step + X, X)

    def zs(step):
        return lax.rem(z + step + 2 * Z, Z)

    def at_x(step):
        return (ctx, z * X + xs(step))

    def at_z(step):
        return (ctx, zs(step) * X + x)

    def at_y(place):
        return (place * 2 + core, tp)

    sign = 1 - 2 * core
    left, right, opp = xs(-1), xs(1), xs(2)

    def send(src, dst, send_sem, recv_sem, device):
        copy = pltpu.make_async_remote_copy(
            src_ref=src,
            dst_ref=dst,
            send_sem=send_sem,
            recv_sem=recv_sem,
            device_id=device,
            device_id_type=MESH,
        )
        copy.start()

    def arrived(ref, sem):
        pltpu.make_async_copy(ref, ref, sem).wait()

    loads = [
        pltpu.make_async_copy(src, dst, in_sems.at[index])
        for index, (src, dst) in enumerate(
            (
                (ld_in, ld_ref),
                (k_in, k_ref),
                (v_in, v_ref),
                (q_in, q_ref),
                (gate_in, gate_ref),
                (gain_in, gain_ref),
                (target_in, target_ref),
            )
        )
    ]
    for load in loads:
        load.start()
    barrier = pltpu.get_barrier_semaphore()
    partners = [sibling] + [at_x(step) for step in range(1, X)]
    partners += [at_z(step) for step in range(1, Z)]
    partners += [at_y(lax.rem(y + step, Y)) for step in range(1, Y)]
    for partner in partners:
        pl.semaphore_signal(barrier, inc=1, device_id=partner, device_id_type=MESH)

    def w_columns(block, x_to):
        start = pl.multiple_of((block * X + x_to) * width, width)
        return pl.ds(start, width)

    my_rows = pl.ds(pl.multiple_of(core * half, half), half)
    x_far = xs(sign)

    def w_far(block, carry):
        send(w_ref.at[my_rows, w_columns(block, opp)], wrelay.at[block], w_send.at[0], w_recv.at[0], (ctx, z * X + x_far))
        return carry

    def w_near(block, carry):
        send(w_ref.at[my_rows, w_columns(block, right)], wb.at[block, x, core], w_send.at[1], w_recv.at[1], at_x(1))
        send(w_ref.at[my_rows, w_columns(block, left)], wb.at[block, x, core], w_send.at[2], w_recv.at[2], at_x(-1))
        return carry

    def w_mine(block, carry):
        for part in range(2):
            pltpu.make_async_copy(
                w_ref.at[pl.ds(part * half, half), w_columns(block, x)], wb.at[block, x, part], w_own
            ).start()
        return carry

    row = lax.broadcasted_iota(jnp.int32, (tokens, tokens), 0)
    column = lax.broadcasted_iota(jnp.int32, (tokens, tokens), 1)
    causal = row >= column
    loads[0].wait()
    upto = jnp.where(row <= column, 1.0, 0.0).astype(BF16)
    rest = ld_ref[...]
    cum = jnp.zeros_like(rest)
    for _ in range(3):
        piece = rest.astype(BF16)
        cum = cum + nn(piece, upto)
        rest = rest - piece.astype(F32)
    cum_rows = [cum[h : h + 1, :] for h in range(heads)]
    cums = [as_columns(c) for c in cum_rows]
    totals = [c[tokens - 1 : tokens, :] for c in cums]
    bown[...] = jnp.zeros_like(bown)
    for h in range(heads):
        bown[h : h + 1, :] = totals[h]
    loads[1].wait()
    loads[2].wait()

    def lanes(h):
        return slice(h * DH, (h + 1) * DH)

    for h in range(heads):
        until_end[h] = jnp.exp(totals[h] - cums[h])
    order = (core, 1 - core)
    others = (1 - core, core)

    def any_lanes(h):
        return pl.ds(pl.multiple_of(h * DH, DH), DH)

    def of_core(pair):
        return jnp.where(is_zero, pair[0], pair[1])

    def scan_give(turn, mine, value):
        if mine:
            s_keep[turn] = value
        else:
            s_out[turn] = value.astype(BF16)
            send(s_out.at[turn], s_in.at[turn], s_send.at[turn], s_recv.at[turn], sibling)

    def scan_way(turn):
        step = 1 if turn == 0 else -1
        first_here = is_zero if turn == 0 else jnp.logical_not(is_zero)
        return step, first_here

    def decays(ref):
        return of_core((ref[0:1, :], ref[1:2, :]))

    def reaches(place):
        return jnp.logical_and(place >= 0, place < Y)

    def scan_send(turn):
        step, first_here = scan_way(turn)
        arrived(s_in.at[turn], s_recv.at[turn])
        mine = s_keep[turn]
        theirs = s_in[turn].astype(F32)
        first = jnp.where(first_here, mine, theirs)
        second = jnp.where(first_here, theirs, mine)
        s_keep[turn] = first
        b_second = jnp.where(first_here, decays(bsib), decays(bown))
        t_out[turn] = (jnp.exp(b_second) * first + second).astype(BF16)
        for distance in range(1, Y):
            place = y + step * distance

            @pl.when(reaches(place))
            def _():
                send(
                    t_out.at[turn],
                    t_in.at[turn, distance - 1],
                    t_send.at[turn, distance - 1],
                    t_recv.at[turn, distance - 1],
                    at_y(place),
                )

    def scan_end(turn):
        step, first_here = scan_way(turn)
        c_acc[...] = jnp.zeros_like(c_acc)
        d_acc[...] = jnp.zeros_like(d_acc)
        for distance in range(1, Y):
            place = y - step * distance

            @pl.when(reaches(place))
            def _():
                slot = t_in.at[turn, distance - 1]
                arrived(slot, t_recv.at[turn, distance - 1])
                between = d_acc[0:1, :]
                c_acc[...] += jnp.exp(between) * slot[...].astype(F32)
                d_acc[0:1, :] = between + decays(bchip.at[place])

        b_first = jnp.where(first_here, decays(bown), decays(bsib))
        carried = c_acc[...]
        after = jnp.exp(b_first) * carried + s_keep[turn]
        c_out[turn] = jnp.where(first_here, after, carried).astype(BF16)
        send(c_out.at[turn], state.at[turn, core], c_send.at[turn], c_recv.at[turn], sibling)
        state[turn, core] = jnp.where(first_here, carried, after).astype(BF16)

    def scan_take(turn):
        arrived(state.at[turn, 1 - core], c_recv.at[turn])

    pl.semaphore_wait(barrier, len(partners))
    send(bown, bsib, b_send, b_recv, sibling)
    for mine, h in enumerate(others):
        at = any_lanes(h)
        decayed = (k_ref[:, at].astype(F32) * until_end[h]).astype(BF16)
        kdec[:, at] = decayed
        scan_give(0, mine, tn(decayed, v_ref[:, at]))
    lax.fori_loop(0, Z, w_far, 0)
    lax.fori_loop(0, Z, w_near, 0)

    arrived(bsib, b_recv)
    scan_send(0)
    bchip[y] = bown[...] + bsib[...]
    for distance in range(1, Y):
        place = lax.rem(y + distance, Y)
        send(bchip.at[y], bchip.at[y], bc_send, bc_recv.at[distance - 1], at_y(place))

    for load in loads[3:]:
        load.wait()
    for h in range(heads):
        gaps = cums[h][:, 0:1] - cum_rows[h]
        decay = jnp.where(causal, jnp.exp(jnp.minimum(gaps, 0.0)), 0.0)
        weight[h] = decay
        probs[h] = (nt(q_ref[:, lanes(h)], k_ref[:, lanes(h)]) * decay).astype(BF16)
        att[:, lanes(h)] = nn(probs[h], v_ref[:, lanes(h)])
        from_start[h] = jnp.exp(cums[h])
        gate_open = jax.nn.sigmoid(gate_ref[:, lanes(h)].astype(F32))
        scale[:, lanes(h)] = gain_ref[:, lanes(h)] * gate_open

    for distance in range(1, Y):
        arrived(bchip.at[lax.rem(y - distance + Y, Y)], bc_recv.at[distance - 1])

    scan_end(0)

    far, near = Z // 2, Z - 1 - Z // 2
    hops = (far, near)
    ways = (sign, -sign)

    def u_part(way, step, part, h):
        return uall.at[zs(-ways[way] * step), part, h]

    def u_start(way, step, part, h):
        ref = u_part(way, step, part, h)
        send(ref, ref, u_send, u_recv.at[way, step, part, h], at_z(ways[way]))

    for turn, h in enumerate(order):
        if turn == 1:
            scan_take(0)
        for part in range(2):
            span = slice(part * half_tokens, (part + 1) * half_tokens)
            from_state = nn(q_ref[span, any_lanes(h)], state[0, h]) * from_start[h, span, :]
            attended = att[span, any_lanes(h)] + from_state
            att[span, any_lanes(h)] = attended
            uall[z, part, h] = (attended * scale[span, any_lanes(h)]).astype(BF16)
            for way in range(2):
                if hops[way] > 0:
                    u_start(way, 0, part, h)

    def small_share(turn, value):
        small_z[turn, 0] = value
        for step in range(1, Z):
            send(small_z.at[turn, 0], small_z.at[turn, step], sz_send, sz_recv.at[turn, step - 1], at_z(step))

    def small_cross(turn):
        for step in range(1, Z):
            arrived(small_z.at[turn, step], sz_recv.at[turn, step - 1])
        sum_z = small_z[turn, 0]
        for step in range(1, Z):
            sum_z = sum_z + small_z[turn, step]
        small_x[turn, 0] = sum_z
        for step in range(1, X):
            send(small_x.at[turn, 0], small_x.at[turn, step], sx_send, sx_recv.at[turn, step - 1], at_x(step))

    def small_sum(turn):
        for step in range(1, X):
            arrived(small_x.at[turn, step], sx_recv.at[turn, step - 1])
        sum_x = small_x[turn, 0]
        for step in range(1, X):
            sum_x = sum_x + small_x[turn, step]
        return sum_x

    squares = jnp.zeros((tokens, 1), F32)
    for h in range(heads):
        attended = att[:, lanes(h)]
        squares = squares + jnp.sum(attended * attended, axis=1, keepdims=True)
    small_share(0, as_row(squares))
    lax.fori_loop(0, Z, w_mine, 0)

    arrived(wrelay, w_recv.at[0])
    send(wrelay, wb.at[:, xs(-sign), core], w_send.at[3], w_recv.at[3], (ctx, z * X + x_far))

    for h in range(heads):
        qdec[:, lanes(h)] = (q_ref[:, lanes(h)].astype(F32) * from_start[h]).astype(BF16)
        closed[:, lanes(h)] = 1.0 - jax.nn.sigmoid(gate_ref[:, lanes(h)].astype(F32))

    def w_pair(source, sem, slot):
        ref = wb.at[:, source, core]
        arrived(ref, sem)
        send(ref, ref, ws_send.at[slot], ws_recv.at[slot], sibling)

    def w_block(block):
        return wb[block].reshape(X * rows, width)

    def u_block(block, part):
        return jnp.concatenate([uall[block, part, h] for h in range(heads)], axis=1)

    def product(block):
        both = nt(w_block(block), jnp.concatenate([u_block(block, part) for part in range(2)], axis=0))
        return [both[:, part * half_tokens : (part + 1) * half_tokens].reshape(yacc.shape[1:]) for part in range(2)]

    def u_pass(step, part, some):
        for h in some:
            for way in range(2):
                if step < hops[way]:
                    arrived(u_part(way, step + 1, part, h), u_recv.at[way, step, part, h])
                    if step + 1 < hops[way]:
                        u_start(way, step + 1, part, h)

    def absorb(step):
        for way in range(2):
            if step < hops[way]:
                for part, value in enumerate(product(zs(-ways[way] * (step + 1)))):
                    yacc[part] += value

    def w_forward():
        small_cross(0)
        w_pair(left, w_recv.at[1], 0)
        w_pair(right, w_recv.at[2], 1)
        w_pair(opp, w_recv.at[3], 2)

    for step in range(far - 1):
        if step == far - 2:
            w_forward()
        for h in order:
            for part in range(2):
                u_pass(step, part, (h,))
    if far < 2:
        w_forward()
    for part in range(2):
        arrived(wb.at[:, x, part], w_own)
    for slot, source in enumerate((left, right, opp)):
        arrived(wb.at[:, source, 1 - core], ws_recv.at[slot])
    for part, value in enumerate(product(z)):
        yacc[part] = value
    for step in range(far - 1):
        absorb(step)

    steps = (2, 1, 3)

    def y_start(part, step):
        ystage[part, step - 1] = yacc[part, xs(step)].astype(BF16)
        send(
            ystage.at[part, step - 1],
            yrecv.at[part, step - 1],
            y_send,
            y_recv.at[part, step - 1],
            at_x(step),
        )

    def y_arrived(part, step):
        arrived(yrecv.at[part, step - 1], y_recv.at[part, step - 1])
        return yrecv[part, step - 1].astype(F32)

    for part in range(2):
        u_pass(far - 1, part, order)
        last = zs(sign * far)
        last_u = u_block(last, part)

        def finish(rows_of):
            block = wb[last, rows_of].reshape(rows, width)
            yacc[part, rows_of] += nt(block, last_u)

        for step in steps:
            finish(xs(step))
            y_start(part, step)
        finish(x)

    inv_rms = lax.rsqrt(small_sum(0) / total_features + EPS)

    def g_arrived(part, step):
        arrived(gx.at[part, xs(-step)], g_recv.at[part, step - 1])

    products = []
    for part in range(2):
        span = slice(part * half_tokens, (part + 1) * half_tokens)
        total = yacc[part, x]
        for step in (1, 3, 2):
            total = total + y_arrived(part, step)
        rounded = (total * inv_rms[:, span]).astype(BF16)
        grad = (rounded.astype(F32) - target_ref[:, span].astype(F32)).astype(BF16)
        gx[part, x] = grad
        for step in steps:
            ref = gx.at[part, x]
            send(ref, ref, g_send, g_recv.at[part, step - 1], at_x(step))
        out_ref[:, span] = rounded
        products.append(jnp.sum(grad.astype(F32) * total, axis=0, keepdims=True))
    small_share(1, jnp.concatenate(products, axis=1))

    eye = identity(half_tokens)

    def feature_part(block, part):
        return nn(gall[part], w_block(block))

    def f_slot(way, step):
        return way * far + step

    def f_start(way, step, part, h, value):
        slot = f_slot(way, step)
        fstage[slot, part, h] = value.astype(BF16)
        send(
            fstage.at[slot, part, h],
            frecv.at[slot, part, h],
            f_send,
            f_recv.at[slot, part, h],
            at_z(ways[way]),
        )

    def f_arrived(way, step, part, h):
        slot = f_slot(way, step)
        arrived(frecv.at[slot, part, h], f_recv.at[slot, part, h])
        return frecv[slot, part, h].astype(F32)

    def by_head(value):
        first, second = value[:, lanes(0)], value[:, lanes(1)]
        return jnp.where(is_zero, second, first), jnp.where(is_zero, first, second)

    for part in range(2):
        for x_step in (1, 3, 2):
            g_arrived(part, x_step)
        gall[part] = nt(eye, gx[part].reshape(X * rows, half_tokens)).astype(BF16)
        sums = [by_head(feature_part(zs(ways[way] * hops[way]), part)) if hops[way] > 0 else None for way in range(2)]
        for turn in range(heads):
            for way in range(2):
                if hops[way] > 0:
                    f_start(way, 0, part, turn, sums[way][turn])
    small_cross(1)

    def feature_both(block):
        return by_head(nn(gall[...].reshape(tokens, X * rows), w_block(block)))

    for step in range(1, far):
        sums = [feature_both(zs(ways[way] * (hops[way] - step))) if step < hops[way] else None for way in range(2)]
        for part in range(2):
            span = slice(part * half_tokens, (part + 1) * half_tokens)
            for turn in range(heads):
                for way in range(2):
                    if step < hops[way]:
                        value = sums[way][turn][span, :] + f_arrived(way, step - 1, part, turn)
                        f_start(way, step, part, turn, value)

    own_feature = feature_both(z)
    mean_product = as_columns(small_sum(1) / total_features)
    inv = as_columns(inv_rms)

    normed_grads = []
    for turn, h in enumerate(others):
        at = any_lanes(h)
        pieces = []
        for part in range(2):
            value = own_feature[turn][part * half_tokens : (part + 1) * half_tokens, :]
            for way in range(2):
                if hops[way] > 0:
                    value = value + f_arrived(way, hops[way] - 1, part, turn)
            pieces.append(value)
        attended = att[:, at]
        normed_grad = jnp.concatenate(pieces, axis=0) * scale[:, at]
        grad = (inv * normed_grad - inv * inv * inv * attended * mean_product).astype(BF16)
        agrad[:, at] = grad
        scan_give(1, turn, tn(qdec[:, at], grad))
        normed_grads.append(normed_grad)
    scan_send(1)
    for turn, h in enumerate(others):
        at = any_lanes(h)
        gg_ref[:, at] = (normed_grads[turn] * att[:, at] * inv * closed[:, at]).astype(BF16)

    for h in range(heads):
        grad = agrad[:, lanes(h)]
        score_grad = (nt(grad, v_ref[:, lanes(h)]) * weight[h]).astype(BF16)
        qg_ref[:, lanes(h)] = (
            nn(score_grad, k_ref[:, lanes(h)]) + from_start[h] * nt(grad, state[0, h])
        ).astype(BF16)
        klocal[:, lanes(h)] = tn(score_grad, q_ref[:, lanes(h)])
        vlocal[:, lanes(h)] = tn(probs[h], grad)
    for index in range(4):
        arrived(wrelay, w_send.at[index])
    for index in range(3):
        arrived(wrelay, ws_send.at[index])
    arrived(uall.at[pl.ds(0, Z - 1)], u_send)
    arrived(fstage, f_send)
    arrived(ystage, y_send)
    arrived(ystage, g_send)
    arrived(bown, b_send)
    if Y > 1:
        arrived(bchip.at[pl.ds(0, Y - 1)], bc_send)
    arrived(small_z.at[:, pl.ds(0, Z - 1)], sz_send)
    arrived(small_x.at[:, pl.ds(0, X - 1)], sx_send)
    for turn in range(2):
        arrived(s_out.at[turn], s_send.at[turn])

    def scan_sent(turn):
        step, _ = scan_way(turn)
        for distance in range(1, Y):

            @pl.when(reaches(y + step * distance))
            def _():
                arrived(t_out.at[turn], t_send.at[turn, distance - 1])

    scan_sent(0)
    arrived(c_out.at[0], c_send.at[0])

    scan_end(1)
    for turn, h in enumerate(order):
        if turn == 1:
            scan_sent(1)
            scan_take(1)
        at = any_lanes(h)
        later = state[1, h]
        kg_ref[:, at] = (klocal[:, at] + until_end[h] * nt(v_ref[:, at], later)).astype(BF16)
        vg_ref[:, at] = (vlocal[:, at] + nn(kdec[:, at], later)).astype(BF16)

    arrived(c_out.at[1], c_send.at[1])


def store(*refs):
    *refs, sems = refs
    count = len(refs) // 2
    copies = [pltpu.make_async_copy(refs[i], refs[count + i], sems.at[i]) for i in range(count)]
    for copy in copies:
        copy.start()
    for copy in copies:
        copy.wait()


def on_device(chips, queries, keys, values, log_decay, gate, norm_gain, out_weight, target):
    Y, Z = chips
    tokens, width = queries.shape
    rows, features = out_weight.shape
    half = rows // 2
    far = Z // 2
    vmem = pltpu.VMEM
    dma = pltpu.SemaphoreType.DMA
    scratch = [
        vmem((tokens, width), BF16),
        vmem((tokens, width), BF16),
        vmem((tokens, width), BF16),
        vmem((width // DH, tokens), F32),
        vmem((tokens, width), BF16),
        vmem((1, width), F32),
        vmem((rows, tokens), BF16),
        dma((7,)),
        vmem((Z, X, 2, half, width), BF16),
        vmem((Z, half, width), BF16),
        vmem((Z, 2, width // DH, tokens // 2, DH), BF16),
        vmem((2, X, rows, tokens // 2), F32),
        vmem((2, X - 1, rows, tokens // 2), BF16),
        vmem((2, X - 1, rows, tokens // 2), BF16),
        vmem((2, X, rows, tokens // 2), BF16),
        vmem((2, tokens // 2, X * rows), BF16),
        vmem((Z - 1, 2, 2, tokens // 2, DH), BF16),
        vmem((Z - 1, 2, 2, tokens // 2, DH), BF16),
        vmem((width // DH, tokens, tokens), F32),
        vmem((width // DH, tokens, tokens), BF16),
        vmem((tokens, width), BF16),
        vmem((tokens, width), F32),
        vmem((tokens, width), F32),
        vmem((tokens, width), F32),
        vmem((tokens, width), BF16),
        vmem((width // DH, tokens, DH), F32),
        vmem((width // DH, tokens, DH), F32),
        vmem((tokens, width), BF16),
        vmem((tokens, width), F32),
        vmem((tokens, width), F32),
        vmem((8, 128), F32),
        vmem((8, 128), F32),
        vmem((Y, 8, 128), F32),
        vmem((2, DH, DH), BF16),
        vmem((2, DH, DH), BF16),
        vmem((2, DH, DH), F32),
        vmem((2, DH, DH), BF16),
        vmem((2, max(Y - 1, 1), DH, DH), BF16),
        vmem((DH, DH), F32),
        vmem((8, 128), F32),
        vmem((2, DH, DH), BF16),
        vmem((2, 2, DH, DH), BF16),
        vmem((2, Z, 1, tokens), F32),
        vmem((2, X, 1, tokens), F32),
        dma((4,)),
        dma((4,)),
        dma,
        dma((3,)),
        dma((3,)),
        dma,
        dma((2, far, 2, 2)),
        dma,
        dma((2, X - 1)),
        dma,
        dma((2, X - 1)),
        dma,
        dma((Z - 1, 2, 2)),
        dma,
        dma,
        dma,
        dma((max(Y - 1, 1),)),
        dma((2,)),
        dma((2,)),
        dma((2, max(Y - 1, 1))),
        dma((2, max(Y - 1, 1))),
        dma((2,)),
        dma((2,)),
        dma,
        dma((2, Z - 1)),
        dma,
        dma((2, X - 1)),
    ]
    in_vmem = pl.BlockSpec(memory_space=pltpu.VMEM)
    in_hbm = pl.BlockSpec(memory_space=pltpu.HBM)
    shapes = [(rows, tokens)] + [(tokens, width)] * 4
    operands = (queries, keys, values, log_decay.T, gate, norm_gain.reshape(1, width), out_weight, target.T)
    results = pl.pallas_call(
        functools.partial(kernel, chips),
        out_shape=tuple(pltpu.VMEM(shape, BF16) for shape in shapes),
        in_specs=[in_hbm] * 8,
        out_specs=(in_vmem,) * 5,
        scratch_shapes=scratch,
        compiler_params=pltpu.CompilerParams(
            collective_id=0, has_side_effects=True, vmem_limit_bytes=48 * 1024 * 1024
        ),
        cost_estimate=pl.CostEstimate(flops=2 * 10**9, bytes_accessed=8 * 10**6, transcendentals=10**6),
        name="attention_layer",
    )(*[pltpu.with_memory_space_constraint(operand, pltpu.HBM) for operand in operands])
    output, *grads = pl.pallas_call(
        store,
        out_shape=tuple(jax.ShapeDtypeStruct(shape, BF16) for shape in shapes),
        in_specs=[in_vmem] * 5,
        out_specs=(in_hbm,) * 5,
        scratch_shapes=[dma((5,))],
        compiler_params=pltpu.CompilerParams(vmem_limit_bytes=4 * 1024 * 1024),
        name="store",
    )(*results)
    return (output.T, *grads)


def solution(mesh):
    chips = (mesh.shape["ctx"] // 2, mesh.shape["tp"] // X)
    return jax.shard_map(
        functools.partial(on_device, chips),
        mesh=mesh,
        in_specs=(
            P("ctx", "tp"),
            P("ctx", "tp"),
            P("ctx", "tp"),
            P("ctx", "tp"),
            P("ctx", "tp"),
            P("tp"),
            P("tp", None),
            P("ctx", "tp"),
        ),
        out_specs=(P("ctx", "tp"),) * 5,
        check_vma=False,
    )
```

```python
import functools

import jax
import jax.numpy as jnp
from jax import lax
from jax.experimental import pallas as pl
from jax.experimental.pallas import tpu as pltpu
from jax.sharding import PartitionSpec as P

DH = 128
EPS = 1e-06
MESH = pl.DeviceIdType.MESH
F32 = jnp.float32
BF16 = jnp.bfloat16
X = 4


def nn(a, b):
    return lax.dot_general(a, b, (((1,), (0,)), ((), ())), preferred_element_type=F32)


def nt(a, b):
    return lax.dot_general(a, b, (((1,), (1,)), ((), ())), preferred_element_type=F32)


def tn(a, b):
    return lax.dot_general(a, b, (((0,), (0,)), ((), ())), preferred_element_type=F32)


def identity(size):
    row = lax.broadcasted_iota(jnp.int32, (size, size), 0)
    column = lax.broadcasted_iota(jnp.int32, (size, size), 1)
    return jnp.where(row == column, 1.0, 0.0).astype(BF16)


def as_row(column):
    return jnp.broadcast_to(column, (column.shape[0], 128)).T[0:1, :]


def as_columns(row):
    return jnp.broadcast_to(row, (128, row.shape[1])).T


def kernel(
    sizes,
    q_in,
    k_in,
    v_in,
    ld_in,
    gate_in,
    gain_in,
    w_ref,
    target_in,
    out_ref,
    qg_ref,
    kg_ref,
    vg_ref,
    gg_ref,
    q_ref,
    k_ref,
    v_ref,
    ld_ref,
    gate_ref,
    gain_ref,
    target_ref,
    in_sems,
    wb,
    wrelay,
    uall,
    yacc,
    ystage,
    yrecv,
    gx,
    gall,
    fstage,
    frecv,
    weight,
    probs,
    kdec,
    att,
    klocal,
    vlocal,
    agrad,
    until_end,
    from_start,
    qdec,
    scale,
    closed,
    bown,
    bsib,
    bchip,
    s_out,
    s_in,
    s_keep,
    t_out,
    t_in,
    c_acc,
    d_acc,
    c_out,
    state,
    small_z,
    small_x,
    w_send,
    w_recv,
    w_own,
    ws_send,
    ws_recv,
    u_send,
    u_recv,
    y_send,
    y_recv,
    g_send,
    g_recv,
    f_send,
    f_recv,
    b_send,
    b_recv,
    bc_send,
    bc_recv,
    s_send,
    s_recv,
    t_send,
    t_recv,
    c_send,
    c_recv,
    sz_send,
    sz_recv,
    sx_send,
    sx_recv,
):
    Y, Z = sizes
    tokens = q_ref.shape[0]
    half_tokens = tokens // 2
    rows = w_ref.shape[0]
    half = rows // 2
    width = q_ref.shape[1]
    total_features = w_ref.shape[1]
    heads = width // DH

    ctx = lax.axis_index("ctx")
    tp = lax.axis_index("tp")
    core = lax.rem(ctx, 2)
    y = lax.div(ctx, 2)
    x = lax.rem(tp, X)
    z = lax.div(tp, X)
    sibling = (y * 2 + 1 - core, tp)
    is_zero = core == 0

    def xs(step):
        return lax.rem(x + step + X, X)

    def zs(step):
        return lax.rem(z + step + 2 * Z, Z)

    def at_x(step):
        return (ctx, z * X + xs(step))

    def at_z(step):
        return (ctx, zs(step) * X + x)

    def at_y(place):
        return (place * 2 + core, tp)

    sign = 1 - 2 * core
    left, right, opp = xs(-1), xs(1), xs(2)

    def send(src, dst, send_sem, recv_sem, device):
        copy = pltpu.make_async_remote_copy(
            src_ref=src,
            dst_ref=dst,
            send_sem=send_sem,
            recv_sem=recv_sem,
            device_id=device,
            device_id_type=MESH,
        )
        copy.start()

    def arrived(ref, sem):
        pltpu.make_async_copy(ref, ref, sem).wait()

    loads = [
        pltpu.make_async_copy(src, dst, in_sems.at[index])
        for index, (src, dst) in enumerate(
            (
                (ld_in, ld_ref),
                (k_in, k_ref),
                (v_in, v_ref),
                (q_in, q_ref),
                (gate_in, gate_ref),
                (gain_in, gain_ref),
                (target_in, target_ref),
            )
        )
    ]
    for load in loads:
        load.start()
    barrier = pltpu.get_barrier_semaphore()
    partners = [sibling] + [at_x(step) for step in range(1, X)]
    partners += [at_z(step) for step in range(1, Z)]
    partners += [at_y(lax.rem(y + step, Y)) for step in range(1, Y)]
    for partner in partners:
        pl.semaphore_signal(barrier, inc=1, device_id=partner, device_id_type=MESH)

    def w_columns(block, x_to):
        start = pl.multiple_of((block * X + x_to) * width, width)
        return pl.ds(start, width)

    my_rows = pl.ds(pl.multiple_of(core * half, half), half)
    x_far = xs(sign)

    def w_far(block, carry):
        send(w_ref.at[my_rows, w_columns(block, opp)], wrelay.at[block], w_send.at[0], w_recv.at[0], (ctx, z * X + x_far))
        return carry

    def w_near(block, carry):
        send(w_ref.at[my_rows, w_columns(block, right)], wb.at[block, x, core], w_send.at[1], w_recv.at[1], at_x(1))
        send(w_ref.at[my_rows, w_columns(block, left)], wb.at[block, x, core], w_send.at[2], w_recv.at[2], at_x(-1))
        return carry

    def w_mine(block, carry):
        for part in range(2):
            pltpu.make_async_copy(
                w_ref.at[pl.ds(part * half, half), w_columns(block, x)], wb.at[block, x, part], w_own
            ).start()
        return carry

    row = lax.broadcasted_iota(jnp.int32, (tokens, tokens), 0)
    column = lax.broadcasted_iota(jnp.int32, (tokens, tokens), 1)
    causal = row >= column
    loads[0].wait()
    upto = jnp.where(row <= column, 1.0, 0.0).astype(BF16)
    rest = ld_ref[...]
    cum = jnp.zeros_like(rest)
    for _ in range(3):
        piece = rest.astype(BF16)
        cum = cum + nn(piece, upto)
        rest = rest - piece.astype(F32)
    cum_rows = [cum[h : h + 1, :] for h in range(heads)]
    cums = [as_columns(c) for c in cum_rows]
    totals = [c[tokens - 1 : tokens, :] for c in cums]
    bown[...] = jnp.zeros_like(bown)
    for h in range(heads):
        bown[h : h + 1, :] = totals[h]
    loads[1].wait()
    loads[2].wait()

    def lanes(h):
        return slice(h * DH, (h + 1) * DH)

    for h in range(heads):
        until_end[h] = jnp.exp(totals[h] - cums[h])
    order = (core, 1 - core)
    others = (1 - core, core)

    def any_lanes(h):
        return pl.ds(pl.multiple_of(h * DH, DH), DH)

    def of_core(pair):
        return jnp.where(is_zero, pair[0], pair[1])

    def scan_give(turn, mine, value):
        if mine:
            s_keep[turn] = value
        else:
            s_out[turn] = value.astype(BF16)
            send(s_out.at[turn], s_in.at[turn], s_send.at[turn], s_recv.at[turn], sibling)

    def scan_way(turn):
        step = 1 if turn == 0 else -1
        first_here = is_zero if turn == 0 else jnp.logical_not(is_zero)
        return step, first_here

    def decays(ref):
        return of_core((ref[0:1, :], ref[1:2, :]))

    def reaches(place):
        return jnp.logical_and(place >= 0, place < Y)

    def scan_send(turn):
        step, first_here = scan_way(turn)
        arrived(s_in.at[turn], s_recv.at[turn])
        mine = s_keep[turn]
        theirs = s_in[turn].astype(F32)
        first = jnp.where(first_here, mine, theirs)
        second = jnp.where(first_here, theirs, mine)
        s_keep[turn] = first
        b_second = jnp.where(first_here, decays(bsib), decays(bown))
        t_out[turn] = (jnp.exp(b_second) * first + second).astype(BF16)
        for distance in range(1, Y):
            place = y + step * distance

            @pl.when(reaches(place))
            def _():
                send(
                    t_out.at[turn],
                    t_in.at[turn, distance - 1],
                    t_send.at[turn, distance - 1],
                    t_recv.at[turn, distance - 1],
                    at_y(place),
                )

    def scan_end(turn):
        step, first_here = scan_way(turn)
        c_acc[...] = jnp.zeros_like(c_acc)
        d_acc[...] = jnp.zeros_like(d_acc)
        for distance in range(1, Y):
            place = y - step * distance

            @pl.when(reaches(place))
            def _():
                slot = t_in.at[turn, distance - 1]
                arrived(slot, t_recv.at[turn, distance - 1])
                between = d_acc[0:1, :]
                c_acc[...] += jnp.exp(between) * slot[...].astype(F32)
                d_acc[0:1, :] = between + decays(bchip.at[place])

        b_first = jnp.where(first_here, decays(bown), decays(bsib))
        carried = c_acc[...]
        after = jnp.exp(b_first) * carried + s_keep[turn]
        c_out[turn] = jnp.where(first_here, after, carried).astype(BF16)
        send(c_out.at[turn], state.at[turn, core], c_send.at[turn], c_recv.at[turn], sibling)
        state[turn, core] = jnp.where(first_here, carried, after).astype(BF16)

    def scan_take(turn):
        arrived(state.at[turn, 1 - core], c_recv.at[turn])

    pl.semaphore_wait(barrier, len(partners))
    send(bown, bsib, b_send, b_recv, sibling)
    for mine, h in enumerate(others):
        at = any_lanes(h)
        decayed = (k_ref[:, at].astype(F32) * until_end[h]).astype(BF16)
        kdec[:, at] = decayed
        scan_give(0, mine, tn(decayed, v_ref[:, at]))
    lax.fori_loop(0, Z, w_far, 0)
    lax.fori_loop(0, Z, w_near, 0)

    arrived(bsib, b_recv)
    bchip[y] = bown[...] + bsib[...]
    for distance in range(1, Y):
        place = lax.rem(y + distance, Y)
        send(bchip.at[y], bchip.at[y], bc_send, bc_recv.at[distance - 1], at_y(place))
    scan_send(0)

    for load in loads[3:]:
        load.wait()
    for h in range(heads):
        gaps = cums[h][:, 0:1] - cum_rows[h]
        decay = jnp.where(causal, jnp.exp(jnp.minimum(gaps, 0.0)), 0.0)
        weight[h] = decay
        probs[h] = (nt(q_ref[:, lanes(h)], k_ref[:, lanes(h)]) * decay).astype(BF16)
        att[:, lanes(h)] = nn(probs[h], v_ref[:, lanes(h)])
        from_start[h] = jnp.exp(cums[h])
        gate_open = jax.nn.sigmoid(gate_ref[:, lanes(h)].astype(F32))
        scale[:, lanes(h)] = gain_ref[:, lanes(h)] * gate_open

    for distance in range(1, Y):
        arrived(bchip.at[lax.rem(y - distance + Y, Y)], bc_recv.at[distance - 1])

    scan_end(0)

    far, near = Z // 2, Z - 1 - Z // 2
    hops = (far, near)
    ways = (sign, -sign)

    def u_part(way, step, part, h):
        return uall.at[zs(-ways[way] * step), part, h]

    def u_start(way, step, part, h):
        ref = u_part(way, step, part, h)
        send(ref, ref, u_send, u_recv.at[way, step, part, h], at_z(ways[way]))

    for turn, h in enumerate(order):
        if turn == 1:
            scan_take(0)
        for part in range(2):
            span = slice(part * half_tokens, (part + 1) * half_tokens)
            from_state = nn(q_ref[span, any_lanes(h)], state[0, h]) * from_start[h, span, :]
            attended = att[span, any_lanes(h)] + from_state
            att[span, any_lanes(h)] = attended
            uall[z, part, h] = (attended * scale[span, any_lanes(h)]).astype(BF16)
            for way in range(2):
                if hops[way] > 0:
                    u_start(way, 0, part, h)

    def small_share(turn, value):
        small_z[turn, 0] = value
        for step in range(1, Z):
            send(small_z.at[turn, 0], small_z.at[turn, step], sz_send, sz_recv.at[turn, step - 1], at_z(step))

    def small_cross(turn):
        for step in range(1, Z):
            arrived(small_z.at[turn, step], sz_recv.at[turn, step - 1])
        sum_z = small_z[turn, 0]
        for step in range(1, Z):
            sum_z = sum_z + small_z[turn, step]
        small_x[turn, 0] = sum_z
        for step in range(1, X):
            send(small_x.at[turn, 0], small_x.at[turn, step], sx_send, sx_recv.at[turn, step - 1], at_x(step))

    def small_sum(turn):
        for step in range(1, X):
            arrived(small_x.at[turn, step], sx_recv.at[turn, step - 1])
        sum_x = small_x[turn, 0]
        for step in range(1, X):
            sum_x = sum_x + small_x[turn, step]
        return sum_x

    squares = jnp.zeros((tokens, 1), F32)
    for h in range(heads):
        attended = att[:, lanes(h)]
        squares = squares + jnp.sum(attended * attended, axis=1, keepdims=True)
    small_share(0, as_row(squares))
    lax.fori_loop(0, Z, w_mine, 0)

    arrived(wrelay, w_recv.at[0])
    send(wrelay, wb.at[:, xs(-sign), core], w_send.at[3], w_recv.at[3], (ctx, z * X + x_far))

    for h in range(heads):
        qdec[:, lanes(h)] = (q_ref[:, lanes(h)].astype(F32) * from_start[h]).astype(BF16)
        closed[:, lanes(h)] = 1.0 - jax.nn.sigmoid(gate_ref[:, lanes(h)].astype(F32))

    def w_pair(source, sem, slot):
        ref = wb.at[:, source, core]
        arrived(ref, sem)
        send(ref, ref, ws_send.at[slot], ws_recv.at[slot], sibling)

    def w_block(block):
        return wb[block].reshape(X * rows, width)

    def u_block(block, part):
        return jnp.concatenate([uall[block, part, h] for h in range(heads)], axis=1)

    def product(block):
        both = nt(w_block(block), jnp.concatenate([u_block(block, part) for part in range(2)], axis=0))
        return [both[:, part * half_tokens : (part + 1) * half_tokens].reshape(yacc.shape[1:]) for part in range(2)]

    def u_pass(step, part, some):
        for h in some:
            for way in range(2):
                if step < hops[way]:
                    arrived(u_part(way, step + 1, part, h), u_recv.at[way, step, part, h])
                    if step + 1 < hops[way]:
                        u_start(way, step + 1, part, h)

    def absorb(step):
        for way in range(2):
            if step < hops[way]:
                for part, value in enumerate(product(zs(-ways[way] * (step + 1)))):
                    yacc[part] += value

    def w_forward():
        small_cross(0)
        w_pair(left, w_recv.at[1], 0)
        w_pair(right, w_recv.at[2], 1)
        w_pair(opp, w_recv.at[3], 2)

    for step in range(far - 1):
        if step == far - 2:
            w_forward()
        for h in order:
            for part in range(2):
                u_pass(step, part, (h,))
    if far < 2:
        w_forward()
    for part in range(2):
        arrived(wb.at[:, x, part], w_own)
    for slot, source in enumerate((left, right, opp)):
        arrived(wb.at[:, source, 1 - core], ws_recv.at[slot])
    for part, value in enumerate(product(z)):
        yacc[part] = value
    for step in range(far - 1):
        absorb(step)

    steps = (2, 1, 3)

    def y_start(part, step):
        ystage[part, step - 1] = yacc[part, xs(step)].astype(BF16)
        send(
            ystage.at[part, step - 1],
            yrecv.at[part, step - 1],
            y_send,
            y_recv.at[part, step - 1],
            at_x(step),
        )

    def y_arrived(part, step):
        arrived(yrecv.at[part, step - 1], y_recv.at[part, step - 1])
        return yrecv[part, step - 1].astype(F32)

    for part in range(2):
        u_pass(far - 1, part, order)
        last = zs(sign * far)
        last_u = u_block(last, part)

        def finish(rows_of):
            block = wb[last, rows_of].reshape(rows, width)
            yacc[part, rows_of] += nt(block, last_u)

        for step in steps:
            finish(xs(step))
            y_start(part, step)
        finish(x)

    inv_rms = lax.rsqrt(small_sum(0) / total_features + EPS)

    def g_arrived(part, step):
        arrived(gx.at[part, xs(-step)], g_recv.at[part, step - 1])

    products = []
    for part in range(2):
        span = slice(part * half_tokens, (part + 1) * half_tokens)
        total = yacc[part, x]
        for step in (1, 3, 2):
            total = total + y_arrived(part, step)
        rounded = (total * inv_rms[:, span]).astype(BF16)
        grad = (rounded.astype(F32) - target_ref[:, span].astype(F32)).astype(BF16)
        gx[part, x] = grad
        for step in steps:
            ref = gx.at[part, x]
            send(ref, ref, g_send, g_recv.at[part, step - 1], at_x(step))
        out_ref[:, span] = rounded
        products.append(jnp.sum(grad.astype(F32) * total, axis=0, keepdims=True))
    small_share(1, jnp.concatenate(products, axis=1))

    eye = identity(half_tokens)

    def feature_part(block, part):
        return nn(gall[part], w_block(block))

    def f_slot(way, step):
        return way * far + step

    def f_start(way, step, part, h, value):
        slot = f_slot(way, step)
        fstage[slot, part, h] = value.astype(BF16)
        send(
            fstage.at[slot, part, h],
            frecv.at[slot, part, h],
            f_send,
            f_recv.at[slot, part, h],
            at_z(ways[way]),
        )

    def f_arrived(way, step, part, h):
        slot = f_slot(way, step)
        arrived(frecv.at[slot, part, h], f_recv.at[slot, part, h])
        return frecv[slot, part, h].astype(F32)

    def by_head(value):
        first, second = value[:, lanes(0)], value[:, lanes(1)]
        return jnp.where(is_zero, second, first), jnp.where(is_zero, first, second)

    for part in range(2):
        for x_step in (1, 3, 2):
            g_arrived(part, x_step)
        gall[part] = nt(eye, gx[part].reshape(X * rows, half_tokens)).astype(BF16)
        sums = [by_head(feature_part(zs(ways[way] * hops[way]), part)) if hops[way] > 0 else None for way in range(2)]
        for turn in range(heads):
            for way in range(2):
                if hops[way] > 0:
                    f_start(way, 0, part, turn, sums[way][turn])
    small_cross(1)

    def feature_both(block):
        return by_head(nn(gall[...].reshape(tokens, X * rows), w_block(block)))

    for step in range(1, far):
        sums = [feature_both(zs(ways[way] * (hops[way] - step))) if step < hops[way] else None for way in range(2)]
        for part in range(2):
            span = slice(part * half_tokens, (part + 1) * half_tokens)
            for turn in range(heads):
                for way in range(2):
                    if step < hops[way]:
                        value = sums[way][turn][span, :] + f_arrived(way, step - 1, part, turn)
                        f_start(way, step, part, turn, value)

    own_feature = feature_both(z)
    mean_product = as_columns(small_sum(1) / total_features)
    inv = as_columns(inv_rms)

    normed_grads = []
    for turn, h in enumerate(others):
        at = any_lanes(h)
        pieces = []
        for part in range(2):
            value = own_feature[turn][part * half_tokens : (part + 1) * half_tokens, :]
            for way in range(2):
                if hops[way] > 0:
                    value = value + f_arrived(way, hops[way] - 1, part, turn)
            pieces.append(value)
        attended = att[:, at]
        normed_grad = jnp.concatenate(pieces, axis=0) * scale[:, at]
        grad = (inv * normed_grad - inv * inv * inv * attended * mean_product).astype(BF16)
        agrad[:, at] = grad
        scan_give(1, turn, tn(qdec[:, at], grad))
        normed_grads.append(normed_grad)
    scan_send(1)
    for turn, h in enumerate(others):
        at = any_lanes(h)
        gg_ref[:, at] = (normed_grads[turn] * att[:, at] * inv * closed[:, at]).astype(BF16)

    for h in range(heads):
        grad = agrad[:, lanes(h)]
        score_grad = (nt(grad, v_ref[:, lanes(h)]) * weight[h]).astype(BF16)
        qg_ref[:, lanes(h)] = (
            nn(score_grad, k_ref[:, lanes(h)]) + from_start[h] * nt(grad, state[0, h])
        ).astype(BF16)
        klocal[:, lanes(h)] = tn(score_grad, q_ref[:, lanes(h)])
        vlocal[:, lanes(h)] = tn(probs[h], grad)
    for index in range(4):
        arrived(wrelay, w_send.at[index])
    for index in range(3):
        arrived(wrelay, ws_send.at[index])
    arrived(uall.at[pl.ds(0, Z - 1)], u_send)
    arrived(fstage, f_send)
    arrived(ystage, y_send)
    arrived(ystage, g_send)
    arrived(bown, b_send)
    if Y > 1:
        arrived(bchip.at[pl.ds(0, Y - 1)], bc_send)
    arrived(small_z.at[:, pl.ds(0, Z - 1)], sz_send)
    arrived(small_x.at[:, pl.ds(0, X - 1)], sx_send)
    for turn in range(2):
        arrived(s_out.at[turn], s_send.at[turn])

    def scan_sent(turn):
        step, _ = scan_way(turn)
        for distance in range(1, Y):

            @pl.when(reaches(y + step * distance))
            def _():
                arrived(t_out.at[turn], t_send.at[turn, distance - 1])

    scan_sent(0)
    arrived(c_out.at[0], c_send.at[0])

    scan_end(1)
    for turn, h in enumerate(order):
        if turn == 1:
            scan_sent(1)
            scan_take(1)
        at = any_lanes(h)
        later = state[1, h]
        kg_ref[:, at] = (klocal[:, at] + until_end[h] * nt(v_ref[:, at], later)).astype(BF16)
        vg_ref[:, at] = (vlocal[:, at] + nn(kdec[:, at], later)).astype(BF16)

    arrived(c_out.at[1], c_send.at[1])


def store(*refs):
    *refs, sems = refs
    count = len(refs) // 2
    copies = [pltpu.make_async_copy(refs[i], refs[count + i], sems.at[i]) for i in range(count)]
    for copy in copies:
        copy.start()
    for copy in copies:
        copy.wait()


def on_device(chips, queries, keys, values, log_decay, gate, norm_gain, out_weight, target):
    Y, Z = chips
    tokens, width = queries.shape
    rows, features = out_weight.shape
    half = rows // 2
    far = Z // 2
    vmem = pltpu.VMEM
    dma = pltpu.SemaphoreType.DMA
    scratch = [
        vmem((tokens, width), BF16),
        vmem((tokens, width), BF16),
        vmem((tokens, width), BF16),
        vmem((width // DH, tokens), F32),
        vmem((tokens, width), BF16),
        vmem((1, width), F32),
        vmem((rows, tokens), BF16),
        dma((7,)),
        vmem((Z, X, 2, half, width), BF16),
        vmem((Z, half, width), BF16),
        vmem((Z, 2, width // DH, tokens // 2, DH), BF16),
        vmem((2, X, rows, tokens // 2), F32),
        vmem((2, X - 1, rows, tokens // 2), BF16),
        vmem((2, X - 1, rows, tokens // 2), BF16),
        vmem((2, X, rows, tokens // 2), BF16),
        vmem((2, tokens // 2, X * rows), BF16),
        vmem((Z - 1, 2, 2, tokens // 2, DH), BF16),
        vmem((Z - 1, 2, 2, tokens // 2, DH), BF16),
        vmem((width // DH, tokens, tokens), F32),
        vmem((width // DH, tokens, tokens), BF16),
        vmem((tokens, width), BF16),
        vmem((tokens, width), F32),
        vmem((tokens, width), F32),
        vmem((tokens, width), F32),
        vmem((tokens, width), BF16),
        vmem((width // DH, tokens, DH), F32),
        vmem((width // DH, tokens, DH), F32),
        vmem((tokens, width), BF16),
        vmem((tokens, width), F32),
        vmem((tokens, width), F32),
        vmem((8, 128), F32),
        vmem((8, 128), F32),
        vmem((Y, 8, 128), F32),
        vmem((2, DH, DH), BF16),
        vmem((2, DH, DH), BF16),
        vmem((2, DH, DH), F32),
        vmem((2, DH, DH), BF16),
        vmem((2, max(Y - 1, 1), DH, DH), BF16),
        vmem((DH, DH), F32),
        vmem((8, 128), F32),
        vmem((2, DH, DH), BF16),
        vmem((2, 2, DH, DH), BF16),
        vmem((2, Z, 1, tokens), F32),
        vmem((2, X, 1, tokens), F32),
        dma((4,)),
        dma((4,)),
        dma,
        dma((3,)),
        dma((3,)),
        dma,
        dma((2, far, 2, 2)),
        dma,
        dma((2, X - 1)),
        dma,
        dma((2, X - 1)),
        dma,
        dma((Z - 1, 2, 2)),
        dma,
        dma,
        dma,
        dma((max(Y - 1, 1),)),
        dma((2,)),
        dma((2,)),
        dma((2, max(Y - 1, 1))),
        dma((2, max(Y - 1, 1))),
        dma((2,)),
        dma((2,)),
        dma,
        dma((2, Z - 1)),
        dma,
        dma((2, X - 1)),
    ]
    in_vmem = pl.BlockSpec(memory_space=pltpu.VMEM)
    in_hbm = pl.BlockSpec(memory_space=pltpu.HBM)
    shapes = [(rows, tokens)] + [(tokens, width)] * 4
    operands = (queries, keys, values, log_decay.T, gate, norm_gain.reshape(1, width), out_weight, target.T)
    results = pl.pallas_call(
        functools.partial(kernel, chips),
        out_shape=tuple(pltpu.VMEM(shape, BF16) for shape in shapes),
        in_specs=[in_hbm] * 8,
        out_specs=(in_vmem,) * 5,
        scratch_shapes=scratch,
        compiler_params=pltpu.CompilerParams(
            collective_id=0, has_side_effects=True, vmem_limit_bytes=48 * 1024 * 1024
        ),
        cost_estimate=pl.CostEstimate(flops=2 * 10**9, bytes_accessed=8 * 10**6, transcendentals=10**6),
        name="attention_layer",
    )(*[pltpu.with_memory_space_constraint(operand, pltpu.HBM) for operand in operands])
    output, *grads = pl.pallas_call(
        store,
        out_shape=tuple(jax.ShapeDtypeStruct(shape, BF16) for shape in shapes),
        in_specs=[in_vmem] * 5,
        out_specs=(in_hbm,) * 5,
        scratch_shapes=[dma((5,))],
        compiler_params=pltpu.CompilerParams(vmem_limit_bytes=4 * 1024 * 1024),
        name="store",
    )(*results)
    return (output.T, *grads)


def solution(mesh):
    chips = (mesh.shape["ctx"] // 2, mesh.shape["tp"] // X)
    return jax.shard_map(
        functools.partial(on_device, chips),
        mesh=mesh,
        in_specs=(
            P("ctx", "tp"),
            P("ctx", "tp"),
            P("ctx", "tp"),
            P("ctx", "tp"),
            P("ctx", "tp"),
            P("tp"),
            P("tp", None),
            P("ctx", "tp"),
        ),
        out_specs=(P("ctx", "tp"),) * 5,
        check_vma=False,
    )
```
